256 devices in a mesh: grp: 8 (over z_hi, core), blk: 32 (over y, x, z_lo).
Axes of the slice: x: 4, y: 4, z: 8 (z_hi: 4, z_lo: 2; z = z_hi * 2 + z_lo), core: 2. Of those that a mesh axis runs over, the one named last changes fastest.
Arguments:
- integrals: bfloat16 [2, 5120, 20480], P(None, 'blk', 'grp'), may hold values from -0.59765625 to 0.59765625
- tiles: bfloat16 [1440, 128, 128], P('grp'), may hold values from -0.1875 to 0.1875
- tile_index: int32 [1440, 2], P('grp'), may hold values from 0 to 159, as said below
- vir_energy: float32 [5120], replicated, may hold values from 0.5 to 4
- occ_energy: float32 [1000], replicated, may hold values from -3 to -0.5
- pair_index: int32 [2], replicated, may hold values from 0 to 999
Outputs:
- density: bfloat16 [5120, 20480], P('blk', 'grp')
The draws below stay inside these ranges and needn't reach their ends.
Inputs may be any that keep to these rules, and one draw needn't show every extreme that they name: tile_index[s, 1] is 0 or 1. Where it is 1, tile_index[s, 0] is c(s) + (s % 9) - 4; where it is 0, it is c(s). Every slot with (s % 9) == 4 is listed.
All inputs are finite; a program needn't handle non-finite values.
Results may differ from the reference program's by a relative error of at most 0.0057.
Values may be sent and summed in bfloat16 or wider, within the bound.
No kernel may reach another device: no remote copies, remote signals or barrier semaphores. Data moves between devices by JAX's collectives and lax.ppermute only.
A program may use at most 128 MiB of HBM per device.

```python
import jax
import jax.numpy as jnp
from jax import lax

NVIR = 5120
NAUX = 20480
NOCC = 1000
TILE = 128
HB = 4
CT = 20
SLOTS = 180
TILE_ALL = 1440
N_GRP = 8


def draw_tile_index(key, part):
    key = jax.random.fold_in(key, 7)
    band_width = 2 * HB + 1
    group_total = TILE_ALL // SLOTS
    position = jnp.arange(TILE_ALL, dtype=jnp.int32)
    group_of = position // SLOTS
    within = position % SLOTS
    column = group_of * CT + within // band_width
    offset = within % band_width - HB
    tile_row = column + offset
    is_valid = (tile_row >= 0) & (tile_row < NAUX // TILE)
    first_key, second_key = jax.random.split(key)
    chance = jax.random.randint(first_key, (group_total,), 30, 101)
    rolled = jax.random.randint(second_key, (TILE_ALL,), 0, 100)
    listed = (rolled < chance[group_of]) & is_valid | (offset == 0)
    chosen_row = jnp.where(listed, tile_row, column)
    return jnp.stack([chosen_row, listed.astype(jnp.int32)], axis=1).astype(jnp.int32)


def block_levels(own_key, dims, pieces, low, top_value):
    gain = 1.0
    for dim, parts in pieces:
        heights = jax.random.uniform(jax.random.fold_in(jax.random.fold_in(own_key, 6), dim), (parts,), jnp.float32, low / len(pieces), top_value / len(pieces))
        gain = gain * jnp.repeat(jnp.exp(heights), dims[dim] // parts).reshape((-1,) + (1,) * (len(dims) - 1 - dim))
    return gain


def bell_draw(rng, shape, deviation, reach, cuts=(), kind=jnp.bfloat16):
    result = deviation * jax.random.normal(rng, shape, jnp.float32)
    if cuts:
        result = result * block_levels(rng, shape, cuts, -0.22, 0.18)
    return jnp.clip(result, -reach, reach).astype(kind)


def setup_inputs(seed: int = 0) -> dict:
    key_list = jax.random.split(jax.random.key(seed), 7)
    return {
        "integrals": bell_draw(key_list[0], (2, NVIR, NAUX), 0.1, 0.59765625, ((1, 32), (2, 8))),
        "tiles": bell_draw(key_list[1], (TILE_ALL, TILE, TILE), (TILE * (2 * HB + 1)) ** -0.5, 0.1875, ((0, 8),)),
        "tile_index": draw_tile_index(jax.random.fold_in(key_list[6], 71), 0),
        "vir_energy": jnp.clip(jax.random.uniform(key_list[3], (NVIR,), jnp.float32, 0.5, 4.0), 0.5, 4.0),
        "occ_energy": jnp.clip(jax.random.uniform(key_list[4], (NOCC,), jnp.float32, -3.0, -0.5), -3.0, -0.5),
        "pair_index": jax.random.randint(key_list[5], (2,), 0, NOCC).astype(jnp.int32),
    }


def fit_window(window, group_tiles, group_list, first_column):
    band_width = 2 * HB + 1
    row_count = window.shape[0]
    column_count = group_tiles.shape[0] // band_width
    blocked = window.reshape(row_count, -1, TILE)
    local_rows = (group_list[:, 0] - first_column + HB).astype(jnp.int32)
    live_mask = group_list[:, 1].astype(jnp.float32)

    def one_column(column):
        picked_rows = lax.dynamic_slice_in_dim(local_rows, column * band_width, band_width)
        picked_mask = lax.dynamic_slice_in_dim(live_mask, column * band_width, band_width)
        picked_tiles = lax.dynamic_slice_in_dim(group_tiles, column * band_width, band_width, 0)
        gathered = jnp.take(blocked, picked_rows, axis=1).astype(jnp.float32)
        products = jnp.einsum("xsk,skn->xsn", gathered, picked_tiles.astype(jnp.float32), precision=lax.Precision.HIGHEST)
        return jnp.einsum("xsn,s->xn", products, picked_mask, precision=lax.Precision.HIGHEST)

    columns_out = lax.map(one_column, jnp.arange(column_count, dtype=jnp.int32))
    return columns_out.transpose(1, 0, 2).reshape(row_count, column_count * TILE)


def reference(integrals, tiles, tile_index, vir_energy, occ_energy, pair_index):
    flat = integrals.reshape(2 * NVIR, NAUX)
    padded = jnp.pad(flat, ((0, 0), (HB * TILE, HB * TILE)))

    def one_group(group_index):
        window = lax.dynamic_slice_in_dim(padded, group_index * CT * TILE, (CT + 2 * HB) * TILE, 1)
        group_tiles = lax.dynamic_slice_in_dim(tiles, group_index * SLOTS, SLOTS, 0)
        group_list = lax.dynamic_slice_in_dim(tile_index, group_index * SLOTS, SLOTS, 0)
        return fit_window(window, group_tiles, group_list, group_index * CT)

    fields = lax.map(one_group, jnp.arange(N_GRP, dtype=jnp.int32))
    fitted = fields.transpose(1, 0, 2).reshape(2 * NVIR, NAUX).astype(jnp.bfloat16)
    own_rows = fitted[:NVIR]
    partner = fitted[NVIR:]
    pair_sum = jnp.dot(own_rows, partner.T, preferred_element_type=jnp.float32)
    occ_total = occ_energy[pair_index[0]] + occ_energy[pair_index[1]]
    denominator = (vir_energy[:, None] + vir_energy[None, :]) - occ_total
    amplitudes = (pair_sum / denominator).astype(jnp.bfloat16)
    return jnp.dot(amplitudes, partner, preferred_element_type=jnp.float32).astype(jnp.bfloat16)
```

```python
import functools

import jax
import jax.numpy as jnp
from jax import lax
from jax.experimental import pallas as pl
from jax.experimental.pallas import tpu as pltpu
from jax.sharding import PartitionSpec as P

TILE = 128
HB = 4
BAND = 2 * HB + 1
ROWS = 160
AUX = 2560
HALO = HB * TILE
bf16 = jnp.bfloat16
f32 = jnp.float32
MIB = 1 << 20


def blk_index(y, x, z):
    return ((y % 4) * 4 + x) * 2 + z


PLACES = [(y, x, z) for y in range(4) for x in range(4) for z in range(2)]
OUTER = (3, 2, 1, 0)


def send_y(v, step):
    pairs = [(blk_index(y, x, z), blk_index(y + step, x, z)) for y, x, z in PLACES]
    return lax.ppermute(v, "blk", pairs)


def send_outer(v):
    pairs = [(blk_index(y, x, z), blk_index(y, OUTER[x], z)) for y, x, z in PLACES]
    return lax.ppermute(v, "blk", pairs)


def send_inner(v):
    pairs = [(blk_index(y, x, z), blk_index(y, x ^ 1, z)) for y, x, z in PLACES]
    return lax.ppermute(v, "blk", pairs)


def send_z(v):
    pairs = [(blk_index(y, x, z), blk_index(y, x, 1 - z)) for y, x, z in PLACES]
    return lax.ppermute(v, "blk", pairs)


def send_core(v):
    return lax.ppermute(v, "grp", [(g, g ^ 1) for g in range(8)])


def send_high(v, step):
    return lax.ppermute(v, "grp", [(g, (g + 2 * step) % 8) for g in range(8)])


def params(mib, **kw):
    return pltpu.CompilerParams(vmem_limit_bytes=mib * MIB, **kw)


def cost(flops, nbytes):
    return pl.CostEstimate(flops=int(flops), bytes_accessed=int(nbytes), transcendentals=0)


def fit_kernel(index_ref, left, own, right, tiles, out_a, out_b, ext, weights):
    p = pl.program_id(0)

    @pl.when(p == 0)
    def _():
        ext[:, :HALO] = left[...]
        ext[:, HALO : HALO + AUX] = own[...]
        ext[:, HALO + AUX :] = right[...]
        weights[...] = jnp.zeros_like(weights)

    for q in range(2):
        for o in range(BAND):
            slot = q * BAND + o
            listed = index_ref[1, p * (2 * BAND) + slot] == 1
            tile = tiles[slot]
            j = q + o
            weights[j * TILE : (j + 1) * TILE, q * TILE : (q + 1) * TILE] = jnp.where(
                listed, tile, jnp.zeros_like(tile)
            )
    window = ext[:, pl.ds(pl.multiple_of(p * (2 * TILE), 2 * TILE), (BAND + 1) * TILE)]
    fitted = jnp.dot(window, weights[...], preferred_element_type=f32).astype(bf16)
    out_a[...] = fitted[:ROWS]
    out_b[...] = fitted[ROWS:]


def fit(left, own, right, tiles, index):
    whole = lambda shape: pl.BlockSpec(shape, lambda p, i: (0, 0))
    grid_spec = pltpu.PrefetchScalarGridSpec(
        num_scalar_prefetch=1,
        grid=(10,),
        in_specs=[
            whole((2 * ROWS, HALO)),
            whole((2 * ROWS, AUX)),
            whole((2 * ROWS, HALO)),
            pl.BlockSpec((2 * BAND, TILE, TILE), lambda p, i: (p, 0, 0)),
        ],
        out_specs=[pl.BlockSpec((ROWS, 2 * TILE), lambda p, i: (0, p))] * 2,
        scratch_shapes=[
            pltpu.VMEM((2 * ROWS, AUX + 2 * HALO), bf16),
            pltpu.VMEM(((BAND + 1) * TILE, 2 * TILE), bf16),
        ],
    )
    return pl.pallas_call(
        fit_kernel,
        grid_spec=grid_spec,
        out_shape=[jax.ShapeDtypeStruct((ROWS, AUX), bf16)] * 2,
        compiler_params=params(32),
        cost_estimate=cost(2.1e9, 10e6),
        name="fit",
    )(index, left, own, right, tiles)


def pair_kernel(core_ref, *refs, steps):
    a0, ax, az, d1, d2 = refs[:5]
    bs = refs[5:-5]
    keep, send, acc, acat, bcat = refs[-5:]
    k = pl.program_id(0)
    core = core_ref[0]
    first = pl.multiple_of(core * (2 * ROWS), 2 * ROWS)
    second = pl.multiple_of((1 - core) * (2 * ROWS), 2 * ROWS)
    acat[pl.ds(first, ROWS)] = a0[...]
    acat[pl.ds(first + ROWS, ROWS)] = ax[...]
    acat[pl.ds(second, ROWS)] = az[...]
    acat[pl.ds(second + ROWS, ROWS // 2)] = d1[...]
    acat[pl.ds(second + ROWS + ROWS // 2, ROWS // 2)] = d2[...]
    at = 0
    for b in bs:
        bcat[at : at + b.shape[0]] = b[...]
        at += b.shape[0]
    product = lax.dot_general(
        acat[...], bcat[...], (((1,), (1,)), ((), ())), preferred_element_type=f32
    )

    @pl.when(k == 0)
    def _():
        acc[...] = product

    @pl.when(k > 0)
    def _():
        acc[...] += product

    @pl.when(k == steps - 1)
    def _():
        keep[...] = acc[: 2 * ROWS]
        send[...] = acc[2 * ROWS :].astype(bf16)


def pair(core, a_parts, b_parts):
    width = sum(b.shape[0] for b in b_parts)
    chunk = 512
    steps = AUX // chunk
    spec = lambda rows: pl.BlockSpec((rows, chunk), lambda k, c: (0, k))
    grid_spec = pltpu.PrefetchScalarGridSpec(
        num_scalar_prefetch=1,
        grid=(steps,),
        in_specs=[spec(v.shape[0]) for v in (*a_parts, *b_parts)],
        out_specs=[pl.BlockSpec((2 * ROWS, width), lambda k, c: (0, 0))] * 2,
        scratch_shapes=[
            pltpu.VMEM((4 * ROWS, width), f32),
            pltpu.VMEM((4 * ROWS, chunk), bf16),
            pltpu.VMEM((width, chunk), bf16),
        ],
    )
    return pl.pallas_call(
        functools.partial(pair_kernel, steps=steps),
        grid_spec=grid_spec,
        out_shape=[
            jax.ShapeDtypeStruct((2 * ROWS, width), f32),
            jax.ShapeDtypeStruct((2 * ROWS, width), bf16),
        ],
        compiler_params=params(32),
        cost_estimate=cost(2 * 4 * ROWS * width * AUX, 2 * (4 * ROWS + width) * AUX),
        name="pair",
    )(core, *a_parts, *b_parts)


SHARE = ROWS // 2


def core_sum_kernel(high_ref, keep, got, own, s1, s2, s3):
    high = high_ref[0]
    for step, out in enumerate((own, s1, s2, s3)):
        at = pl.multiple_of(((high + step) % 4) * SHARE, SHARE)
        value = keep[pl.ds(at, SHARE)] + got[pl.ds(at, SHARE)].astype(f32)
        out[...] = value.astype(out.dtype)


def core_sum(high, keep, got):
    width = keep.shape[1]
    vmem = pl.BlockSpec(memory_space=pltpu.VMEM)
    return pl.pallas_call(
        core_sum_kernel,
        in_specs=[pl.BlockSpec(memory_space=pltpu.SMEM), vmem, vmem],
        out_specs=[vmem] * 4,
        out_shape=[jax.ShapeDtypeStruct((SHARE, width), f32)]
        + [jax.ShapeDtypeStruct((SHARE, width), bf16)] * 3,
        compiler_params=params(16),
        cost_estimate=cost(1e6, 3e6),
        name="core_sum",
    )(high, keep, got)


def amplitude(own, received, row_energy, column_energy, occ_total):
    total = own
    for r in received:
        total = total + r.astype(f32)
    denominator = (row_energy[:, None] + column_energy[None, :]) - occ_total
    return (total / denominator).astype(bf16)


def density_kernel(place_ref, *refs, n_b, blocks, halves):
    shares = refs[:4]
    bs = refs[4 : 4 + n_b]
    outs = refs[4 + n_b : -2]
    tcat, bcat = refs[-2:]
    core = place_ref[0]
    high = place_ref[1]

    @pl.when(pl.program_id(0) == 0)
    def _():
        for piece in range(2):
            mine, other = shares[2 * piece], shares[2 * piece + 1]
            columns = slice(piece * 4 * ROWS, (piece + 1) * 4 * ROWS)
            for k in range(4):
                at = ((high - k + 4) % 4) * SHARE
                here = pl.multiple_of(core * (2 * ROWS) + at, SHARE)
                there = pl.multiple_of((1 - core) * (2 * ROWS) + at, SHARE)
                tcat[pl.ds(here, SHARE), columns] = mine[k * SHARE : (k + 1) * SHARE]
                tcat[pl.ds(there, SHARE), columns] = other[k * SHARE : (k + 1) * SHARE]

    at = 0
    for b in bs:
        bcat[at : at + b.shape[0]] = b[...]
        at += b.shape[0]
    first, last = blocks
    value = jnp.dot(
        tcat[first * ROWS : last * ROWS], bcat[...], preferred_element_type=f32
    )
    for i, out in enumerate(outs):
        rows = ROWS // 2 if halves else ROWS
        out[...] = value[i * rows : (i + 1) * rows].astype(out.dtype)


def density(place, shares, b_parts, blocks, halves, types):
    chunk = 512
    steps = AUX // chunk
    rows = ROWS // 2 if halves else ROWS
    whole = pl.BlockSpec((2 * ROWS, 4 * ROWS), lambda k, c: (0, 0))
    grid_spec = pltpu.PrefetchScalarGridSpec(
        num_scalar_prefetch=1,
        grid=(steps,),
        in_specs=[whole] * 4
        + [pl.BlockSpec((v.shape[0], chunk), lambda k, c: (0, k)) for v in b_parts],
        out_specs=[pl.BlockSpec((rows, chunk), lambda k, c: (0, k)) for _ in types],
        scratch_shapes=[
            pltpu.VMEM((4 * ROWS, 8 * ROWS), bf16),
            pltpu.VMEM((8 * ROWS, chunk), bf16),
        ],
    )
    n = blocks[1] - blocks[0]
    return pl.pallas_call(
        functools.partial(
            density_kernel, n_b=len(b_parts), blocks=blocks, halves=halves
        ),
        grid_spec=grid_spec,
        out_shape=[jax.ShapeDtypeStruct((rows, AUX), t) for t in types],
        compiler_params=params(32),
        cost_estimate=cost(2 * n * ROWS * 8 * ROWS * AUX, 2 * 8 * ROWS * AUX),
        name="density",
    )(place, *shares, *b_parts)


def local(integrals, tiles, tile_index, vir_energy, occ_energy, pair_index):
    group = lax.axis_index("grp").astype(jnp.int32)
    me = lax.axis_index("blk").astype(jnp.int32)
    high, core = group // 2, group % 2
    y, x, z = me // 8, (me // 2) % 4, me % 2
    place = jnp.stack([core, high])

    window = integrals.reshape(2 * ROWS, AUX)
    up = [(g, g + 1) for g in range(7)]
    down = [(g + 1, g) for g in range(7)]
    left = lax.ppermute(window[:, AUX - HALO :], "grp", up)
    right = lax.ppermute(window[:, :HALO], "grp", down)
    a, b = fit(left, window, right, tiles, tile_index.T)

    bm = send_y(b, 1)
    bp = send_y(b, -1)
    bo = send_outer(b)
    ax = send_inner(a)
    az = send_z(a)
    half = ROWS // 2
    d1 = send_inner(az[:half])
    d2 = send_z(ax[half:])
    a_parts = (a, ax, az, d1, d2)
    bom = send_y(bo, 1)
    b2 = send_y(bp, -1)
    bop = send_outer(bp)
    c1 = send_outer(b2[:64])
    c2 = send_y(bom[64:112], 1)
    c3 = send_y(bop[112:], -1)
    pieces = ((b, bm, bp, bo), (bom, b2, bop, c1, c2, c3))

    ox = jnp.asarray(OUTER, jnp.int32)[x]
    index = lambda yy, xx, zz: ((yy % 4) * 4 + xx) * 2 + zz
    energy = lambda at, n: lax.dynamic_slice_in_dim(vir_energy, at, n)
    columns = (
        (index(y, x, z), index(y + 3, x, z), index(y + 1, x, z), index(y, ox, z)),
        (index(y + 3, ox, z), index(y + 2, x, z), index(y + 1, ox, z), index(y + 2, ox, z)),
    )
    row_x = jnp.where(high < 2, x, x ^ 1)
    row_z = jnp.where(core == 0, z, 1 - z)
    row_energy = energy(index(y, row_x, row_z) * ROWS + (high % 2) * half, half)
    occ_total = occ_energy[pair_index[0]] + occ_energy[pair_index[1]]

    shares = []
    for parts, places in zip(pieces, columns):
        keep, send = pair(core[None], a_parts, parts)
        own, s1, s2, s3 = core_sum(high[None], keep, send_core(send))
        received = [send_high(s1, 1), send_high(s2, 2), send_high(s3, 3)]
        column_energy = jnp.concatenate([energy(p * ROWS, ROWS) for p in places])
        mine = amplitude(own, received, row_energy, column_energy, occ_total)
        mine = jnp.concatenate([mine] + [send_high(mine, k) for k in (1, 2, 3)], axis=0)
        shares += [mine, send_core(mine)]

    b_parts = (*pieces[0], *pieces[1])
    dense = functools.partial(density, place, shares, b_parts)
    to_d1, to_d2 = dense((3, 4), True, (bf16, bf16))
    x1, x2, z1, z2 = dense((1, 3), True, (bf16, f32, f32, bf16))
    o1, o2 = dense((0, 1), True, (f32, f32))
    from_x = send_inner(to_d1)
    from_z = send_z(to_d2)
    got_x1 = send_inner(x1)
    got_z2 = send_z(z2)
    got_z1 = send_z((z1 + from_x.astype(f32)).astype(bf16))
    got_x2 = send_inner((x2 + from_z.astype(f32)).astype(bf16))
    h1 = o1 + got_x1.astype(f32) + got_z1.astype(f32)
    h2 = o2 + got_x2.astype(f32) + got_z2.astype(f32)
    return jnp.concatenate([h1, h2], axis=0).astype(bf16)


def solution(mesh):
    in_specs = (P(None, "blk", "grp"), P("grp", None, None), P("grp", None), P(), P(), P())
    return jax.shard_map(
        local, mesh=mesh, in_specs=in_specs, out_specs=P("blk", "grp"), check_vma=False
    )
```

```python
import functools

import jax
import jax.numpy as jnp
from jax import lax
from jax.experimental import pallas as pl
from jax.experimental.pallas import tpu as pltpu
from jax.sharding import PartitionSpec as P

TILE = 128
HB = 4
BAND = 2 * HB + 1
ROWS = 160
AUX = 2560
HALO = HB * TILE
bf16 = jnp.bfloat16
f32 = jnp.float32
MIB = 1 << 20


def blk_index(y, x, z):
    return ((y % 4) * 4 + x) * 2 + z


PLACES = [(y, x, z) for y in range(4) for x in range(4) for z in range(2)]
OUTER = (3, 2, 1, 0)


def send_y(v, step):
    pairs = [(blk_index(y, x, z), blk_index(y + step, x, z)) for y, x, z in PLACES]
    return lax.ppermute(v, "blk", pairs)


def send_outer(v):
    pairs = [(blk_index(y, x, z), blk_index(y, OUTER[x], z)) for y, x, z in PLACES]
    return lax.ppermute(v, "blk", pairs)


def send_inner(v):
    pairs = [(blk_index(y, x, z), blk_index(y, x ^ 1, z)) for y, x, z in PLACES]
    return lax.ppermute(v, "blk", pairs)


def send_z(v):
    pairs = [(blk_index(y, x, z), blk_index(y, x, 1 - z)) for y, x, z in PLACES]
    return lax.ppermute(v, "blk", pairs)


def send_core(v):
    return lax.ppermute(v, "grp", [(g, g ^ 1) for g in range(8)])


def send_high(v, step):
    return lax.ppermute(v, "grp", [(g, (g + 2 * step) % 8) for g in range(8)])


def params():
    return pltpu.CompilerParams(vmem_limit_bytes=56 * MIB)


def cost(flops, nbytes):
    return pl.CostEstimate(flops=int(flops), bytes_accessed=int(nbytes), transcendentals=0)


def position():
    group = lax.axis_index("grp").astype(jnp.int32)
    me = lax.axis_index("blk").astype(jnp.int32)
    return group // 2, group % 2, me // 8, (me // 2) % 4, me % 2


def fit_kernel(index_ref, *refs, pairs, edge):
    if edge:
        left, own, right, tiles, _, _, out_a, out_b, ext, weights = refs
    else:
        own, tiles, out_a, out_b, weights = refs
    step = pl.program_id(0)
    p = pairs(step)

    @pl.when(step == 0)
    def _():
        if edge:
            ext[:, :HALO] = left[...]
            ext[:, HALO : 3 * HALO] = own[:, : 2 * HALO]
            ext[:, 3 * HALO : 5 * HALO] = own[:, AUX - 2 * HALO :]
            ext[:, 5 * HALO :] = right[...]
        weights[...] = jnp.zeros_like(weights)

    for q in range(2):
        for o in range(BAND):
            slot = q * BAND + o
            listed = index_ref[1, p * (2 * BAND) + slot] == 1
            tile = tiles[slot]
            j = q + o
            weights[j * TILE : (j + 1) * TILE, q * TILE : (q + 1) * TILE] = jnp.where(
                listed, tile, jnp.zeros_like(tile)
            )
    if edge:
        at = jnp.where(step < 2, step * 2, 12 + (step - 2) * 2) * TILE
        window = ext[:, pl.ds(pl.multiple_of(at, 2 * TILE), (BAND + 1) * TILE)]
    else:
        at = (p * 2 - HB) * TILE
        window = own[:, pl.ds(pl.multiple_of(at, 2 * TILE), (BAND + 1) * TILE)]
    fitted = jnp.dot(window, weights[...], preferred_element_type=f32).astype(bf16)
    out_a[...] = fitted[:ROWS]
    out_b[...] = fitted[ROWS:]


def fit(index, own, tiles, halos=None, partial=None):
    edge = halos is not None
    pairs = (lambda p: jnp.where(p < 2, p, p + 6)) if edge else (lambda p: p + 2)
    whole = lambda shape: pl.BlockSpec(shape, lambda p, i: (0, 0))
    own_spec = whole((2 * ROWS, AUX))
    halo_spec = whole((2 * ROWS, HALO))
    tile_spec = pl.BlockSpec((2 * BAND, TILE, TILE), lambda p, i: (pairs(p), 0, 0))
    anywhere = pl.BlockSpec(memory_space=pl.ANY)
    scratch = [pltpu.VMEM(((BAND + 1) * TILE, 2 * TILE), bf16)]
    if edge:
        in_specs = [halo_spec, own_spec, halo_spec, tile_spec, anywhere, anywhere]
        scratch = [pltpu.VMEM((2 * ROWS, 6 * HALO), bf16)] + scratch
        args = (halos[0], own, halos[1], tiles, *partial)
    else:
        in_specs = [own_spec, tile_spec]
        args = (own, tiles)
    grid_spec = pltpu.PrefetchScalarGridSpec(
        num_scalar_prefetch=1,
        grid=(4 if edge else 6,),
        in_specs=in_specs,
        out_specs=[pl.BlockSpec((ROWS, 2 * TILE), lambda p, i: (0, pairs(p)))] * 2,
        scratch_shapes=scratch,
    )
    return pl.pallas_call(
        functools.partial(fit_kernel, pairs=pairs, edge=edge),
        grid_spec=grid_spec,
        out_shape=[jax.ShapeDtypeStruct((ROWS, AUX), bf16)] * 2,
        input_output_aliases={5: 0, 6: 1} if edge else {},
        compiler_params=params(),
        cost_estimate=cost(1e9, 5e6),
        name="fit_edge" if edge else "fit_inner",
    )(index, *args)


def pair_kernel(*refs, n_a, steps):
    a_refs, bs = refs[:n_a], refs[n_a : -4 if n_a == 1 else -5]
    if n_a == 1:
        (acat,) = a_refs
        keep, send, bcat, acc = refs[-4:]
    else:
        keep, send, bcat, acat, acc = refs[-5:]
    k = pl.program_id(0)
    if n_a > 1:
        core = position()[1]
        at = pl.multiple_of(core * (2 * ROWS), 2 * ROWS)
        for i, a in enumerate(a_refs):
            if i == 2:
                at = pl.multiple_of((1 - core) * (2 * ROWS), 2 * ROWS)
            acat[pl.ds(at, a.shape[0])] = a[...]
            at = at + a.shape[0]
    at = 0
    for b in bs:
        bcat[at : at + b.shape[0]] = b[...]
        at += b.shape[0]
    product = lax.dot_general(
        acat[...], bcat[...], (((1,), (1,)), ((), ())), preferred_element_type=f32
    )

    @pl.when(k == 0)
    def _():
        acc[...] = product

    @pl.when(k > 0)
    def _():
        acc[...] += product

    @pl.when(k == steps - 1)
    def _():
        keep[...] = acc[: 2 * ROWS]
        send[...] = acc[2 * ROWS :].astype(bf16)


def pair(a_parts, b_parts):
    width = sum(b.shape[0] for b in b_parts)
    chunk = 512
    steps = AUX // chunk
    spec = lambda rows: pl.BlockSpec((rows, chunk), lambda k: (0, k))
    whole = pl.BlockSpec((2 * ROWS, width), lambda k: (0, 0))
    n_a = len(a_parts)
    first = n_a > 1
    return pl.pallas_call(
        functools.partial(pair_kernel, n_a=n_a, steps=steps),
        grid=(steps,),
        in_specs=[spec(v.shape[0]) for v in (*a_parts, *b_parts)],
        out_specs=[whole, whole, spec(width)] + [spec(4 * ROWS)] * first,
        scratch_shapes=[pltpu.VMEM((4 * ROWS, width), f32)],
        out_shape=[
            jax.ShapeDtypeStruct((2 * ROWS, width), f32),
            jax.ShapeDtypeStruct((2 * ROWS, width), bf16),
            jax.ShapeDtypeStruct((width, AUX), bf16),
        ]
        + [jax.ShapeDtypeStruct((4 * ROWS, AUX), bf16)] * first,
        compiler_params=params(),
        cost_estimate=cost(2 * 4 * ROWS * width * AUX, 2 * (4 * ROWS + width) * AUX),
        name="pair",
    )(*a_parts, *b_parts)


SHARE = ROWS // 2


def core_sum_kernel(keep, got, own, s1, s2, s3):
    high = position()[0]
    for step, out in enumerate((own, s1, s2, s3)):
        at = pl.multiple_of(((high + step) % 4) * SHARE, SHARE)
        value = keep[pl.ds(at, SHARE)] + got[pl.ds(at, SHARE)].astype(f32)
        out[...] = value.astype(out.dtype)


def core_sum(keep, got):
    width = keep.shape[1]
    vmem = pl.BlockSpec(memory_space=pltpu.VMEM)
    return pl.pallas_call(
        core_sum_kernel,
        in_specs=[vmem, vmem],
        out_specs=[vmem] * 4,
        out_shape=[jax.ShapeDtypeStruct((SHARE, width), f32)]
        + [jax.ShapeDtypeStruct((SHARE, width), bf16)] * 3,
        compiler_params=params(),
        cost_estimate=cost(1e6, 3e6),
        name="core_sum",
    )(keep, got)


def amplitude_kernel(vir, occ, chosen, own, r1, r2, r3, out, *, offsets):
    high, core, y, x, z = position()
    outer = 3 - x
    occ_total = occ[chosen[0]] + occ[chosen[1]]
    inner = x + 1 - 2 * (x % 2)
    row_x = jnp.where(high < 2, x, inner)
    row_z = jnp.where(core == 0, z, 1 - z)
    block = vir[pl.ds((y * 4 + row_x) * 2 + row_z, 1), :]
    lane = lax.broadcasted_iota(jnp.int32, (SHARE, ROWS), 1)
    row = lax.broadcasted_iota(jnp.int32, (SHARE, ROWS), 0)
    chosen_lane = lane == row + (high % 2) * SHARE
    rows = jnp.sum(jnp.where(chosen_lane, block, 0.0), axis=1, keepdims=True)
    total = own[...] + r1[...].astype(f32) + r2[...].astype(f32) + r3[...].astype(f32)
    for i, (step, away) in enumerate(offsets):
        at = (((y + step) % 4) * 4 + (outer if away else x)) * 2 + z
        columns = slice(i * ROWS, (i + 1) * ROWS)
        denominator = (rows + vir[pl.ds(at, 1), :]) - occ_total
        out[:, columns] = (total[:, columns] / denominator).astype(bf16)


def amplitude(vir, occ, chosen, own, received, offsets):
    vmem = pl.BlockSpec(memory_space=pltpu.VMEM)
    smem = pl.BlockSpec(memory_space=pltpu.SMEM)
    return pl.pallas_call(
        functools.partial(amplitude_kernel, offsets=offsets),
        in_specs=[vmem, smem, smem] + [vmem] * 4,
        out_specs=vmem,
        out_shape=jax.ShapeDtypeStruct(own.shape, bf16),
        compiler_params=params(),
        cost_estimate=cost(1e6, 1e6),
        name="amplitude",
    )(vir, occ, chosen, own, *received)


def density_kernel(*refs, blocks, halves):
    shares, bs, outs, tcat = refs[:4], refs[4:6], refs[6:-1], refs[-1]
    high, core = position()[:2]

    @pl.when(pl.program_id(0) == 0)
    def _():
        for piece in range(2):
            mine, other = shares[2 * piece], shares[2 * piece + 1]
            columns = slice(piece * 4 * ROWS, (piece + 1) * 4 * ROWS)
            for k in range(4):
                at = ((high - k + 4) % 4) * SHARE
                here = pl.multiple_of(core * (2 * ROWS) + at, SHARE)
                there = pl.multiple_of((1 - core) * (2 * ROWS) + at, SHARE)
                tcat[pl.ds(here, SHARE), columns] = mine[k * SHARE : (k + 1) * SHARE]
                tcat[pl.ds(there, SHARE), columns] = other[k * SHARE : (k + 1) * SHARE]

    rows = slice(blocks[0] * ROWS, blocks[1] * ROWS)
    value = jnp.dot(tcat[rows, : 4 * ROWS], bs[0][...], preferred_element_type=f32)
    value += jnp.dot(tcat[rows, 4 * ROWS :], bs[1][...], preferred_element_type=f32)
    for i, out in enumerate(outs):
        rows = ROWS // 2 if halves else ROWS
        out[...] = value[i * rows : (i + 1) * rows].astype(out.dtype)


def density(shares, b_parts, blocks, halves, types):
    chunk = 512
    steps = AUX // chunk
    rows = ROWS // 2 if halves else ROWS
    whole = pl.BlockSpec((2 * ROWS, 4 * ROWS), lambda k: (0, 0))
    n = blocks[1] - blocks[0]
    return pl.pallas_call(
        functools.partial(density_kernel, blocks=blocks, halves=halves),
        grid=(steps,),
        in_specs=[whole] * 4 + [pl.BlockSpec((4 * ROWS, chunk), lambda k: (0, k))] * 2,
        out_specs=[pl.BlockSpec((rows, chunk), lambda k: (0, k)) for _ in types],
        scratch_shapes=[pltpu.VMEM((4 * ROWS, 8 * ROWS), bf16)],
        out_shape=[jax.ShapeDtypeStruct((rows, AUX), t) for t in types],
        compiler_params=params(),
        cost_estimate=cost(2 * n * ROWS * 8 * ROWS * AUX, 2 * 8 * ROWS * AUX),
        name="density",
    )(*shares, *b_parts)


def local(integrals, tiles, tile_index, vir_energy, occ_energy, pair_index):
    window = integrals.reshape(2 * ROWS, AUX)
    index = tile_index.T
    vir = vir_energy.reshape(-1, ROWS)
    up = [(g, g + 1) for g in range(7)]
    down = [(g + 1, g) for g in range(7)]
    left = lax.ppermute(window[:, AUX - HALO :], "grp", up)
    right = lax.ppermute(window[:, :HALO], "grp", down)
    inner = fit(index, window, tiles)
    a, b = fit(index, window, tiles, (left, right), inner)

    half = ROWS // 2
    ax = send_inner(a)
    az = send_z(a)
    bm = send_y(b, 1)
    bp = send_y(b, -1)
    bo = send_outer(b)
    d1 = send_inner(az[:half])
    d2 = send_z(ax[half:])
    bom = send_y(bo, 1)
    b2 = send_y(bp, -1)
    bop = send_outer(bp)
    c1 = send_outer(b2[:64])
    c2 = send_y(bom[64:112], 1)
    c3 = send_y(bop[112:], -1)

    def reduced(keep, send, offsets):
        own, s1, s2, s3 = core_sum(keep, send_core(send))
        received = [send_high(s1, 1), send_high(s2, 2), send_high(s3, 3)]
        mine = amplitude(vir, occ_energy, pair_index, own, received, offsets)
        mine = jnp.concatenate([mine] + [send_high(mine, k) for k in (1, 2, 3)], axis=0)
        return [mine, send_core(mine)]

    keep, send, b_first, acat = pair((a, ax, az, d1, d2), (b, bm, bp, bo))
    shares = reduced(keep, send, ((0, 0), (3, 0), (1, 0), (0, 1)))
    keep, send, b_second = pair((acat,), (bom, b2, bop, c1, c2, c3))
    shares += reduced(keep, send, ((3, 1), (2, 0), (1, 1), (2, 1)))

    dense = functools.partial(density, shares, (b_first, b_second))
    to_d1, to_d2 = dense((3, 4), True, (bf16, bf16))
    x1, x2, z1, z2 = dense((1, 3), True, (bf16, f32, f32, bf16))
    o1, o2 = dense((0, 1), True, (f32, f32))
    from_x = send_inner(to_d1)
    from_z = send_z(to_d2)
    got_x1 = send_inner(x1)
    got_z2 = send_z(z2)
    got_z1 = send_z((z1 + from_x.astype(f32)).astype(bf16))
    got_x2 = send_inner((x2 + from_z.astype(f32)).astype(bf16))
    h1 = o1 + got_x1.astype(f32) + got_z1.astype(f32)
    h2 = o2 + got_x2.astype(f32) + got_z2.astype(f32)
    return jnp.concatenate([h1, h2], axis=0).astype(bf16)


def solution(mesh):
    in_specs = (P(None, "blk", "grp"), P("grp", None, None), P("grp", None), P(), P(), P())
    return jax.shard_map(
        local, mesh=mesh, in_specs=in_specs, out_specs=P("blk", "grp"), check_vma=False
    )
```

```python
import functools

import jax
import jax.numpy as jnp
from jax import lax
from jax.experimental import pallas as pl
from jax.experimental.pallas import tpu as pltpu
from jax.sharding import PartitionSpec as P

TILE = 128
HB = 4
BAND = 2 * HB + 1
ROWS = 160
AUX = 2560
HALO = HB * TILE
bf16 = jnp.bfloat16
f32 = jnp.float32
MIB = 1 << 20


def blk_index(y, x, z):
    return ((y % 4) * 4 + x) * 2 + z


PLACES = [(y, x, z) for y in range(4) for x in range(4) for z in range(2)]
OUTER = (3, 2, 1, 0)


def send_y(v, step):
    pairs = [(blk_index(y, x, z), blk_index(y + step, x, z)) for y, x, z in PLACES]
    return lax.ppermute(v, "blk", pairs)


def send_outer(v):
    pairs = [(blk_index(y, x, z), blk_index(y, OUTER[x], z)) for y, x, z in PLACES]
    return lax.ppermute(v, "blk", pairs)


def send_inner(v):
    pairs = [(blk_index(y, x, z), blk_index(y, x ^ 1, z)) for y, x, z in PLACES]
    return lax.ppermute(v, "blk", pairs)


def send_z(v):
    pairs = [(blk_index(y, x, z), blk_index(y, x, 1 - z)) for y, x, z in PLACES]
    return lax.ppermute(v, "blk", pairs)


def send_core(v):
    return lax.ppermute(v, "grp", [(g, g ^ 1) for g in range(8)])


def send_high(v, step):
    return lax.ppermute(v, "grp", [(g, (g + 2 * step) % 8) for g in range(8)])


def params(mib=40):
    return pltpu.CompilerParams(vmem_limit_bytes=mib * MIB)


def cost(flops, nbytes):
    return pl.CostEstimate(flops=int(flops), bytes_accessed=int(nbytes), transcendentals=0)


def position():
    group = lax.axis_index("grp").astype(jnp.int32)
    me = lax.axis_index("blk").astype(jnp.int32)
    return group // 2, group % 2, me // 8, (me // 2) % 4, me % 2


ANY = pl.BlockSpec(memory_space=pl.ANY)
VMEM = pl.BlockSpec(memory_space=pltpu.VMEM)
SMEM = pl.BlockSpec(memory_space=pltpu.SMEM)
DMA = pltpu.SemaphoreType.DMA
HALF = ROWS // 2
SHARE = ROWS // 2
WIDE = 4 * ROWS
K2 = AUX // 2


def hbm(shape, dtype=bf16):
    return jax.ShapeDtypeStruct(shape, dtype)


def vmem(shape, dtype=bf16):
    return pltpu.VMEM(shape, dtype)


def call(kernel, args, outs, scratch=(), name=None, flops=1e6, nbytes=1e6, aliases=None, mib=40):
    return pl.pallas_call(
        kernel,
        in_specs=[spec for _, spec in args],
        out_specs=[VMEM] * len(outs),
        out_shape=list(outs),
        scratch_shapes=list(scratch),
        input_output_aliases=aliases or {},
        compiler_params=params(mib),
        cost_estimate=cost(flops, nbytes),
        name=name,
    )(*[a for a, _ in args])


INNER = (2, 3, 4, 5, 6, 7)
EDGE = (0, 1, 8, 9)


def fit_inner_kernel(index, own_in, tiles_in, _, a, b, own, edge, tiles, weights, own_sem, sems):
    own_copies = [
        pltpu.make_async_copy(
            own_in.at[pl.ds(i * ROWS, ROWS)], own.at[pl.ds(i * ROWS, ROWS)], own_sem.at[i]
        )
        for i in range(2)
    ]
    copies = {}
    for p in INNER + EDGE:
        part = pl.ds(p * 2 * BAND, 2 * BAND)
        copies[p] = pltpu.make_async_copy(tiles_in.at[part], tiles.at[part], sems.at[p])
    copies[INNER[0]].start()
    for c in own_copies:
        c.start()
    for p in (INNER + EDGE)[1:]:
        copies[p].start()
    zero = jnp.zeros((TILE, TILE), bf16)

    def build(p, out):
        out[:TILE, TILE:] = zero
        out[BAND * TILE :, :TILE] = zero
        for q in range(2):
            for o in range(BAND):
                slot = p * 2 * BAND + q * BAND + o
                at = (q + o) * TILE
                out[at : at + TILE, q * TILE : (q + 1) * TILE] = jnp.where(
                    index[1, slot] == 1, tiles[slot], zero
                )

    for p in INNER:
        copies[p].wait()
        if p == INNER[0]:
            for c in own_copies:
                c.wait()
        build(p, weights)
        window = own[:, (2 * p - HB) * TILE : (2 * p + HB + 2) * TILE]
        fitted = jnp.dot(window, weights[...], preferred_element_type=f32).astype(bf16)
        columns = slice(p * 2 * TILE, (p + 1) * 2 * TILE)
        a[:, columns] = fitted[:ROWS]
        b[:, columns] = fitted[ROWS:]
    for n, p in enumerate(EDGE):
        copies[p].wait()
        build(p, edge.at[n])


def fit_edge_kernel(left, right, own, edge, _, __, a, b, ext):
    ext[:, :HALO] = left[...]
    ext[:, HALO : 3 * HALO] = own[:, : 2 * HALO]
    ext[:, 3 * HALO : 5 * HALO] = own[:, AUX - 2 * HALO :]
    ext[:, 5 * HALO :] = right[...]
    for n, p in enumerate(EDGE):
        at = (0, 2, 12, 14)[n] * TILE
        window = ext[:, at : at + (BAND + 1) * TILE]
        fitted = jnp.dot(window, edge[n], preferred_element_type=f32).astype(bf16)
        columns = slice(p * 2 * TILE, (p + 1) * 2 * TILE)
        a[:, columns] = fitted[:ROWS]
        b[:, columns] = fitted[ROWS:]


def fit(index, own, tiles, left, right, early):
    banded = ((BAND + 1) * TILE, 2 * TILE)
    a, b, own, edge = call(
        fit_inner_kernel,
        [(index, SMEM), (own, ANY), (tiles, ANY), (early, ANY)],
        [vmem((ROWS, AUX)), vmem((ROWS, AUX)), vmem((2 * ROWS, AUX)), vmem((4, *banded))],
        [pltpu.VMEM(tiles.shape, bf16), pltpu.VMEM(banded, bf16), DMA((2,)), DMA((10,))],
        name="fit_inner",
        mib=56,
        flops=1.2e9,
        nbytes=9e6,
    )
    return call(
        fit_edge_kernel,
        [(v, VMEM) for v in (left, right, own, edge, a, b)],
        [vmem((ROWS, AUX))] * 2,
        [pltpu.VMEM((2 * ROWS, 6 * HALO), bf16)],
        name="fit_edge",
        flops=8e8,
        aliases={4: 0, 5: 1},
    )


def cut(parts, after=(), name=None):
    def kernel(*refs):
        ins, outs, sems = refs[: len(parts)], refs[-1 - len(parts) : -1], refs[-1]
        copies = [
            pltpu.make_async_copy(i.at[pl.ds(at, n)], o, sems.at[j])
            for j, (i, o, (_, at, n)) in enumerate(zip(ins, outs, parts))
        ]
        for c in copies:
            c.start()
        for c in copies:
            c.wait()

    return pl.pallas_call(
        kernel,
        in_specs=[ANY] * (len(parts) + len(after)),
        out_specs=[ANY] * len(parts),
        out_shape=[hbm((n, AUX)) for _, _, n in parts],
        scratch_shapes=[DMA((len(parts),))],
        compiler_params=params(),
        cost_estimate=cost(1e5, 2e6),
        name=name,
    )(*[v for v, _, _ in parts], *after)


def row_copies(parts, out, sems, offsets):
    copies = []
    for h in range(2):
        columns = pl.ds(h * K2, K2)
        copies.append(
            [
                pltpu.make_async_copy(
                    p.at[:, columns], out.at[pl.ds(at, p.shape[0]), columns], sems.at[i, h]
                )
                for i, (p, at) in enumerate(zip(parts, offsets))
            ]
        )
    return copies


def b_offsets(parts, at=0):
    offsets = []
    for p in parts:
        offsets.append(at)
        at += p.shape[0]
    return offsets


def products(acat, bcat, rows, copies):
    total = None
    for h in range(2):
        for c in copies[h]:
            c.wait()
        columns = slice(h * K2, (h + 1) * K2)
        part = lax.dot_general(
            acat[:, columns], bcat[rows, columns], (((1,), (1,)), ((), ())),
            preferred_element_type=f32,
        )
        total = part if total is None else total + part
    return total


def pair_first_kernel(*refs):
    a_refs, b_refs = refs[:5], refs[5:9]
    keep, send, bcat, acat, a_sems, b_sems = refs[9:]
    core = position()[1]
    first = pl.multiple_of(core * (2 * ROWS), 2 * ROWS)
    second = pl.multiple_of((1 - core) * (2 * ROWS), 2 * ROWS)
    a_at = (first, first + ROWS, second, second + ROWS, second + ROWS + HALF)
    a_copies = row_copies(a_refs, acat, a_sems, a_at)
    b_copies = row_copies(b_refs, bcat, b_sems, b_offsets(b_refs))
    copies = [x + y for x, y in zip(a_copies, b_copies)]
    for half in copies:
        for c in half:
            c.start()
    total = products(acat, bcat, slice(0, WIDE), copies)
    keep[...] = total[: 2 * ROWS]
    send[...] = total[2 * ROWS :].astype(bf16)


def pair_first(a_parts, b_parts):
    return call(
        pair_first_kernel,
        [(v, ANY) for v in (*a_parts, *b_parts)],
        [
            vmem((2 * ROWS, WIDE), f32),
            hbm((2 * ROWS, WIDE)),
            vmem((WIDE, AUX)),
            vmem((WIDE, AUX)),
        ],
        [DMA((5, 2)), DMA((4, 2))],
        name="pair_first",
        flops=2 * WIDE * WIDE * AUX,
        nbytes=8e6,
    )


def pair_early_kernel(acat, *refs):
    b_refs = refs[:3]
    total, bcat, sems = refs[-3:]
    copies = row_copies(b_refs, bcat, sems, b_offsets(b_refs))
    for half in copies:
        for c in half:
            c.start()
    total[...] = products(acat, bcat, slice(0, 3 * ROWS), copies)


def pair_early(acat, b_parts):
    return call(
        pair_early_kernel,
        [(acat, VMEM)] + [(v, ANY) for v in b_parts],
        [vmem((WIDE, 3 * ROWS), f32), vmem((WIDE, AUX))],
        [DMA((3, 2))],
        name="pair_early",
        flops=2 * WIDE * 3 * ROWS * AUX,
        nbytes=4e6,
    )


def pair_late_kernel(acat, early, bcat_in, *refs):
    b_refs = refs[:3]
    keep, send, bcat, sems = refs[-4:]
    copies = row_copies(b_refs, bcat, sems, b_offsets(b_refs, 3 * ROWS))
    for half in copies:
        for c in half:
            c.start()
    columns = slice(0, 3 * ROWS)
    keep[:, columns] = early[: 2 * ROWS]
    send[:, columns] = early[2 * ROWS :].astype(bf16)
    total = products(acat, bcat, slice(3 * ROWS, WIDE), copies)
    columns = slice(3 * ROWS, WIDE)
    keep[:, columns] = total[: 2 * ROWS]
    send[:, columns] = total[2 * ROWS :].astype(bf16)


def pair_late(acat, early, bcat, b_parts, after):
    return call(
        pair_late_kernel,
        [(acat, VMEM), (early, VMEM), (bcat, VMEM)] + [(v, ANY) for v in (*b_parts, *after)],
        [vmem((2 * ROWS, WIDE), f32), hbm((2 * ROWS, WIDE)), vmem((WIDE, AUX))],
        [DMA((3, 2))],
        name="pair_late",
        flops=2 * WIDE * ROWS * AUX,
        nbytes=2e6,
        aliases={2: 2},
    )


def core_sum_kernel(keep, got_in, *refs):
    own, s1, s2, s3, got, sem = refs[-6:]
    copy = pltpu.make_async_copy(got_in, got, sem)
    copy.start()
    copy.wait()
    high = position()[0]
    for step, out in enumerate((own, s1, s2, s3)):
        at = pl.multiple_of(((high + step) % 4) * SHARE, SHARE)
        value = keep[pl.ds(at, SHARE)] + got[pl.ds(at, SHARE)].astype(f32)
        out[...] = value.astype(out.dtype)


def core_sum(keep, got, after):
    width = keep.shape[1]
    return call(
        core_sum_kernel,
        [(keep, VMEM), (got, ANY)] + [(v, ANY) for v in after],
        [vmem((SHARE, width), f32)] + [hbm((SHARE, width))] * 3,
        [pltpu.VMEM(got.shape, bf16), DMA(())],
        name="core_sum",
    )


def amplitude_kernel(vir, occ, chosen, own, *refs, offsets):
    arrived, out, got, sems = refs[:3], refs[-3], refs[-2], refs[-1]
    copies = [
        pltpu.make_async_copy(r, got.at[i], sems.at[i]) for i, r in enumerate(arrived)
    ]
    for c in copies:
        c.start()
    high, core, y, x, z = position()
    occ_total = occ[chosen[0]] + occ[chosen[1]]
    inner = x + 1 - 2 * (x % 2)
    row_x = jnp.where(high < 2, x, inner)
    row_z = jnp.where(core == 0, z, 1 - z)
    block = vir[pl.ds((y * 4 + row_x) * 2 + row_z, 1), :]
    lane = lax.broadcasted_iota(jnp.int32, (SHARE, ROWS), 1)
    row = lax.broadcasted_iota(jnp.int32, (SHARE, ROWS), 0)
    own_lane = lane == row + (high % 2) * SHARE
    rows = jnp.sum(jnp.where(own_lane, block, 0.0), axis=1, keepdims=True)
    columns = jnp.concatenate(
        [
            vir[pl.ds((((y + step) % 4) * 4 + (3 - x if away else x)) * 2 + z, 1), :]
            for step, away in offsets
        ],
        axis=1,
    )
    denominator = (rows + columns) - occ_total
    for c in copies:
        c.wait()
    total = own[...]
    for i in range(3):
        total = total + got[i].astype(f32)
    out[...] = (total / denominator).astype(bf16)


def amplitude(vir, occ, chosen, own, arrived, offsets, after=()):
    return call(
        functools.partial(amplitude_kernel, offsets=offsets),
        [(vir, VMEM), (occ, SMEM), (chosen, SMEM), (own, VMEM)]
        + [(v, ANY) for v in (*arrived, *after)],
        [hbm(own.shape)],
        [pltpu.VMEM((3, *own.shape), bf16), DMA((3,))],
        name="amplitude",
    )[0]


def density_part(tcat, b1, b2, blocks, outs):
    rows = slice(blocks[0] * ROWS, blocks[1] * ROWS)
    for h in range(2):
        columns = slice(h * K2, (h + 1) * K2)
        value = jnp.dot(tcat[rows, :WIDE], b1[:, columns], preferred_element_type=f32)
        value += jnp.dot(tcat[rows, WIDE:], b2[:, columns], preferred_element_type=f32)
        for i, out in enumerate(outs):
            out[:, columns] = value[i * HALF : (i + 1) * HALF].astype(out.dtype)


def density_first_kernel(*refs):
    mine, other = (refs[0:4], refs[4:8]), refs[8:10]
    b1, b2, o1, o2, tcat, sems = refs[10:]
    high, core = position()[:2]
    copies = []
    for k in range(4):
        at = ((high - k + 4) % 4) * SHARE
        here = pl.multiple_of(core * (2 * ROWS) + at, SHARE)
        there = pl.multiple_of((1 - core) * (2 * ROWS) + at, SHARE)
        for piece in range(2):
            columns = pl.ds(piece * WIDE, WIDE)
            copies.append(
                pltpu.make_async_copy(
                    mine[piece][k], tcat.at[pl.ds(here, SHARE), columns], sems.at[piece, k, 0]
                )
            )
            copies.append(
                pltpu.make_async_copy(
                    other[piece].at[pl.ds(k * SHARE, SHARE)],
                    tcat.at[pl.ds(there, SHARE), columns],
                    sems.at[piece, k, 1],
                )
            )
    for c in copies:
        c.start()
    for c in copies:
        c.wait()
    density_part(tcat, b1, b2, (3, 4), (o1, o2))


def density_first(mine, other, b1, b2):
    return call(
        density_first_kernel,
        [(v, ANY) for v in (*mine[0], *mine[1], *other)] + [(b1, VMEM), (b2, VMEM)],
        [hbm((HALF, AUX))] * 2 + [vmem((WIDE, 2 * WIDE))],
        [DMA((2, 4, 2))],
        name="density_first",
        flops=2 * ROWS * 2 * WIDE * AUX,
    )


def density(tcat, b1, b2, blocks, types):
    def kernel(tcat, b1, b2, *outs):
        density_part(tcat, b1, b2, blocks, outs)

    return call(
        kernel,
        [(tcat, VMEM), (b1, VMEM), (b2, VMEM)],
        [hbm((HALF, AUX), t) for t in types],
        name="density",
        flops=2 * (blocks[1] - blocks[0]) * ROWS * 2 * WIDE * AUX,
    )


def local(integrals, tiles, tile_index, vir_energy, occ_energy, pair_index):
    window = integrals.reshape(2 * ROWS, AUX)
    vir = vir_energy.reshape(-1, ROWS)
    up = [(g, g + 1) for g in range(7)]
    down = [(g + 1, g) for g in range(7)]
    left = lax.ppermute(window[:, AUX - HALO :], "grp", up)
    right = lax.ppermute(window[:, :HALO], "grp", down)
    a, b = fit(tile_index.T, window, tiles, left, right, vir)

    with jax.named_scope("first"):
        bm = send_y(b, 1)
        bp = send_y(b, -1)
        bo = send_outer(b)
        ax = send_inner(a)
        az = send_z(a)
    az1, ax2 = cut([(az, 0, HALF), (ax, HALF, HALF)], (bm, bp, bo), name="cut_a")
    with jax.named_scope("second"):
        d1 = send_inner(az1)
        d2 = send_z(ax2)
        bom = send_y(bo, 1)
        b2 = send_y(bp, -1)
        bop = send_outer(bp)

    def core_total(keep, send, after=()):
        with jax.named_scope("core"):
            return core_sum(keep, send_core(send), after)

    def shares(s):
        with jax.named_scope("shares"):
            return [send_high(v, k + 1) for k, v in enumerate(s)]

    def spread(mine):
        with jax.named_scope("spread"):
            return [mine] + [send_high(mine, k) for k in (1, 2, 3)]

    def other_core(mine):
        with jax.named_scope("other"):
            return send_core(jnp.concatenate(mine, axis=0))

    keep, send, b_first, acat = pair_first((a, ax, az, d1, d2), (b, bm, bp, bo))
    own, *s = core_total(keep, send)
    arrived = shares(s)
    c1, c2, c3 = cut([(b2, 0, 64), (bom, 64, 48), (bop, 112, 48)], (own,), name="cut_b")
    with jax.named_scope("third"):
        c1 = send_outer(c1)
        c2 = send_y(c2, 1)
        c3 = send_y(c3, -1)
    early, b_second = pair_early(acat, (bom, b2, bop))
    offsets = ((0, 0), (3, 0), (1, 0), (0, 1))
    mine1 = amplitude(vir, occ_energy, pair_index, own, arrived, offsets, (early,))
    keep, send, b_second = pair_late(acat, early, b_second, (c1, c2, c3), (mine1,))
    mine1 = spread(mine1)
    own, *s = core_total(keep, send, (mine1[1], mine1[3]))
    arrived = shares(s)
    offsets = ((3, 1), (2, 0), (1, 1), (2, 1))
    mine2 = spread(amplitude(vir, occ_energy, pair_index, own, arrived, offsets))
    other = (other_core(mine1), other_core(mine2))

    to_d1, to_d2, tcat = density_first((mine1, mine2), other, b_first, b_second)
    x1, x2, z1, z2 = density(tcat, b_first, b_second, (1, 3), (bf16, f32, f32, bf16))
    o1, o2 = density(tcat, b_first, b_second, (0, 1), (f32, f32))
    with jax.named_scope("out"):
        from_x = send_inner(to_d1)
        from_z = send_z(to_d2)
        got_x1 = send_inner(x1)
        got_z2 = send_z(z2)
        got_z1 = send_z((z1 + from_x.astype(f32)).astype(bf16))
        got_x2 = send_inner((x2 + from_z.astype(f32)).astype(bf16))
    h1 = o1 + got_x1.astype(f32) + got_z1.astype(f32)
    h2 = o2 + got_x2.astype(f32) + got_z2.astype(f32)
    return jnp.concatenate([h1, h2], axis=0).astype(bf16)


def solution(mesh):
    in_specs = (P(None, "blk", "grp"), P("grp", None, None), P("grp", None), P(), P(), P())
    return jax.shard_map(
        local, mesh=mesh, in_specs=in_specs, out_specs=P("blk", "grp"), check_vma=False
    )
```

```python
import functools

import jax
import jax.numpy as jnp
from jax import lax
from jax.experimental import pallas as pl
from jax.experimental.pallas import tpu as pltpu
from jax.sharding import PartitionSpec as P

TILE = 128
HB = 4
BAND = 2 * HB + 1
ROWS = 160
AUX = 2560
HALO = HB * TILE
bf16 = jnp.bfloat16
f32 = jnp.float32
MIB = 1 << 20


def blk_index(y, x, z):
    return ((y % 4) * 4 + x) * 2 + z


PLACES = [(y, x, z) for y in range(4) for x in range(4) for z in range(2)]
OUTER = (3, 2, 1, 0)


def send_y(v, step):
    pairs = [(blk_index(y, x, z), blk_index(y + step, x, z)) for y, x, z in PLACES]
    return lax.ppermute(v, "blk", pairs)


def send_outer(v):
    pairs = [(blk_index(y, x, z), blk_index(y, OUTER[x], z)) for y, x, z in PLACES]
    return lax.ppermute(v, "blk", pairs)


def send_inner(v):
    pairs = [(blk_index(y, x, z), blk_index(y, x ^ 1, z)) for y, x, z in PLACES]
    return lax.ppermute(v, "blk", pairs)


def send_z(v):
    pairs = [(blk_index(y, x, z), blk_index(y, x, 1 - z)) for y, x, z in PLACES]
    return lax.ppermute(v, "blk", pairs)


def send_core(v):
    return lax.ppermute(v, "grp", [(g, g ^ 1) for g in range(8)])


def send_high(v, step):
    return lax.ppermute(v, "grp", [(g, (g + 2 * step) % 8) for g in range(8)])


def params(mib=40):
    return pltpu.CompilerParams(vmem_limit_bytes=mib * MIB)


def cost():
    return pl.CostEstimate(flops=1000, bytes_accessed=1000, transcendentals=0)


def position():
    group = lax.axis_index("grp").astype(jnp.int32)
    me = lax.axis_index("blk").astype(jnp.int32)
    return group // 2, group % 2, me // 8, (me // 2) % 4, me % 2


ANY = pl.BlockSpec(memory_space=pl.ANY)
VMEM = pl.BlockSpec(memory_space=pltpu.VMEM)
SMEM = pl.BlockSpec(memory_space=pltpu.SMEM)
DMA = pltpu.SemaphoreType.DMA
HALF = ROWS // 2
SHARE = ROWS // 2
WIDE = 4 * ROWS
K2 = AUX // 2


def hbm(shape, dtype=bf16):
    return jax.ShapeDtypeStruct(shape, dtype)


def vmem(shape, dtype=bf16):
    return pltpu.VMEM(shape, dtype)


def call(kernel, args, outs, scratch=(), name=None, aliases=None, mib=40):
    return pl.pallas_call(
        kernel,
        in_specs=[spec for _, spec in args],
        out_specs=[VMEM] * len(outs),
        out_shape=list(outs),
        scratch_shapes=list(scratch),
        input_output_aliases=aliases or {},
        compiler_params=params(mib),
        cost_estimate=cost(),
        name=name,
    )(*[a for a, _ in args])


INNER = (2, 3, 4, 5, 6, 7)
EDGE = (0, 1, 8, 9)


def fit_inner_kernel(index, own_in, tiles_in, a, b, own, edge, inner, own_sem, sems):
    own_copies = [
        pltpu.make_async_copy(
            own_in.at[pl.ds(i * ROWS, ROWS)], own.at[pl.ds(i * ROWS, ROWS)], own_sem.at[i]
        )
        for i in range(2)
    ]
    where = {p: inner.at[n] for n, p in enumerate(INNER)}
    where |= {p: edge.at[n] for n, p in enumerate(EDGE)}
    depth = BAND * TILE
    copies = {
        p: [
            pltpu.make_async_copy(
                tiles_in.at[pl.ds((2 * p + q) * depth, depth)],
                where[p].at[pl.ds(q * TILE, depth), pl.ds(q * TILE, TILE)],
                sems.at[p, q],
            )
            for q in range(2)
        ]
        for p in INNER + EDGE
    }
    order = INNER + EDGE
    for c in copies[order[0]] + own_copies:
        c.start()
    for p in order[1:]:
        for c in copies[p]:
            c.start()
    zero = jnp.zeros((TILE, TILE), bf16)
    for p in order:
        where[p][:TILE, TILE:] = zero
        where[p][depth:, :TILE] = zero

    def ready(p):
        for c in copies[p]:
            c.wait()
        for q in range(2):
            for o in range(BAND):
                at = (q + o) * TILE

                @pl.when(index[1, p * 2 * BAND + q * BAND + o] == 0)
                def _():
                    where[p][at : at + TILE, q * TILE : (q + 1) * TILE] = zero

    for n, p in enumerate(INNER):
        ready(p)
        if n == 0:
            for c in own_copies:
                c.wait()
        window = own[:, (2 * p - HB) * TILE : (2 * p + HB + 2) * TILE]
        fitted = jnp.dot(window, inner[n], preferred_element_type=f32).astype(bf16)
        columns = slice(p * 2 * TILE, (p + 1) * 2 * TILE)
        a[:, columns] = fitted[:ROWS]
        b[:, columns] = fitted[ROWS:]
    for p in EDGE:
        ready(p)


def fit_edge_kernel(left, right, own, edge, _, __, a, b, ext):
    ext[:, :HALO] = left[...]
    ext[:, HALO : 3 * HALO] = own[:, : 2 * HALO]
    ext[:, 3 * HALO : 5 * HALO] = own[:, AUX - 2 * HALO :]
    ext[:, 5 * HALO :] = right[...]
    for n, p in enumerate(EDGE):
        at = (0, 2, 12, 14)[n] * TILE
        window = ext[:, at : at + (BAND + 1) * TILE]
        fitted = jnp.dot(window, edge[n], preferred_element_type=f32).astype(bf16)
        columns = slice(p * 2 * TILE, (p + 1) * 2 * TILE)
        a[:, columns] = fitted[:ROWS]
        b[:, columns] = fitted[ROWS:]


def fit(index, own, tiles, left, right):
    banded = ((BAND + 1) * TILE, 2 * TILE)
    a, b, own, edge = call(
        fit_inner_kernel,
        [(index, SMEM), (own, ANY), (tiles.reshape(-1, TILE), ANY)],
        [vmem((ROWS, AUX)), vmem((ROWS, AUX)), vmem((2 * ROWS, AUX)), vmem((4, *banded))],
        [pltpu.VMEM((6, *banded), bf16), DMA((2,)), DMA((10, 2))],
        name="fit_inner",
        mib=56,
    )
    return call(
        fit_edge_kernel,
        [(v, VMEM) for v in (left, right, own, edge, a, b)],
        [vmem((ROWS, AUX))] * 2,
        [pltpu.VMEM((2 * ROWS, 6 * HALO), bf16)],
        name="fit_edge",
        aliases={4: 0, 5: 1},
    )


def cut(parts, after=(), name=None, mib=40):
    parts = [(*p, 0, AUX)[:5] for p in parts]

    def kernel(*refs):
        ins, outs, sems = refs[: len(parts)], refs[-1 - len(parts) : -1], refs[-1]
        copies = [
            pltpu.make_async_copy(i.at[pl.ds(r, n), pl.ds(c, m)], o, sems.at[j])
            for j, (i, o, (_, r, n, c, m)) in enumerate(zip(ins, outs, parts))
        ]
        for c in copies:
            c.start()
        for c in copies:
            c.wait()

    return pl.pallas_call(
        kernel,
        in_specs=[ANY] * (len(parts) + len(after)),
        out_specs=[ANY] * len(parts),
        out_shape=[hbm((n, m)) for _, _, n, _, m in parts],
        scratch_shapes=[DMA((len(parts),))],
        compiler_params=params(mib),
        cost_estimate=cost(),
        name=name,
    )(*[p[0] for p in parts], *after)


def row_copies(parts, out, sems, offsets):
    copies = []
    for h in range(2):
        columns = pl.ds(h * K2, K2)
        copies.append(
            [
                pltpu.make_async_copy(
                    p.at[:, columns], out.at[pl.ds(at, p.shape[0]), columns], sems.at[i, h]
                )
                for i, (p, at) in enumerate(zip(parts, offsets))
            ]
        )
    return copies


def b_offsets(parts, at=0):
    offsets = []
    for p in parts:
        offsets.append(at)
        at += p.shape[0]
    return offsets


def products(acat, bcat, rows, copies):
    total = None
    for h in range(2):
        for c in copies[h]:
            c.wait()
        columns = slice(h * K2, (h + 1) * K2)
        part = lax.dot_general(
            acat[:, columns], bcat[rows, columns], (((1,), (1,)), ((), ())),
            preferred_element_type=f32,
        )
        total = part if total is None else total + part
    return total


def pair_first_kernel(*refs):
    a_refs, b_refs = refs[:5], refs[5:9]
    keep, send, bcat, acat, a_sems, b_sems = refs[9:]
    core = position()[1]
    first = pl.multiple_of(core * (2 * ROWS), 2 * ROWS)
    second = pl.multiple_of((1 - core) * (2 * ROWS), 2 * ROWS)
    a_at = (first, first + ROWS, second, second + ROWS, second + ROWS + HALF)
    a_copies = row_copies(a_refs, acat, a_sems, a_at)
    b_copies = row_copies(b_refs, bcat, b_sems, b_offsets(b_refs))
    copies = [x + y for x, y in zip(a_copies, b_copies)]
    for half in copies:
        for c in half:
            c.start()
    total = products(acat, bcat, slice(0, WIDE), copies)
    keep[...] = total[: 2 * ROWS]
    send[...] = total[2 * ROWS :].astype(bf16)


def pair_first(a_parts, b_parts):
    return call(
        pair_first_kernel,
        [(v, ANY) for v in (*a_parts, *b_parts)],
        [
            vmem((2 * ROWS, WIDE), f32),
            hbm((2 * ROWS, WIDE)),
            vmem((WIDE, AUX)),
            vmem((WIDE, AUX)),
        ],
        [DMA((5, 2)), DMA((4, 2))],
        name="pair_first",
    )


def pair_early_kernel(acat, *refs):
    b_refs = refs[:3]
    total, bcat, sems = refs[-3:]
    copies = row_copies(b_refs, bcat, sems, b_offsets(b_refs))
    for half in copies:
        for c in half:
            c.start()
    total[...] = products(acat, bcat, slice(0, 3 * ROWS), copies)


def pair_early(acat, b_parts):
    return call(
        pair_early_kernel,
        [(acat, VMEM)] + [(v, ANY) for v in b_parts],
        [vmem((WIDE, 3 * ROWS), f32), vmem((WIDE, AUX))],
        [DMA((3, 2))],
        name="pair_early",
    )


def pair_late_kernel(acat, early, bcat_in, *refs):
    b_refs = refs[:3]
    keep, send, bcat, sems = refs[-4:]
    copies = row_copies(b_refs, bcat, sems, b_offsets(b_refs, 3 * ROWS))
    for half in copies:
        for c in half:
            c.start()
    columns = slice(0, 3 * ROWS)
    keep[:, columns] = early[: 2 * ROWS]
    send[:, columns] = early[2 * ROWS :].astype(bf16)
    total = products(acat, bcat, slice(3 * ROWS, WIDE), copies)
    columns = slice(3 * ROWS, WIDE)
    keep[:, columns] = total[: 2 * ROWS]
    send[:, columns] = total[2 * ROWS :].astype(bf16)


def pair_late(acat, early, bcat, b_parts, after):
    return call(
        pair_late_kernel,
        [(acat, VMEM), (early, VMEM), (bcat, VMEM)] + [(v, ANY) for v in (*b_parts, *after)],
        [vmem((2 * ROWS, WIDE), f32), hbm((2 * ROWS, WIDE)), vmem((WIDE, AUX))],
        [DMA((3, 2))],
        name="pair_late",
        aliases={2: 2},
    )


def core_sum_kernel(keep, got_in, own, s1, s2, s3, got, sem):
    copy = pltpu.make_async_copy(got_in, got, sem)
    copy.start()
    copy.wait()
    high = position()[0]
    for step, out in enumerate((own, s1, s2, s3)):
        at = pl.multiple_of(((high + step) % 4) * SHARE, SHARE)
        value = keep[pl.ds(at, SHARE)] + got[pl.ds(at, SHARE)].astype(f32)
        out[...] = value.astype(out.dtype)


def core_sum(keep, got):
    width = keep.shape[1]
    return call(
        core_sum_kernel,
        [(keep, VMEM), (got, ANY)],
        [vmem((SHARE, width), f32)] + [hbm((SHARE, width))] * 3,
        [pltpu.VMEM(got.shape, bf16), DMA(())],
        name="core_sum",
    )


BLOCKS = ((0, 0), (3, 0), (1, 0), (0, 1), (3, 1), (2, 0), (1, 1), (2, 1))


def amplitude_kernel(vir, occ, chosen, own1, own2, *refs):
    arrived, out, got, sems = refs[:6], refs[-3], refs[-2], refs[-1]
    copies = [
        pltpu.make_async_copy(r, got.at[i], sems.at[i]) for i, r in enumerate(arrived)
    ]
    for c in copies:
        c.start()
    high, core, y, x, z = position()
    occ_total = occ[chosen[0]] + occ[chosen[1]]
    inner = x + 1 - 2 * (x % 2)
    row_x = jnp.where(high < 2, x, inner)
    row_z = jnp.where(core == 0, z, 1 - z)
    block = vir[pl.ds((y * 4 + row_x) * 2 + row_z, 1), :]
    lane = lax.broadcasted_iota(jnp.int32, (SHARE, ROWS), 1)
    row = lax.broadcasted_iota(jnp.int32, (SHARE, ROWS), 0)
    own_lane = lane == row + (high % 2) * SHARE
    rows = jnp.sum(jnp.where(own_lane, block, 0.0), axis=1, keepdims=True)
    columns = jnp.concatenate(
        [
            vir[pl.ds((((y + step) % 4) * 4 + (3 - x if away else x)) * 2 + z, 1), :]
            for step, away in BLOCKS
        ],
        axis=1,
    )
    denominator = (rows + columns) - occ_total
    for c in copies:
        c.wait()
    for piece, own in enumerate((own1, own2)):
        total = own[...]
        for i in range(3):
            total = total + got[3 * piece + i].astype(f32)
        part = slice(piece * WIDE, (piece + 1) * WIDE)
        out[:, part] = (total / denominator[:, part]).astype(bf16)


def amplitude(vir, occ, chosen, own1, own2, arrived):
    return call(
        amplitude_kernel,
        [(vir, VMEM), (occ, SMEM), (chosen, SMEM), (own1, VMEM), (own2, VMEM)]
        + [(v, ANY) for v in arrived],
        [hbm((SHARE, 2 * WIDE))],
        [pltpu.VMEM((6, SHARE, WIDE), bf16), DMA((6,))],
        name="amplitude",
    )[0]


def product(tcat, b1, b2, rows, half):
    columns = slice(half * K2, (half + 1) * K2)
    value = jnp.dot(tcat[rows, :WIDE], b1[:, columns], preferred_element_type=f32)
    return value + jnp.dot(tcat[rows, WIDE:], b2[:, columns], preferred_element_type=f32)


def density_first_kernel(*refs):
    mine, other = refs[:4], refs[4]
    b1, b2, d1, d2, x1, z2, tcat, sems = refs[5:]
    high, core = position()[:2]
    copies = []
    for k in range(4):
        at = ((high - k + 4) % 4) * SHARE
        here = pl.multiple_of(core * (2 * ROWS) + at, SHARE)
        there = pl.multiple_of((1 - core) * (2 * ROWS) + at, SHARE)
        away = other.at[pl.ds(k * SHARE, SHARE)]
        copies += [
            pltpu.make_async_copy(mine[k], tcat.at[pl.ds(here, SHARE)], sems.at[k, 0]),
            pltpu.make_async_copy(away, tcat.at[pl.ds(there, SHARE)], sems.at[k, 1]),
        ]
    for c in copies:
        c.start()
    for c in copies:
        c.wait()
    for half in range(2):
        columns = slice(half * K2, (half + 1) * K2)
        value = product(tcat, b1, b2, slice(3 * ROWS, 4 * ROWS), half).astype(bf16)
        d1[:, columns] = value[:HALF]
        d2[:, columns] = value[HALF:]
        rows = slice(ROWS, ROWS + HALF)
        x1[:, columns] = product(tcat, b1, b2, rows, half).astype(bf16)
        rows = slice(2 * ROWS + HALF, 3 * ROWS)
        z2[:, columns] = product(tcat, b1, b2, rows, half).astype(bf16)


def density_first(mine, other, b1, b2):
    return call(
        density_first_kernel,
        [(v, ANY) for v in (*mine, other)] + [(b1, VMEM), (b2, VMEM)],
        [hbm((HALF, AUX))] * 4 + [vmem((WIDE, 2 * WIDE))],
        [DMA((4, 2))],
        name="density_first",
    )


def density_second_kernel(tcat, b1, b2, from_x, from_z, x2, z1, own, got_x, got_z, sems):
    copies = [
        pltpu.make_async_copy(from_x, got_x, sems.at[0]),
        pltpu.make_async_copy(from_z, got_z, sems.at[1]),
    ]
    for c in copies:
        c.start()
    for half in range(2):
        columns = slice(half * K2, (half + 1) * K2)
        value = product(tcat, b1, b2, slice(ROWS + HALF, 2 * ROWS + HALF), half)
        if half == 0:
            for c in copies:
                c.wait()
        x2[:, columns] = (value[:HALF] + got_z[:, columns].astype(f32)).astype(bf16)
        z1[:, columns] = (value[HALF:] + got_x[:, columns].astype(f32)).astype(bf16)
        own[:, columns] = product(tcat, b1, b2, slice(0, ROWS), half)


def density_second(tcat, b1, b2, from_x, from_z):
    return call(
        density_second_kernel,
        [(v, VMEM) for v in (tcat, b1, b2)] + [(from_x, ANY), (from_z, ANY)],
        [hbm((HALF, AUX))] * 2 + [vmem((ROWS, AUX), f32)],
        [pltpu.VMEM((HALF, AUX), bf16)] * 2 + [DMA((2,))],
        name="density_second",
    )


def total_kernel(own, x1, z1, x2, z2, out, got, sems):
    copies = [
        pltpu.make_async_copy(v, got.at[i], sems.at[i]) for i, v in enumerate((x1, z1, x2, z2))
    ]
    for c in copies:
        c.start()
    for h in range(2):
        rows = slice(h * HALF, (h + 1) * HALF)
        for c in copies[2 * h : 2 * h + 2]:
            c.wait()
        value = own[rows] + got[2 * h].astype(f32) + got[2 * h + 1].astype(f32)
        out[rows] = value.astype(bf16)


def total(own, x1, z1, x2, z2):
    return call(
        total_kernel,
        [(own, VMEM)] + [(v, ANY) for v in (x1, z1, x2, z2)],
        [hbm((ROWS, AUX))],
        [pltpu.VMEM((4, HALF, AUX), bf16), DMA((4,))],
        name="total",
    )[0]


def local(integrals, tiles, tile_index, vir_energy, occ_energy, pair_index):
    window = integrals.reshape(2 * ROWS, AUX)
    vir = vir_energy.reshape(-1, ROWS)
    up = [(g, g + 1) for g in range(7)]
    down = [(g + 1, g) for g in range(7)]
    last, first = cut(
        [(window, 0, 2 * ROWS, AUX - HALO, HALO), (window, 0, 2 * ROWS, 0, HALO)],
        name="cut_halo",
        mib=60,
    )
    left = lax.ppermute(last, "grp", up)
    right = lax.ppermute(first, "grp", down)
    a, b = fit(tile_index.T, window, tiles, left, right)

    with jax.named_scope("first"):
        bm = send_y(b, 1)
        bp = send_y(b, -1)
        bo = send_outer(b)
        ax = send_inner(a)
        az = send_z(a)
    az1, ax2 = cut([(az, 0, HALF), (ax, HALF, HALF)], (bm, bp, bo, vir), name="cut_a")
    with jax.named_scope("second"):
        d1 = send_inner(az1)
        d2 = send_z(ax2)
        bom = send_y(bo, 1)
        b2 = send_y(bp, -1)
        bop = send_outer(bp)

    def core_total(keep, send):
        with jax.named_scope("core"):
            return core_sum(keep, send_core(send))

    def shares(s):
        with jax.named_scope("shares"):
            return [send_high(v, k + 1) for k, v in enumerate(s)]

    def spread(mine):
        with jax.named_scope("spread"):
            return [mine] + [send_high(mine, k) for k in (1, 2, 3)]

    def other_core(mine):
        with jax.named_scope("other"):
            return send_core(jnp.concatenate(mine, axis=0))

    keep, send, b_first, acat = pair_first((a, ax, az, d1, d2), (b, bm, bp, bo))
    own, *s = core_total(keep, send)
    arrived = shares(s)
    c1, c2, c3 = cut([(b2, 0, 64), (bom, 64, 48), (bop, 112, 48)], (own,), name="cut_b")
    with jax.named_scope("third"):
        c1 = send_outer(c1)
        c2 = send_y(c2, 1)
        c3 = send_y(c3, -1)
    early, b_second = pair_early(acat, (bom, b2, bop))
    keep, send, b_second = pair_late(acat, early, b_second, (c1, c2, c3), arrived)
    own2, *s = core_total(keep, send)
    arrived += shares(s)
    mine = spread(amplitude(vir, occ_energy, pair_index, own, own2, arrived))
    other = other_core(mine)
    to_d1, to_d2, x1, z2, tcat = density_first(mine, other, b_first, b_second)
    with jax.named_scope("out"):
        from_x = send_inner(to_d1)
        from_z = send_z(to_d2)
        got_x1 = send_inner(x1)
        got_z2 = send_z(z2)
    x2, z1, own = density_second(tcat, b_first, b_second, from_x, from_z)
    with jax.named_scope("out"):
        got_z1 = send_z(z1)
        got_x2 = send_inner(x2)
    return total(own, got_x1, got_z1, got_x2, got_z2)


def solution(mesh):
    in_specs = (P(None, "blk", "grp"), P("grp", None, None), P("grp", None), P(), P(), P())
    return jax.shard_map(
        local, mesh=mesh, in_specs=in_specs, out_specs=P("blk", "grp"), check_vma=False
    )
```

```python
import functools

import jax
import jax.numpy as jnp
from jax import lax
from jax.experimental import pallas as pl
from jax.experimental.pallas import tpu as pltpu
from jax.sharding import PartitionSpec as P

TILE = 128
HB = 4
BAND = 2 * HB + 1
ROWS = 160
AUX = 2560
HALO = HB * TILE
bf16 = jnp.bfloat16
f32 = jnp.float32
MIB = 1 << 20


def blk_index(y, x, z):
    return ((y % 4) * 4 + x) * 2 + z


PLACES = [(y, x, z) for y in range(4) for x in range(4) for z in range(2)]
OUTER = (3, 2, 1, 0)


def send_y(v, step):
    pairs = [(blk_index(y, x, z), blk_index(y + step, x, z)) for y, x, z in PLACES]
    return lax.ppermute(v, "blk", pairs)


def send_outer(v):
    pairs = [(blk_index(y, x, z), blk_index(y, OUTER[x], z)) for y, x, z in PLACES]
    return lax.ppermute(v, "blk", pairs)


def send_inner(v):
    pairs = [(blk_index(y, x, z), blk_index(y, x ^ 1, z)) for y, x, z in PLACES]
    return lax.ppermute(v, "blk", pairs)


def send_z(v):
    pairs = [(blk_index(y, x, z), blk_index(y, x, 1 - z)) for y, x, z in PLACES]
    return lax.ppermute(v, "blk", pairs)


def send_core(v):
    return lax.ppermute(v, "grp", [(g, g ^ 1) for g in range(8)])


def send_high(v, step):
    return lax.ppermute(v, "grp", [(g, (g + 2 * step) % 8) for g in range(8)])


def params(mib=40):
    return pltpu.CompilerParams(vmem_limit_bytes=mib * MIB)


def cost():
    return pl.CostEstimate(flops=1000, bytes_accessed=1000, transcendentals=0)


def position():
    group = lax.axis_index("grp").astype(jnp.int32)
    me = lax.axis_index("blk").astype(jnp.int32)
    return group // 2, group % 2, me // 8, (me // 2) % 4, me % 2


ANY = pl.BlockSpec(memory_space=pl.ANY)
VMEM = pl.BlockSpec(memory_space=pltpu.VMEM)
SMEM = pl.BlockSpec(memory_space=pltpu.SMEM)
DMA = pltpu.SemaphoreType.DMA
HALF = ROWS // 2
SHARE = ROWS // 2
WIDE = 4 * ROWS
K2 = AUX // 2


def hbm(shape, dtype=bf16):
    return jax.ShapeDtypeStruct(shape, dtype)


def vmem(shape, dtype=bf16):
    return pltpu.VMEM(shape, dtype)


def call(kernel, args, outs, scratch=(), name=None, aliases=None, mib=40):
    return pl.pallas_call(
        kernel,
        in_specs=[spec for _, spec in args],
        out_specs=[VMEM] * len(outs),
        out_shape=list(outs),
        scratch_shapes=list(scratch),
        input_output_aliases=aliases or {},
        compiler_params=params(mib),
        cost_estimate=cost(),
        name=name,
    )(*[a for a, _ in args])


INNER = (2, 3, 4, 5, 6, 7)
EDGE = (0, 1, 8, 9)


def fit_inner_kernel(index, own_in, tiles_in, a, b, own, edge, tiles, weights, own_sem, sems):
    own_copies = [
        pltpu.make_async_copy(
            own_in.at[pl.ds(i * ROWS, ROWS)], own.at[pl.ds(i * ROWS, ROWS)], own_sem.at[i]
        )
        for i in range(2)
    ]
    copies = {}
    for p in INNER + EDGE:
        part = pl.ds(p * 2 * BAND, 2 * BAND)
        copies[p] = pltpu.make_async_copy(tiles_in.at[part], tiles.at[part], sems.at[p])
    copies[INNER[0]].start()
    for c in own_copies:
        c.start()
    for p in (INNER + EDGE)[1:]:
        copies[p].start()
    zero = jnp.zeros((TILE, TILE), bf16)

    def build(p, out):
        out[:TILE, TILE:] = zero
        out[BAND * TILE :, :TILE] = zero
        for q in range(2):
            for o in range(BAND):
                slot = p * 2 * BAND + q * BAND + o
                at = (q + o) * TILE
                out[at : at + TILE, q * TILE : (q + 1) * TILE] = jnp.where(
                    index[1, slot] == 1, tiles[slot], zero
                )

    for p in INNER:
        copies[p].wait()
        if p == INNER[0]:
            for c in own_copies:
                c.wait()
        build(p, weights)
        window = own[:, (2 * p - HB) * TILE : (2 * p + HB + 2) * TILE]
        fitted = jnp.dot(window, weights[...], preferred_element_type=f32).astype(bf16)
        columns = slice(p * 2 * TILE, (p + 1) * 2 * TILE)
        a[:, columns] = fitted[:ROWS]
        b[:, columns] = fitted[ROWS:]
    for n, p in enumerate(EDGE):
        copies[p].wait()
        build(p, edge.at[n])


def fit_edge_kernel(left, right, own, edge, _, __, a, b, ext):
    ext[:, :HALO] = left[...]
    ext[:, HALO : 3 * HALO] = own[:, : 2 * HALO]
    ext[:, 3 * HALO : 5 * HALO] = own[:, AUX - 2 * HALO :]
    ext[:, 5 * HALO :] = right[...]
    for n, p in enumerate(EDGE):
        at = (0, 2, 12, 14)[n] * TILE
        window = ext[:, at : at + (BAND + 1) * TILE]
        fitted = jnp.dot(window, edge[n], preferred_element_type=f32).astype(bf16)
        columns = slice(p * 2 * TILE, (p + 1) * 2 * TILE)
        a[:, columns] = fitted[:ROWS]
        b[:, columns] = fitted[ROWS:]


def fit(index, own, tiles, left, right):
    banded = ((BAND + 1) * TILE, 2 * TILE)
    a, b, own, edge = call(
        fit_inner_kernel,
        [(index, SMEM), (own, ANY), (tiles, ANY)],
        [vmem((ROWS, AUX)), vmem((ROWS, AUX)), vmem((2 * ROWS, AUX)), vmem((4, *banded))],
        [pltpu.VMEM(tiles.shape, bf16), pltpu.VMEM(banded, bf16), DMA((2,)), DMA((10,))],
        name="fit_inner",
        mib=56,
    )
    return call(
        fit_edge_kernel,
        [(v, VMEM) for v in (left, right, own, edge, a, b)],
        [vmem((ROWS, AUX))] * 2,
        [pltpu.VMEM((2 * ROWS, 6 * HALO), bf16)],
        name="fit_edge",
        aliases={4: 0, 5: 1},
    )


def ends_kernel(own, last, first, sems):
    copies = [
        pltpu.make_async_copy(own.at[:, pl.ds(AUX - HALO, HALO)], last, sems.at[0]),
        pltpu.make_async_copy(own.at[:, pl.ds(0, HALO)], first, sems.at[1]),
    ]
    for c in copies:
        c.start()
    for c in copies:
        c.wait()


def ends(own):
    outs = [vmem((2 * ROWS, HALO))] * 2
    return call(ends_kernel, [(own, ANY)], outs, [DMA((2,))], name="ends", mib=60)


def cut(parts, after=(), name=None):
    def kernel(*refs):
        ins, outs, sems = refs[: len(parts)], refs[-1 - len(parts) : -1], refs[-1]
        copies = [
            pltpu.make_async_copy(i.at[pl.ds(r, n)], o, sems.at[j])
            for j, (i, o, (_, r, n)) in enumerate(zip(ins, outs, parts))
        ]
        for c in copies:
            c.start()
        for c in copies:
            c.wait()

    return pl.pallas_call(
        kernel,
        in_specs=[ANY] * (len(parts) + len(after)),
        out_specs=[ANY] * len(parts),
        out_shape=[hbm((n, AUX)) for _, _, n in parts],
        scratch_shapes=[DMA((len(parts),))],
        compiler_params=params(),
        cost_estimate=cost(),
        name=name,
    )(*[p[0] for p in parts], *after)


def row_copies(parts, out, sems, offsets):
    copies = []
    for h in range(2):
        columns = pl.ds(h * K2, K2)
        copies.append(
            [
                pltpu.make_async_copy(
                    p.at[:, columns], out.at[pl.ds(at, p.shape[0]), columns], sems.at[i, h]
                )
                for i, (p, at) in enumerate(zip(parts, offsets))
            ]
        )
    return copies


def b_offsets(parts, at=0):
    offsets = []
    for p in parts:
        offsets.append(at)
        at += p.shape[0]
    return offsets


def products(acat, bcat, rows, copies):
    total = None
    for h in range(2):
        for c in copies[h]:
            c.wait()
        columns = slice(h * K2, (h + 1) * K2)
        part = lax.dot_general(
            acat[:, columns], bcat[rows, columns], (((1,), (1,)), ((), ())),
            preferred_element_type=f32,
        )
        total = part if total is None else total + part
    return total


def pair_first_kernel(*refs):
    a_refs, b_refs = refs[:5], refs[5:9]
    keep, send, bcat, acat, a_sems, b_sems = refs[9:]
    core = position()[1]
    first = pl.multiple_of(core * (2 * ROWS), 2 * ROWS)
    second = pl.multiple_of((1 - core) * (2 * ROWS), 2 * ROWS)
    a_at = (first, first + ROWS, second, second + ROWS, second + ROWS + HALF)
    a_copies = row_copies(a_refs, acat, a_sems, a_at)
    b_copies = row_copies(b_refs, bcat, b_sems, b_offsets(b_refs))
    copies = [x + y for x, y in zip(a_copies, b_copies)]
    for half in copies:
        for c in half:
            c.start()
    total = products(acat, bcat, slice(0, WIDE), copies)
    keep[...] = total[: 2 * ROWS]
    send[...] = total[2 * ROWS :].astype(bf16)


def pair_first(a_parts, b_parts):
    return call(
        pair_first_kernel,
        [(v, ANY) for v in (*a_parts, *b_parts)],
        [
            vmem((2 * ROWS, WIDE), f32),
            hbm((2 * ROWS, WIDE)),
            vmem((WIDE, AUX)),
            vmem((WIDE, AUX)),
        ],
        [DMA((5, 2)), DMA((4, 2))],
        name="pair_first",
    )


def pair_early_kernel(acat, *refs):
    b_refs = refs[:3]
    total, bcat, sems = refs[-3:]
    copies = row_copies(b_refs, bcat, sems, b_offsets(b_refs))
    for half in copies:
        for c in half:
            c.start()
    total[...] = products(acat, bcat, slice(0, 3 * ROWS), copies)


def pair_early(acat, b_parts):
    return call(
        pair_early_kernel,
        [(acat, VMEM)] + [(v, ANY) for v in b_parts],
        [vmem((WIDE, 3 * ROWS), f32), vmem((WIDE, AUX))],
        [DMA((3, 2))],
        name="pair_early",
    )


def pair_late_kernel(acat, early, bcat_in, *refs):
    b_refs = refs[:3]
    keep, send, bcat, sems = refs[-4:]
    copies = row_copies(b_refs, bcat, sems, b_offsets(b_refs, 3 * ROWS))
    for half in copies:
        for c in half:
            c.start()
    columns = slice(0, 3 * ROWS)
    keep[:, columns] = early[: 2 * ROWS]
    send[:, columns] = early[2 * ROWS :].astype(bf16)
    total = products(acat, bcat, slice(3 * ROWS, WIDE), copies)
    columns = slice(3 * ROWS, WIDE)
    keep[:, columns] = total[: 2 * ROWS]
    send[:, columns] = total[2 * ROWS :].astype(bf16)


def pair_late(acat, early, bcat, b_parts, after):
    return call(
        pair_late_kernel,
        [(acat, VMEM), (early, VMEM), (bcat, VMEM)] + [(v, ANY) for v in (*b_parts, *after)],
        [vmem((2 * ROWS, WIDE), f32), hbm((2 * ROWS, WIDE)), vmem((WIDE, AUX))],
        [DMA((3, 2))],
        name="pair_late",
        aliases={2: 2},
    )


def core_sum_kernel(keep, got_in, own, s1, s2, s3, got, sem):
    copy = pltpu.make_async_copy(got_in, got, sem)
    copy.start()
    copy.wait()
    high = position()[0]
    for step, out in enumerate((own, s1, s2, s3)):
        at = pl.multiple_of(((high + step) % 4) * SHARE, SHARE)
        value = keep[pl.ds(at, SHARE)] + got[pl.ds(at, SHARE)].astype(f32)
        out[...] = value.astype(out.dtype)


def core_sum(keep, got):
    width = keep.shape[1]
    return call(
        core_sum_kernel,
        [(keep, VMEM), (got, ANY)],
        [vmem((SHARE, width), f32)] + [hbm((SHARE, width))] * 3,
        [pltpu.VMEM(got.shape, bf16), DMA(())],
        name="core_sum",
    )


BLOCKS = ((0, 0), (3, 0), (1, 0), (0, 1), (3, 1), (2, 0), (1, 1), (2, 1))


def amplitude_kernel(vir, occ, chosen, own1, own2, *refs):
    arrived, out, got, sems = refs[:6], refs[-3], refs[-2], refs[-1]
    copies = [
        pltpu.make_async_copy(r, got.at[i], sems.at[i]) for i, r in enumerate(arrived)
    ]
    for c in copies:
        c.start()
    high, core, y, x, z = position()
    occ_total = occ[chosen[0]] + occ[chosen[1]]
    inner = x + 1 - 2 * (x % 2)
    row_x = jnp.where(high < 2, x, inner)
    row_z = jnp.where(core == 0, z, 1 - z)
    block = vir[pl.ds((y * 4 + row_x) * 2 + row_z, 1), :]
    lane = lax.broadcasted_iota(jnp.int32, (SHARE, ROWS), 1)
    row = lax.broadcasted_iota(jnp.int32, (SHARE, ROWS), 0)
    own_lane = lane == row + (high % 2) * SHARE
    rows = jnp.sum(jnp.where(own_lane, block, 0.0), axis=1, keepdims=True)
    columns = jnp.concatenate(
        [
            vir[pl.ds((((y + step) % 4) * 4 + (3 - x if away else x)) * 2 + z, 1), :]
            for step, away in BLOCKS
        ],
        axis=1,
    )
    denominator = (rows + columns) - occ_total
    for c in copies:
        c.wait()
    for piece, own in enumerate((own1, own2)):
        total = own[...]
        for i in range(3):
            total = total + got[3 * piece + i].astype(f32)
        part = slice(piece * WIDE, (piece + 1) * WIDE)
        out[:, part] = (total / denominator[:, part]).astype(bf16)


def amplitude(vir, occ, chosen, own1, own2, arrived):
    return call(
        amplitude_kernel,
        [(vir, VMEM), (occ, SMEM), (chosen, SMEM), (own1, VMEM), (own2, VMEM)]
        + [(v, ANY) for v in arrived],
        [hbm((SHARE, 2 * WIDE))],
        [pltpu.VMEM((6, SHARE, WIDE), bf16), DMA((6,))],
        name="amplitude",
    )[0]


def product(tcat, b1, b2, rows, half):
    columns = slice(half * K2, (half + 1) * K2)
    value = jnp.dot(tcat[rows, :WIDE], b1[:, columns], preferred_element_type=f32)
    return value + jnp.dot(tcat[rows, WIDE:], b2[:, columns], preferred_element_type=f32)


def density_first_kernel(*refs):
    mine, other = refs[:4], refs[4]
    b1, b2, d1, d2, x1, z2, tcat, sems = refs[5:]
    high, core = position()[:2]
    copies = []
    for k in range(4):
        share = (high - k + 4) % 4
        of_0 = jnp.where(share < 2, share, 8 - 2 * share)
        of_1 = jnp.where(share == 0, 3, share + 4)
        here = pl.multiple_of(jnp.where(core == 0, of_0, of_1) * SHARE, SHARE)
        there = pl.multiple_of(jnp.where(core == 0, of_1, of_0) * SHARE, SHARE)
        away = other.at[pl.ds(k * SHARE, SHARE)]
        copies += [
            pltpu.make_async_copy(mine[k], tcat.at[pl.ds(here, SHARE)], sems.at[k, 0]),
            pltpu.make_async_copy(away, tcat.at[pl.ds(there, SHARE)], sems.at[k, 1]),
        ]
    for c in copies:
        c.start()
    for c in copies:
        c.wait()
    for half in range(2):
        columns = slice(half * K2, (half + 1) * K2)
        value = product(tcat, b1, b2, slice(2 * ROWS, 4 * ROWS), half).astype(bf16)
        for i, out in enumerate((x1, z2, d1, d2)):
            out[:, columns] = value[i * HALF : (i + 1) * HALF]


def density_first(mine, other, b1, b2):
    return call(
        density_first_kernel,
        [(v, ANY) for v in (*mine, other)] + [(b1, VMEM), (b2, VMEM)],
        [hbm((HALF, AUX))] * 4 + [vmem((WIDE, 2 * WIDE))],
        [DMA((4, 2))],
        name="density_first",
    )


def density_second_kernel(tcat, b1, b2, from_x, from_z, x2, z1, own, got_x, got_z, sems):
    copies = [
        pltpu.make_async_copy(from_x, got_x, sems.at[0]),
        pltpu.make_async_copy(from_z, got_z, sems.at[1]),
    ]
    for c in copies:
        c.start()
    for half in range(2):
        columns = slice(half * K2, (half + 1) * K2)
        value = product(tcat, b1, b2, slice(0, 2 * ROWS), half)
        if half == 0:
            for c in copies:
                c.wait()
        x = value[ROWS : ROWS + HALF] + got_z[:, columns].astype(f32)
        z = value[ROWS + HALF :] + got_x[:, columns].astype(f32)
        x2[:, columns] = x.astype(bf16)
        z1[:, columns] = z.astype(bf16)
        own[:, columns] = value[:ROWS]


def density_second(tcat, b1, b2, from_x, from_z):
    return call(
        density_second_kernel,
        [(v, VMEM) for v in (tcat, b1, b2)] + [(from_x, ANY), (from_z, ANY)],
        [hbm((HALF, AUX))] * 2 + [vmem((ROWS, AUX), f32)],
        [pltpu.VMEM((HALF, AUX), bf16)] * 2 + [DMA((2,))],
        name="density_second",
    )


def total_kernel(own, x1, z1, x2, z2, out, got, sems):
    copies = [
        pltpu.make_async_copy(v, got.at[i], sems.at[i]) for i, v in enumerate((x1, z1, x2, z2))
    ]
    for c in copies:
        c.start()
    for h in range(2):
        rows = slice(h * HALF, (h + 1) * HALF)
        for c in copies[2 * h : 2 * h + 2]:
            c.wait()
        value = own[rows] + got[2 * h].astype(f32) + got[2 * h + 1].astype(f32)
        out[rows] = value.astype(bf16)


def total(own, x1, z1, x2, z2):
    return call(
        total_kernel,
        [(own, VMEM)] + [(v, ANY) for v in (x1, z1, x2, z2)],
        [hbm((ROWS, AUX))],
        [pltpu.VMEM((4, HALF, AUX), bf16), DMA((4,))],
        name="total",
    )[0]


def local(integrals, tiles, tile_index, vir_energy, occ_energy, pair_index):
    window = integrals.reshape(2 * ROWS, AUX)
    vir = vir_energy.reshape(-1, ROWS)
    up = [(g, g + 1) for g in range(7)]
    down = [(g + 1, g) for g in range(7)]
    last, first = ends(window)
    left = lax.ppermute(last, "grp", up)
    right = lax.ppermute(first, "grp", down)
    a, b = fit(tile_index.T, window, tiles, left, right)

    with jax.named_scope("first"):
        bm = send_y(b, 1)
        bp = send_y(b, -1)
        bo = send_outer(b)
        ax = send_inner(a)
        az = send_z(a)
    az1, ax2 = cut([(az, 0, HALF), (ax, HALF, HALF)], (bm, bp, bo, vir), name="cut_a")
    with jax.named_scope("second"):
        d1 = send_inner(az1)
        d2 = send_z(ax2)
        bom = send_y(bo, 1)
        b2 = send_y(bp, -1)
        bop = send_outer(bp)

    def core_total(keep, send):
        with jax.named_scope("core"):
            return core_sum(keep, send_core(send))

    def shares(s):
        with jax.named_scope("shares"):
            return [send_high(v, k + 1) for k, v in enumerate(s)]

    def spread(mine):
        with jax.named_scope("spread"):
            return [mine] + [send_high(mine, k) for k in (1, 2, 3)]

    def other_core(mine):
        with jax.named_scope("other"):
            return send_core(jnp.concatenate(mine, axis=0))

    keep, send, b_first, acat = pair_first((a, ax, az, d1, d2), (b, bm, bp, bo))
    own, *s = core_total(keep, send)
    arrived = shares(s)
    c1, c2, c3 = cut([(b2, 0, 64), (bom, 64, 48), (bop, 112, 48)], (own,), name="cut_b")
    with jax.named_scope("third"):
        c1 = send_outer(c1)
        c2 = send_y(c2, 1)
        c3 = send_y(c3, -1)
    early, b_second = pair_early(acat, (bom, b2, bop))
    keep, send, b_second = pair_late(acat, early, b_second, (c1, c2, c3), arrived[1:2])
    own2, *s = core_total(keep, send)
    arrived += shares(s)
    mine = spread(amplitude(vir, occ_energy, pair_index, own, own2, arrived))
    other = other_core(mine)
    to_d1, to_d2, x1, z2, tcat = density_first(mine, other, b_first, b_second)
    with jax.named_scope("out"):
        from_x = send_inner(to_d1)
        from_z = send_z(to_d2)
        got_x1 = send_inner(x1)
        got_z2 = send_z(z2)
    x2, z1, own = density_second(tcat, b_first, b_second, from_x, from_z)
    with jax.named_scope("out"):
        got_z1 = send_z(z1)
        got_x2 = send_inner(x2)
    return total(own, got_x1, got_z1, got_x2, got_z2)


def solution(mesh):
    in_specs = (P(None, "blk", "grp"), P("grp", None, None), P("grp", None), P(), P(), P())
    return jax.shard_map(
        local, mesh=mesh, in_specs=in_specs, out_specs=P("blk", "grp"), check_vma=False
    )
```

```python
import functools

import jax
import jax.numpy as jnp
from jax import lax
from jax.experimental import pallas as pl
from jax.experimental.pallas import tpu as pltpu
from jax.sharding import PartitionSpec as P

TILE = 128
HB = 4
BAND = 2 * HB + 1
ROWS = 160
AUX = 2560
HALO = HB * TILE
bf16 = jnp.bfloat16
f32 = jnp.float32
MIB = 1 << 20


def blk_index(y, x, z):
    return ((y % 4) * 4 + x) * 2 + z


PLACES = [(y, x, z) for y in range(4) for x in range(4) for z in range(2)]
OUTER = (3, 2, 1, 0)


def send_y(v, step):
    pairs = [(blk_index(y, x, z), blk_index(y + step, x, z)) for y, x, z in PLACES]
    return lax.ppermute(v, "blk", pairs)


def send_outer(v):
    pairs = [(blk_index(y, x, z), blk_index(y, OUTER[x], z)) for y, x, z in PLACES]
    return lax.ppermute(v, "blk", pairs)


def send_inner(v):
    pairs = [(blk_index(y, x, z), blk_index(y, x ^ 1, z)) for y, x, z in PLACES]
    return lax.ppermute(v, "blk", pairs)


def send_z(v):
    pairs = [(blk_index(y, x, z), blk_index(y, x, 1 - z)) for y, x, z in PLACES]
    return lax.ppermute(v, "blk", pairs)


def send_core(v):
    return lax.ppermute(v, "grp", [(g, g ^ 1) for g in range(8)])


def send_high(v, step):
    return lax.ppermute(v, "grp", [(g, (g + 2 * step) % 8) for g in range(8)])


def params(mib=28):
    return pltpu.CompilerParams(vmem_limit_bytes=mib * MIB)


def cost():
    return pl.CostEstimate(flops=1000, bytes_accessed=1000, transcendentals=0)


def position():
    group = lax.axis_index("grp").astype(jnp.int32)
    me = lax.axis_index("blk").astype(jnp.int32)
    return group // 2, group % 2, me // 8, (me // 2) % 4, me % 2


ANY = pl.BlockSpec(memory_space=pl.ANY)
VMEM = pl.BlockSpec(memory_space=pltpu.VMEM)
SMEM = pl.BlockSpec(memory_space=pltpu.SMEM)
DMA = pltpu.SemaphoreType.DMA
HALF = ROWS // 2
SHARE = ROWS // 2
WIDE = 4 * ROWS
K2 = AUX // 2


def hbm(shape, dtype=bf16):
    return jax.ShapeDtypeStruct(shape, dtype)


def vmem(shape, dtype=bf16):
    return pltpu.VMEM(shape, dtype)


def call(kernel, args, outs, scratch=(), name=None, aliases=None, mib=28):
    return pl.pallas_call(
        kernel,
        in_specs=[spec for _, spec in args],
        out_specs=[VMEM] * len(outs),
        out_shape=list(outs),
        scratch_shapes=list(scratch),
        input_output_aliases=aliases or {},
        compiler_params=params(mib),
        cost_estimate=cost(),
        name=name,
    )(*[a for a, _ in args])


INNER = (2, 3, 4, 5, 6, 7)
EDGE = (0, 1, 8, 9)


def fit_inner_kernel(index, own_in, tiles_in, a, b, own, edge, tiles, weights, own_sem, sems):
    own_copies = [
        pltpu.make_async_copy(
            own_in.at[pl.ds(i * ROWS, ROWS)], own.at[pl.ds(i * ROWS, ROWS)], own_sem.at[i]
        )
        for i in range(2)
    ]
    copies = {}
    for p in INNER + EDGE:
        part = pl.ds(p * 2 * BAND, 2 * BAND)
        copies[p] = pltpu.make_async_copy(tiles_in.at[part], tiles.at[part], sems.at[p])
    copies[INNER[0]].start()
    for c in own_copies:
        c.start()
    for p in (INNER + EDGE)[1:]:
        copies[p].start()
    zero = jnp.zeros((TILE, TILE), bf16)

    def build(p, out):
        out[:TILE, TILE:] = zero
        out[BAND * TILE :, :TILE] = zero
        for q in range(2):
            for o in range(BAND):
                slot = p * 2 * BAND + q * BAND + o
                at = (q + o) * TILE
                out[at : at + TILE, q * TILE : (q + 1) * TILE] = jnp.where(
                    index[1, slot] == 1, tiles[slot], zero
                )

    for p in INNER:
        copies[p].wait()
        if p == INNER[0]:
            for c in own_copies:
                c.wait()
        build(p, weights)
        window = own[:, (2 * p - HB) * TILE : (2 * p + HB + 2) * TILE]
        fitted = jnp.dot(window, weights[...], preferred_element_type=f32).astype(bf16)
        columns = slice(p * 2 * TILE, (p + 1) * 2 * TILE)
        a[:, columns] = fitted[:ROWS]
        b[:, columns] = fitted[ROWS:]
    for n, p in enumerate(EDGE):
        copies[p].wait()
        build(p, edge.at[n])


def fit_edge_kernel(left, right, own, edge, _, __, a, b, ext):
    ext[:, :HALO] = left[...]
    ext[:, HALO : 3 * HALO] = own[:, : 2 * HALO]
    ext[:, 3 * HALO : 5 * HALO] = own[:, AUX - 2 * HALO :]
    ext[:, 5 * HALO :] = right[...]
    for n, p in enumerate(EDGE):
        at = (0, 2, 12, 14)[n] * TILE
        window = ext[:, at : at + (BAND + 1) * TILE]
        fitted = jnp.dot(window, edge[n], preferred_element_type=f32).astype(bf16)
        columns = slice(p * 2 * TILE, (p + 1) * 2 * TILE)
        a[:, columns] = fitted[:ROWS]
        b[:, columns] = fitted[ROWS:]


def fit(index, own, tiles, left, right):
    banded = ((BAND + 1) * TILE, 2 * TILE)
    a, b, own, edge = call(
        fit_inner_kernel,
        [(index, SMEM), (own, ANY), (tiles, ANY)],
        [vmem((ROWS, AUX)), vmem((ROWS, AUX)), vmem((2 * ROWS, AUX)), vmem((4, *banded))],
        [pltpu.VMEM(tiles.shape, bf16), pltpu.VMEM(banded, bf16), DMA((2,)), DMA((10,))],
        name="fit_inner",
        mib=56,
    )
    return call(
        fit_edge_kernel,
        [(v, VMEM) for v in (left, right, own, edge, a, b)],
        [vmem((ROWS, AUX))] * 2,
        [pltpu.VMEM((2 * ROWS, 6 * HALO), bf16)],
        name="fit_edge",
        aliases={4: 0, 5: 1},
    )


def ends_kernel(own, last, first, sems):
    copies = [
        pltpu.make_async_copy(own.at[:, pl.ds(AUX - HALO, HALO)], last, sems.at[0]),
        pltpu.make_async_copy(own.at[:, pl.ds(0, HALO)], first, sems.at[1]),
    ]
    for c in copies:
        c.start()
    for c in copies:
        c.wait()


def ends(own):
    outs = [vmem((2 * ROWS, HALO))] * 2
    return call(ends_kernel, [(own, ANY)], outs, [DMA((2,))], name="ends", mib=60)


def cut(parts, after=(), name=None):
    def kernel(*refs):
        ins, outs, sems = refs[: len(parts)], refs[-1 - len(parts) : -1], refs[-1]
        copies = [
            pltpu.make_async_copy(i.at[pl.ds(r, n)], o, sems.at[j])
            for j, (i, o, (_, r, n)) in enumerate(zip(ins, outs, parts))
        ]
        for c in copies:
            c.start()
        for c in copies:
            c.wait()

    return pl.pallas_call(
        kernel,
        in_specs=[ANY] * (len(parts) + len(after)),
        out_specs=[ANY] * len(parts),
        out_shape=[hbm((n, AUX)) for _, _, n in parts],
        scratch_shapes=[DMA((len(parts),))],
        compiler_params=params(),
        cost_estimate=cost(),
        name=name,
    )(*[p[0] for p in parts], *after)


def arrive(parts, after):
    n = len(parts)
    return pl.pallas_call(
        lambda *refs: None,
        in_specs=[ANY] * (n + len(after)),
        out_specs=[ANY] * n,
        out_shape=[hbm(v.shape, v.dtype) for v in parts],
        input_output_aliases={i: i for i in range(n)},
        compiler_params=params(),
        cost_estimate=cost(),
        name="arrive",
    )(*parts, *after)


def row_copies(moves, out, sems):
    return [
        [
            pltpu.make_async_copy(
                v.at[pl.ds(r, n), pl.ds(h * K2, K2)],
                out.at[pl.ds(at, n), pl.ds(h * K2, K2)],
                sems.at[i, h],
            )
            for i, (v, r, n, at) in enumerate(moves)
        ]
        for h in range(2)
    ]


def b_moves(parts, at=0):
    moves = []
    for p in parts:
        moves.append((p, 0, p.shape[0], at))
        at += p.shape[0]
    return moves


def products(acat, bcat, rows, copies):
    for half in copies:
        for c in half:
            c.start()
    total = None
    for h in range(2):
        for c in copies[h]:
            c.wait()
        columns = slice(h * K2, (h + 1) * K2)
        part = lax.dot_general(
            acat[:, columns], bcat[rows, columns], (((1,), (1,)), ((), ())),
            preferred_element_type=f32,
        )
        total = part if total is None else total + part
    return total


def pair_early_kernel(own, ax, az, ad, *refs):
    b_refs = refs[:7]
    total, bcat, acat, a_sems, b_sems = refs[7:]
    a_moves = [
        (own, 0, ROWS, 0),
        (ax, 0, HALF, 2 * ROWS),
        (ax, HALF, HALF, ROWS),
        (az, 0, HALF, ROWS + HALF),
        (az, HALF, HALF, 2 * ROWS + HALF),
        (ad, 0, ROWS, 3 * ROWS),
    ]
    a_copies = row_copies(a_moves, acat, a_sems)
    b_copies = row_copies(b_moves(b_refs), bcat, b_sems)
    copies = [x + y for x, y in zip(a_copies, b_copies)]
    total[...] = products(acat, bcat, slice(0, 7 * ROWS), copies)


def pair_early(a_parts, b_parts):
    return call(
        pair_early_kernel,
        [(v, ANY) for v in (*a_parts, *b_parts)],
        [vmem((WIDE, 7 * ROWS), f32), vmem((2 * WIDE, AUX)), vmem((WIDE, AUX))],
        [DMA((6, 2)), DMA((7, 2))],
        name="pair_early",
    )


def pair_late_kernel(acat, early, bcat_in, *refs):
    b_refs = refs[:3]
    keep, send, bcat, sems = refs[3:]
    copies = row_copies(b_moves(b_refs, 7 * ROWS), bcat, sems)
    late = products(acat, bcat, slice(7 * ROWS, 8 * ROWS), copies)
    core = position()[1]
    split = 3 * ROWS

    @pl.when(core == 0)
    def _():
        keep[...] = early[:, :WIDE]
        send[:, :split] = early[:, WIDE:].astype(bf16)
        send[:, split:] = late.astype(bf16)

    @pl.when(core == 1)
    def _():
        send[...] = early[:, :WIDE].astype(bf16)
        keep[:, :split] = early[:, WIDE:]
        keep[:, split:] = late


def pair_late(acat, early, bcat, b_parts):
    return call(
        pair_late_kernel,
        [(acat, VMEM), (early, VMEM), (bcat, VMEM)] + [(v, ANY) for v in b_parts],
        [vmem((WIDE, WIDE), f32), hbm((WIDE, WIDE)), vmem((2 * WIDE, AUX))],
        [DMA((3, 2))],
        name="pair_late",
        aliases={2: 2},
    )


def core_sum_kernel(keep, got_in, *refs):
    outs, got, sem = refs[:8], refs[8], refs[9]
    copy = pltpu.make_async_copy(got_in, got, sem)
    copy.start()
    copy.wait()
    high = position()[0]
    for wave in range(2):
        for step in range(4):
            at = pl.multiple_of((1 - wave) * 2 * ROWS + ((high + step) % 4) * SHARE, SHARE)
            value = keep[pl.ds(at, SHARE)] + got[pl.ds(at, SHARE)].astype(f32)
            out = outs[4 * wave + step]
            out[...] = value.astype(out.dtype)


def core_sum(keep, got):
    share = (SHARE, WIDE)
    outs = call(
        core_sum_kernel,
        [(keep, VMEM), (got, ANY)],
        ([vmem(share, f32)] + [hbm(share)] * 3) * 2,
        [pltpu.VMEM(got.shape, bf16), DMA(())],
        name="core_sum",
    )
    return outs[:4], outs[4:]


BLOCKS = (((0, 0), (3, 0), (1, 0), (0, 1)), ((3, 1), (2, 0), (1, 1), (2, 1)))


def amplitude_kernel(vir, occ, chosen, own, *refs, wave):
    arrived, out, got, sems = refs[:3], refs[-3], refs[-2], refs[-1]
    copies = [
        pltpu.make_async_copy(r, got.at[i], sems.at[i]) for i, r in enumerate(arrived)
    ]
    for c in copies:
        c.start()
    high, core, y, x, z = position()
    occ_total = occ[chosen[0]] + occ[chosen[1]]
    if wave == 0:
        in_x, in_z, second = (high != 1), (high != 0), high % 2
    else:
        in_x, in_z = (high == 2), (high == 3)
        second = jnp.where((high == 1) | (high == 2), 1, 0)
    row_x = jnp.where(in_x, x + 1 - 2 * (x % 2), x)
    row_z = jnp.where(in_z, 1 - z, z)
    block = vir[pl.ds((y * 4 + row_x) * 2 + row_z, 1), :]
    lane = lax.broadcasted_iota(jnp.int32, (SHARE, ROWS), 1)
    row = lax.broadcasted_iota(jnp.int32, (SHARE, ROWS), 0)
    own_lane = lane == row + second * SHARE
    rows = jnp.sum(jnp.where(own_lane, block, 0.0), axis=1, keepdims=True)
    places = []
    for first, last in zip(*BLOCKS):
        step = jnp.where(core == 0, first[0], last[0])
        away = jnp.where(core == 0, first[1], last[1])
        places.append((((y + step) % 4) * 4 + jnp.where(away == 1, 3 - x, x)) * 2 + z)
    columns = jnp.concatenate([vir[pl.ds(at, 1), :] for at in places], axis=1)
    denominator = (rows + columns) - occ_total
    for c in copies:
        c.wait()
    total = own[...]
    for i in range(3):
        total = total + got[i].astype(f32)
    out[...] = (total / denominator).astype(bf16)


def amplitude(vir, occ, chosen, own, arrived, wave, after=()):
    return call(
        functools.partial(amplitude_kernel, wave=wave),
        [(vir, VMEM), (occ, SMEM), (chosen, SMEM), (own, VMEM)]
        + [(v, ANY) for v in (*arrived, *after)],
        [hbm(own.shape)],
        [pltpu.VMEM((3, *own.shape), bf16), DMA((3,))],
        name=f"amplitude_{wave}",
    )[0]


def gather_rows(mine, other, tcat, sems):
    high, core = position()[:2]
    copies = []
    for k in range(4):
        rows = pl.ds(pl.multiple_of(((high - k + 4) % 4) * SHARE, SHARE), SHARE)
        for i, (v, of) in enumerate(((mine[k], core), (other[k], 1 - core))):
            columns = pl.ds(pl.multiple_of(of * WIDE, WIDE), WIDE)
            copies.append(pltpu.make_async_copy(v, tcat.at[rows, columns], sems.at[k, i]))
    for c in copies:
        c.start()
    return copies


def product(tcat, bcat, half):
    columns = slice(half * K2, (half + 1) * K2)
    return jnp.dot(tcat[...], bcat[:, columns], preferred_element_type=f32)


TCAT = (2 * ROWS, 2 * WIDE)


def density_first_kernel(*refs):
    mine, other, bcat = refs[:4], refs[4:8], refs[8]
    outs, tcat, sems = refs[9:13], refs[13], refs[14]
    for c in gather_rows(mine, other, tcat, sems):
        c.wait()
    for half in range(2):
        columns = slice(half * K2, (half + 1) * K2)
        value = product(tcat, bcat, half).astype(bf16)
        for i, out in enumerate(outs):
            out[:, columns] = value[i * HALF : (i + 1) * HALF]


def density_first(mine, other, bcat):
    return call(
        density_first_kernel,
        [(v, ANY) for v in (*mine, *other)] + [(bcat, VMEM)],
        [hbm((HALF, AUX))] * 4,
        [pltpu.VMEM(TCAT, bf16), DMA((4, 2))],
        name="density_first",
    )


def density_second_kernel(*refs):
    mine, other, (bcat, from_x, from_z) = refs[:4], refs[4:8], refs[8:11]
    x2, z1, own, tcat, got_x, got_z, row_sems, sems = refs[11:]
    rows_copies = gather_rows(mine, other, tcat, row_sems)
    copies = [
        pltpu.make_async_copy(from_x, got_x, sems.at[0]),
        pltpu.make_async_copy(from_z, got_z, sems.at[1]),
    ]
    for c in copies:
        c.start()
    for c in rows_copies:
        c.wait()
    for half in range(2):
        columns = slice(half * K2, (half + 1) * K2)
        value = product(tcat, bcat, half)
        if half == 0:
            for c in copies:
                c.wait()
        x = value[ROWS : ROWS + HALF] + got_z[:, columns].astype(f32)
        z = value[ROWS + HALF :] + got_x[:, columns].astype(f32)
        x2[:, columns] = x.astype(bf16)
        z1[:, columns] = z.astype(bf16)
        own[:, columns] = value[:ROWS]


def density_second(mine, other, bcat, from_x, from_z):
    return call(
        density_second_kernel,
        [(v, ANY) for v in (*mine, *other)]
        + [(bcat, VMEM), (from_x, ANY), (from_z, ANY)],
        [hbm((HALF, AUX))] * 2 + [vmem((ROWS, AUX), f32)],
        [pltpu.VMEM(TCAT, bf16)]
        + [pltpu.VMEM((HALF, AUX), bf16)] * 2
        + [DMA((4, 2)), DMA((2,))],
        name="density_second",
    )


def total_kernel(own, x1, z1, x2, z2, out, got, sems):
    copies = [
        pltpu.make_async_copy(v, got.at[i], sems.at[i]) for i, v in enumerate((x1, z1, x2, z2))
    ]
    for c in copies:
        c.start()
    for h in range(2):
        rows = slice(h * HALF, (h + 1) * HALF)
        for c in copies[2 * h : 2 * h + 2]:
            c.wait()
        value = own[rows] + got[2 * h].astype(f32) + got[2 * h + 1].astype(f32)
        out[rows] = value.astype(bf16)


def total(own, x1, z1, x2, z2):
    return call(
        total_kernel,
        [(own, VMEM)] + [(v, ANY) for v in (x1, z1, x2, z2)],
        [hbm((ROWS, AUX))],
        [pltpu.VMEM((4, HALF, AUX), bf16), DMA((4,))],
        name="total",
    )[0]


def local(integrals, tiles, tile_index, vir_energy, occ_energy, pair_index):
    window = integrals.reshape(2 * ROWS, AUX)
    vir = vir_energy.reshape(-1, ROWS)
    up = [(g, g + 1) for g in range(7)]
    down = [(g + 1, g) for g in range(7)]
    last, first = ends(window)
    left = lax.ppermute(last, "grp", up)
    right = lax.ppermute(first, "grp", down)
    a, b = fit(tile_index.T, window, tiles, left, right)

    with jax.named_scope("first"):
        bm = send_y(b, 1)
        bp = send_y(b, -1)
        bo = send_outer(b)
        ax = send_inner(a)
        az = send_z(a)
    bo, bp, az = arrive((bo, bp, az), (bm, ax, vir))
    with jax.named_scope("second"):
        bom = send_y(bo, 1)
        b2 = send_y(bp, -1)
        bop = send_outer(bp)
        ad = send_inner(az)
    c1, c2, c3 = cut([(b2, 0, 64), (bom, 64, 48), (bop, 112, 48)], name="cut_b")
    with jax.named_scope("third"):
        c1 = send_outer(c1)
        c2 = send_y(c2, 1)
        c3 = send_y(c3, -1)
    early, bcat, acat = pair_early((a, ax, az, ad), (b, bm, bp, bo, bom, b2, bop))
    keep, send, bcat = pair_late(acat, early, bcat, (c1, c2, c3))
    with jax.named_scope("core"):
        first, second = core_sum(keep, send_core(send))

    def summed(wave, own, *s, after=()):
        with jax.named_scope(f"shares_{wave}"):
            arrived = [send_high(v, k + 1) for k, v in enumerate(s)]
        mine = amplitude(vir, occ_energy, pair_index, own, arrived, wave, after)
        with jax.named_scope(f"spread_{wave}"):
            return [mine] + [send_high(mine, k) for k in (1, 2, 3)]

    def other_core(wave, mine):
        with jax.named_scope(f"other_{wave}"):
            return [send_core(v) for v in mine]

    mine0 = summed(0, *first)
    mine1 = summed(1, *second)
    other0 = other_core(0, mine0)
    other1 = other_core(1, mine1)
    x1, z2, to_d1, to_d2 = density_first(mine0, other0, bcat)
    with jax.named_scope("out"):
        from_x = send_inner(to_d1)
        from_z = send_z(to_d2)
        got_x1 = send_inner(x1)
        got_z2 = send_z(z2)
    x2, z1, own = density_second(mine1, other1, bcat, from_x, from_z)
    with jax.named_scope("out"):
        got_z1 = send_z(z1)
        got_x2 = send_inner(x2)
    return total(own, got_x1, got_z1, got_x2, got_z2)


def solution(mesh):
    in_specs = (P(None, "blk", "grp"), P("grp", None, None), P("grp", None), P(), P(), P())
    return jax.shard_map(
        local, mesh=mesh, in_specs=in_specs, out_specs=P("blk", "grp"), check_vma=False
    )
```

```python
import functools

import jax
import jax.numpy as jnp
from jax import lax
from jax.experimental import pallas as pl
from jax.experimental.pallas import tpu as pltpu
from jax.sharding import PartitionSpec as P

TILE = 128
HB = 4
BAND = 2 * HB + 1
ROWS = 160
AUX = 2560
HALO = HB * TILE
bf16 = jnp.bfloat16
f32 = jnp.float32
MIB = 1 << 20


def blk_index(y, x, z):
    return ((y % 4) * 4 + x) * 2 + z


PLACES = [(y, x, z) for y in range(4) for x in range(4) for z in range(2)]
OUTER = (3, 2, 1, 0)


def send_y(v, step):
    pairs = [(blk_index(y, x, z), blk_index(y + step, x, z)) for y, x, z in PLACES]
    return lax.ppermute(v, "blk", pairs)


def send_outer(v):
    pairs = [(blk_index(y, x, z), blk_index(y, OUTER[x], z)) for y, x, z in PLACES]
    return lax.ppermute(v, "blk", pairs)


def send_inner(v):
    pairs = [(blk_index(y, x, z), blk_index(y, x ^ 1, z)) for y, x, z in PLACES]
    return lax.ppermute(v, "blk", pairs)


def send_z(v):
    pairs = [(blk_index(y, x, z), blk_index(y, x, 1 - z)) for y, x, z in PLACES]
    return lax.ppermute(v, "blk", pairs)


def send_core(v):
    return lax.ppermute(v, "grp", [(g, g ^ 1) for g in range(8)])


def send_high(v, step):
    return lax.ppermute(v, "grp", [(g, (g + 2 * step) % 8) for g in range(8)])


def params(mib=28):
    return pltpu.CompilerParams(vmem_limit_bytes=mib * MIB)


def cost():
    return pl.CostEstimate(flops=1000, bytes_accessed=1000, transcendentals=0)


def position():
    group = lax.axis_index("grp").astype(jnp.int32)
    me = lax.axis_index("blk").astype(jnp.int32)
    return group // 2, group % 2, me // 8, (me // 2) % 4, me % 2


ANY = pl.BlockSpec(memory_space=pl.ANY)
VMEM = pl.BlockSpec(memory_space=pltpu.VMEM)
SMEM = pl.BlockSpec(memory_space=pltpu.SMEM)
DMA = pltpu.SemaphoreType.DMA
HALF = ROWS // 2
SHARE = ROWS // 2
WIDE = 4 * ROWS
K2 = AUX // 2


def hbm(shape, dtype=bf16):
    return jax.ShapeDtypeStruct(shape, dtype)


def vmem(shape, dtype=bf16):
    return pltpu.VMEM(shape, dtype)


def call(kernel, args, outs, scratch=(), name=None, aliases=None, mib=28):
    return pl.pallas_call(
        kernel,
        in_specs=[spec for _, spec in args],
        out_specs=[VMEM] * len(outs),
        out_shape=list(outs),
        scratch_shapes=list(scratch),
        input_output_aliases=aliases or {},
        compiler_params=params(mib),
        cost_estimate=cost(),
        name=name,
    )(*[a for a, _ in args])


INNER = (2, 3, 4, 5, 6, 7)
EDGE = (0, 1, 8, 9)


def fit_inner_kernel(index, own_in, tiles_in, a, b, own, edge, tiles, weights, own_sem, sems):
    own_copies = [
        pltpu.make_async_copy(
            own_in.at[pl.ds(i * ROWS, ROWS)], own.at[pl.ds(i * ROWS, ROWS)], own_sem.at[i]
        )
        for i in range(2)
    ]
    copies = {}
    for p in INNER + EDGE:
        part = pl.ds(p * 2 * BAND, 2 * BAND)
        copies[p] = pltpu.make_async_copy(tiles_in.at[part], tiles.at[part], sems.at[p])
    copies[INNER[0]].start()
    for c in own_copies:
        c.start()
    for p in (INNER + EDGE)[1:]:
        copies[p].start()
    zero = jnp.zeros((TILE, TILE), bf16)

    def build(p, out):
        out[:TILE, TILE:] = zero
        out[BAND * TILE :, :TILE] = zero
        for q in range(2):
            for o in range(BAND):
                slot = p * 2 * BAND + q * BAND + o
                at = (q + o) * TILE
                out[at : at + TILE, q * TILE : (q + 1) * TILE] = jnp.where(
                    index[1, slot] == 1, tiles[slot], zero
                )

    for p in INNER:
        copies[p].wait()
        if p == INNER[0]:
            for c in own_copies:
                c.wait()
        build(p, weights)
        window = own[:, (2 * p - HB) * TILE : (2 * p + HB + 2) * TILE]
        fitted = jnp.dot(window, weights[...], preferred_element_type=f32).astype(bf16)
        columns = slice(p * 2 * TILE, (p + 1) * 2 * TILE)
        a[:, columns] = fitted[:ROWS]
        b[:, columns] = fitted[ROWS:]
    for n, p in enumerate(EDGE):
        copies[p].wait()
        build(p, edge.at[n])


def fit_edge_kernel(left, right, own, edge, _, __, a, b, ext):
    ext[:, :HALO] = left[...]
    ext[:, HALO : 3 * HALO] = own[:, : 2 * HALO]
    ext[:, 3 * HALO : 5 * HALO] = own[:, AUX - 2 * HALO :]
    ext[:, 5 * HALO :] = right[...]
    for n, p in enumerate(EDGE):
        at = (0, 2, 12, 14)[n] * TILE
        window = ext[:, at : at + (BAND + 1) * TILE]
        fitted = jnp.dot(window, edge[n], preferred_element_type=f32).astype(bf16)
        columns = slice(p * 2 * TILE, (p + 1) * 2 * TILE)
        a[:, columns] = fitted[:ROWS]
        b[:, columns] = fitted[ROWS:]


def fit(index, own, tiles, left, right):
    banded = ((BAND + 1) * TILE, 2 * TILE)
    a, b, own, edge = call(
        fit_inner_kernel,
        [(index, SMEM), (own, ANY), (tiles, ANY)],
        [vmem((ROWS, AUX)), vmem((ROWS, AUX)), vmem((2 * ROWS, AUX)), vmem((4, *banded))],
        [pltpu.VMEM(tiles.shape, bf16), pltpu.VMEM(banded, bf16), DMA((2,)), DMA((10,))],
        name="fit_inner",
        mib=56,
    )
    return call(
        fit_edge_kernel,
        [(v, VMEM) for v in (left, right, own, edge, a, b)],
        [vmem((ROWS, AUX))] * 2,
        [pltpu.VMEM((2 * ROWS, 6 * HALO), bf16)],
        name="fit_edge",
        aliases={4: 0, 5: 1},
    )


def ends_kernel(own, last, first, sems):
    copies = [
        pltpu.make_async_copy(own.at[:, pl.ds(AUX - HALO, HALO)], last, sems.at[0]),
        pltpu.make_async_copy(own.at[:, pl.ds(0, HALO)], first, sems.at[1]),
    ]
    for c in copies:
        c.start()
    for c in copies:
        c.wait()


def ends(own):
    outs = [vmem((2 * ROWS, HALO))] * 2
    return call(ends_kernel, [(own, ANY)], outs, [DMA((2,))], name="ends", mib=60)


def cut(parts, after=(), name=None):
    def kernel(*refs):
        ins, outs, sems = refs[: len(parts)], refs[-1 - len(parts) : -1], refs[-1]
        copies = [
            pltpu.make_async_copy(i.at[pl.ds(r, n)], o, sems.at[j])
            for j, (i, o, (_, r, n)) in enumerate(zip(ins, outs, parts))
        ]
        for c in copies:
            c.start()
        for c in copies:
            c.wait()

    return pl.pallas_call(
        kernel,
        in_specs=[ANY] * (len(parts) + len(after)),
        out_specs=[ANY] * len(parts),
        out_shape=[hbm((n, AUX)) for _, _, n in parts],
        scratch_shapes=[DMA((len(parts),))],
        compiler_params=params(),
        cost_estimate=cost(),
        name=name,
    )(*[p[0] for p in parts], *after)


def arrive(parts, after):
    n = len(parts)
    return pl.pallas_call(
        lambda *refs: None,
        in_specs=[ANY] * (n + len(after)),
        out_specs=[ANY] * n,
        out_shape=[hbm(v.shape, v.dtype) for v in parts],
        input_output_aliases={i: i for i in range(n)},
        compiler_params=params(),
        cost_estimate=cost(),
        name="arrive",
    )(*parts, *after)


def row_copies(moves, out, sems):
    return [
        [
            pltpu.make_async_copy(
                v.at[pl.ds(r, n), pl.ds(h * K2, K2)],
                out.at[pl.ds(at, n), pl.ds(h * K2, K2)],
                sems.at[i, h],
            )
            for i, (v, r, n, at) in enumerate(moves)
        ]
        for h in range(2)
    ]


def b_moves(parts, at=0):
    moves = []
    for p in parts:
        moves.append((p, 0, p.shape[0], at))
        at += p.shape[0]
    return moves


def products(acat, bcat, rows, copies):
    for half in copies:
        for c in half:
            c.start()
    total = None
    for h in range(2):
        for c in copies[h]:
            c.wait()
        columns = slice(h * K2, (h + 1) * K2)
        part = lax.dot_general(
            acat[:, columns], bcat[rows, columns], (((1,), (1,)), ((), ())),
            preferred_element_type=f32,
        )
        total = part if total is None else total + part
    return total


def pair_early_kernel(own, ax, az, ad, *refs):
    b_refs = refs[:7]
    total, bcat, acat, a_sems, b_sems = refs[7:]
    a_moves = [
        (own, 0, ROWS, 0),
        (ax, 0, HALF, 2 * ROWS),
        (ax, HALF, HALF, ROWS),
        (az, 0, HALF, ROWS + HALF),
        (az, HALF, HALF, 2 * ROWS + HALF),
        (ad, 0, ROWS, 3 * ROWS),
    ]
    a_copies = row_copies(a_moves, acat, a_sems)
    b_copies = row_copies(b_moves(b_refs), bcat, b_sems)
    copies = [x + y for x, y in zip(a_copies, b_copies)]
    total[...] = products(acat, bcat, slice(0, 7 * ROWS), copies)


def pair_early(a_parts, b_parts):
    return call(
        pair_early_kernel,
        [(v, ANY) for v in (*a_parts, *b_parts)],
        [vmem((WIDE, 7 * ROWS), f32), vmem((2 * WIDE, AUX)), vmem((WIDE, AUX))],
        [DMA((6, 2)), DMA((7, 2))],
        name="pair_early",
    )


def pair_late_kernel(acat, early, bcat_in, *refs):
    b_refs = refs[:3]
    keep, send, bcat, sems = refs[3:]
    copies = row_copies(b_moves(b_refs, 7 * ROWS), bcat, sems)
    late = products(acat, bcat, slice(7 * ROWS, 8 * ROWS), copies)
    core = position()[1]
    split = 3 * ROWS

    @pl.when(core == 0)
    def _():
        keep[...] = early[:, :WIDE]
        send[:, :split] = early[:, WIDE:].astype(bf16)
        send[:, split:] = late.astype(bf16)

    @pl.when(core == 1)
    def _():
        send[...] = early[:, :WIDE].astype(bf16)
        keep[:, :split] = early[:, WIDE:]
        keep[:, split:] = late


def pair_late(acat, early, bcat, b_parts):
    return call(
        pair_late_kernel,
        [(acat, VMEM), (early, VMEM), (bcat, VMEM)] + [(v, ANY) for v in b_parts],
        [vmem((WIDE, WIDE), f32), hbm((WIDE, WIDE)), vmem((2 * WIDE, AUX))],
        [DMA((3, 2))],
        name="pair_late",
        aliases={2: 2},
    )


def core_sum_kernel(keep, got_in, own, s1, s2, s3, got, sem):
    copy = pltpu.make_async_copy(got_in, got, sem)
    copy.start()
    copy.wait()
    high = position()[0]
    for step, out in enumerate((own, s1, s2, s3)):
        for wave in range(2):
            at = pl.multiple_of((1 - wave) * 2 * ROWS + ((high + step) % 4) * SHARE, SHARE)
            value = keep[pl.ds(at, SHARE)] + got[pl.ds(at, SHARE)].astype(f32)
            out[wave * SHARE : (wave + 1) * SHARE] = value.astype(out.dtype)


def core_sum(keep, got):
    share = (2 * SHARE, WIDE)
    return call(
        core_sum_kernel,
        [(keep, VMEM), (got, ANY)],
        [vmem(share, f32)] + [hbm(share)] * 3,
        [pltpu.VMEM(got.shape, bf16), DMA(())],
        name="core_sum",
    )


BLOCKS = (((0, 0), (3, 0), (1, 0), (0, 1)), ((3, 1), (2, 0), (1, 1), (2, 1)))


def amplitude_kernel(vir, occ, chosen, own, *refs):
    arrived, outs, got, sems = refs[:3], refs[3:5], refs[5], refs[6]
    copies = [
        pltpu.make_async_copy(r, got.at[i], sems.at[i]) for i, r in enumerate(arrived)
    ]
    for c in copies:
        c.start()
    high, core, y, x, z = position()
    occ_total = occ[chosen[0]] + occ[chosen[1]]
    lane = lax.broadcasted_iota(jnp.int32, (SHARE, ROWS), 1)
    row = lax.broadcasted_iota(jnp.int32, (SHARE, ROWS), 0)

    def row_energy(in_x, in_z, second):
        row_x = jnp.where(in_x, x + 1 - 2 * (x % 2), x)
        row_z = jnp.where(in_z, 1 - z, z)
        block = vir[pl.ds((y * 4 + row_x) * 2 + row_z, 1), :]
        own_lane = lane == row + second * SHARE
        return jnp.sum(jnp.where(own_lane, block, 0.0), axis=1, keepdims=True)

    middle = jnp.where((high == 1) | (high == 2), 1, 0)
    rows = (
        row_energy(high != 1, high != 0, high % 2),
        row_energy(high == 2, high == 3, middle),
    )
    places = []
    for first, last in zip(*BLOCKS):
        step = jnp.where(core == 0, first[0], last[0])
        away = jnp.where(core == 0, first[1], last[1])
        places.append((((y + step) % 4) * 4 + jnp.where(away == 1, 3 - x, x)) * 2 + z)
    columns = jnp.concatenate([vir[pl.ds(at, 1), :] for at in places], axis=1)
    for c in copies:
        c.wait()
    for wave, out in enumerate(outs):
        part = slice(wave * SHARE, (wave + 1) * SHARE)
        total = own[part]
        for i in range(3):
            total = total + got[i, part].astype(f32)
        denominator = (rows[wave] + columns) - occ_total
        out[...] = (total / denominator).astype(bf16)


def amplitude(vir, occ, chosen, own, arrived):
    return call(
        amplitude_kernel,
        [(vir, VMEM), (occ, SMEM), (chosen, SMEM), (own, VMEM)]
        + [(v, ANY) for v in arrived],
        [hbm((SHARE, WIDE))] * 2,
        [pltpu.VMEM((3, *own.shape), bf16), DMA((3,))],
        name="amplitude",
    )


def gather_rows(mine, other, tcat, sems):
    high, core = position()[:2]
    copies = []
    for k in range(4):
        rows = pl.ds(pl.multiple_of(((high - k + 4) % 4) * SHARE, SHARE), SHARE)
        for i, (v, of) in enumerate(((mine[k], core), (other[k], 1 - core))):
            columns = pl.ds(pl.multiple_of(of * WIDE, WIDE), WIDE)
            copies.append(pltpu.make_async_copy(v, tcat.at[rows, columns], sems.at[k, i]))
    for c in copies:
        c.start()
    return copies


def product(tcat, bcat, half):
    columns = slice(half * K2, (half + 1) * K2)
    return jnp.dot(tcat[...], bcat[:, columns], preferred_element_type=f32)


TCAT = (2 * ROWS, 2 * WIDE)


def density_first_kernel(*refs):
    mine, other, bcat = refs[:4], refs[4:8], refs[8]
    outs, tcat, sems = refs[-6:-2], refs[-2], refs[-1]
    for c in gather_rows(mine, other, tcat, sems):
        c.wait()
    for half in range(2):
        columns = slice(half * K2, (half + 1) * K2)
        value = product(tcat, bcat, half).astype(bf16)
        for i, out in enumerate(outs):
            out[:, columns] = value[i * HALF : (i + 1) * HALF]


def density_first(mine, other, bcat, after):
    return call(
        density_first_kernel,
        [(v, ANY) for v in (*mine, *other)] + [(bcat, VMEM)] + [(v, ANY) for v in after],
        [hbm((HALF, AUX))] * 4,
        [pltpu.VMEM(TCAT, bf16), DMA((4, 2))],
        name="density_first",
    )


def density_second_kernel(*refs):
    mine, other, (bcat, from_x, from_z) = refs[:4], refs[4:8], refs[8:11]
    x2, z1, own, tcat, got_x, got_z, row_sems, sems = refs[11:]
    rows_copies = gather_rows(mine, other, tcat, row_sems)
    copies = [
        pltpu.make_async_copy(from_x, got_x, sems.at[0]),
        pltpu.make_async_copy(from_z, got_z, sems.at[1]),
    ]
    for c in copies:
        c.start()
    for c in rows_copies:
        c.wait()
    for half in range(2):
        columns = slice(half * K2, (half + 1) * K2)
        value = product(tcat, bcat, half)
        if half == 0:
            for c in copies:
                c.wait()
        x = value[ROWS : ROWS + HALF] + got_z[:, columns].astype(f32)
        z = value[ROWS + HALF :] + got_x[:, columns].astype(f32)
        x2[:, columns] = x.astype(bf16)
        z1[:, columns] = z.astype(bf16)
        own[:, columns] = value[:ROWS]


def density_second(mine, other, bcat, from_x, from_z):
    return call(
        density_second_kernel,
        [(v, ANY) for v in (*mine, *other)]
        + [(bcat, VMEM), (from_x, ANY), (from_z, ANY)],
        [hbm((HALF, AUX))] * 2 + [vmem((ROWS, AUX), f32)],
        [pltpu.VMEM(TCAT, bf16)]
        + [pltpu.VMEM((HALF, AUX), bf16)] * 2
        + [DMA((4, 2)), DMA((2,))],
        name="density_second",
    )


def total_kernel(own, x1, z1, x2, z2, out, got, sems):
    copies = [
        pltpu.make_async_copy(v, got.at[i], sems.at[i]) for i, v in enumerate((x1, z1, x2, z2))
    ]
    for c in copies:
        c.start()
    for h in range(2):
        rows = slice(h * HALF, (h + 1) * HALF)
        for c in copies[2 * h : 2 * h + 2]:
            c.wait()
        value = own[rows] + got[2 * h].astype(f32) + got[2 * h + 1].astype(f32)
        out[rows] = value.astype(bf16)


def total(own, x1, z1, x2, z2):
    return call(
        total_kernel,
        [(own, VMEM)] + [(v, ANY) for v in (x1, z1, x2, z2)],
        [hbm((ROWS, AUX))],
        [pltpu.VMEM((4, HALF, AUX), bf16), DMA((4,))],
        name="total",
    )[0]


def local(integrals, tiles, tile_index, vir_energy, occ_energy, pair_index):
    window = integrals.reshape(2 * ROWS, AUX)
    vir = vir_energy.reshape(-1, ROWS)
    up = [(g, g + 1) for g in range(7)]
    down = [(g + 1, g) for g in range(7)]
    last, first = ends(window)
    left = lax.ppermute(last, "grp", up)
    right = lax.ppermute(first, "grp", down)
    a, b = fit(tile_index.T, window, tiles, left, right)

    with jax.named_scope("first"):
        bm = send_y(b, 1)
        bp = send_y(b, -1)
        bo = send_outer(b)
        ax = send_inner(a)
        az = send_z(a)
    bo, bp, az = arrive((bo, bp, az), (bm, ax, vir))
    with jax.named_scope("second"):
        bom = send_y(bo, 1)
        b2 = send_y(bp, -1)
        bop = send_outer(bp)
        ad = send_inner(az)
    c1, c2, c3 = cut([(b2, 0, 64), (bom, 64, 48), (bop, 112, 48)], name="cut_b")
    with jax.named_scope("third"):
        c1 = send_outer(c1)
        c2 = send_y(c2, 1)
        c3 = send_y(c3, -1)
    early, bcat, acat = pair_early((a, ax, az, ad), (b, bm, bp, bo, bom, b2, bop))
    keep, send, bcat = pair_late(acat, early, bcat, (c1, c2, c3))
    with jax.named_scope("core"):
        own, *s = core_sum(keep, send_core(send))
    with jax.named_scope("shares"):
        arrived = [send_high(v, k + 1) for k, v in enumerate(s)]
    mine = amplitude(vir, occ_energy, pair_index, own, arrived)

    def spread(wave):
        with jax.named_scope(f"spread_{wave}"):
            return [mine[wave]] + [send_high(mine[wave], k) for k in (1, 2, 3)]

    def other_core(wave, mine):
        with jax.named_scope(f"other_{wave}"):
            return [send_core(v) for v in mine]

    mine0, mine1 = spread(0), spread(1)
    other0 = other_core(0, mine0)
    other1 = other_core(1, mine1)
    x1, z2, to_d1, to_d2 = density_first(mine0, other0, bcat, (mine1[1], mine1[3]))
    with jax.named_scope("out"):
        from_x = send_inner(to_d1)
        from_z = send_z(to_d2)
        got_x1 = send_inner(x1)
        got_z2 = send_z(z2)
    x2, z1, own = density_second(mine1, other1, bcat, from_x, from_z)
    with jax.named_scope("out"):
        got_z1 = send_z(z1)
        got_x2 = send_inner(x2)
    return total(own, got_x1, got_z1, got_x2, got_z2)


def solution(mesh):
    in_specs = (P(None, "blk", "grp"), P("grp", None, None), P("grp", None), P(), P(), P())
    return jax.shard_map(
        local, mesh=mesh, in_specs=in_specs, out_specs=P("blk", "grp"), check_vma=False
    )
```

```python
import functools

import jax
import jax.numpy as jnp
from jax import lax
from jax.experimental import pallas as pl
from jax.experimental.pallas import tpu as pltpu
from jax.sharding import PartitionSpec as P

TILE = 128
HB = 4
BAND = 2 * HB + 1
ROWS = 160
AUX = 2560
HALO = HB * TILE
bf16 = jnp.bfloat16
f32 = jnp.float32
MIB = 1 << 20


def blk_index(y, x, z):
    return ((y % 4) * 4 + x % 4) * 2 + z


PLACES = [(y, x, z) for y in range(4) for x in range(4) for z in range(2)]


def send_y(v, step):
    pairs = [(blk_index(y, x, z), blk_index(y + step, x, z)) for y, x, z in PLACES]
    return lax.ppermute(v, "blk", pairs)


def send_x(v, step):
    pairs = [(blk_index(y, x, z), blk_index(y, x + step, z)) for y, x, z in PLACES]
    return lax.ppermute(v, "blk", pairs)


def send_z(v):
    pairs = [(blk_index(y, x, z), blk_index(y, x, 1 - z)) for y, x, z in PLACES]
    return lax.ppermute(v, "blk", pairs)


def send_core(v):
    return lax.ppermute(v, "grp", [(g, g ^ 1) for g in range(8)])


def send_high(v, step):
    return lax.ppermute(v, "grp", [(g, (g + 2 * step) % 8) for g in range(8)])


def params(mib=28):
    return pltpu.CompilerParams(vmem_limit_bytes=mib * MIB)


def cost():
    return pl.CostEstimate(flops=1000, bytes_accessed=1000, transcendentals=0)


def position():
    group = lax.axis_index("grp").astype(jnp.int32)
    me = lax.axis_index("blk").astype(jnp.int32)
    return group // 2, group % 2, me // 8, (me // 2) % 4, me % 2


ANY = pl.BlockSpec(memory_space=pl.ANY)
VMEM = pl.BlockSpec(memory_space=pltpu.VMEM)
SMEM = pl.BlockSpec(memory_space=pltpu.SMEM)
DMA = pltpu.SemaphoreType.DMA
HALF = ROWS // 2
SHARE = ROWS // 2
WIDE = 4 * ROWS
K2 = AUX // 2


def hbm(shape, dtype=bf16):
    return jax.ShapeDtypeStruct(shape, dtype)


def vmem(shape, dtype=bf16):
    return pltpu.VMEM(shape, dtype)


def call(kernel, args, outs, scratch=(), name=None, aliases=None, mib=28):
    return pl.pallas_call(
        kernel,
        in_specs=[spec for _, spec in args],
        out_specs=[VMEM] * len(outs),
        out_shape=list(outs),
        scratch_shapes=list(scratch),
        input_output_aliases=aliases or {},
        compiler_params=params(mib),
        cost_estimate=cost(),
        name=name,
    )(*[a for a, _ in args])


INNER = (2, 3, 4, 5, 6, 7)
EDGE = (0, 1, 8, 9)


def fit_inner_kernel(index, own_in, tiles_in, a, b, own, edge, tiles, weights, own_sem, sems):
    own_copies = [
        pltpu.make_async_copy(
            own_in.at[pl.ds(i * ROWS, ROWS)], own.at[pl.ds(i * ROWS, ROWS)], own_sem.at[i]
        )
        for i in range(2)
    ]
    copies = {}
    for p in INNER + EDGE:
        part = pl.ds(p * 2 * BAND, 2 * BAND)
        copies[p] = pltpu.make_async_copy(tiles_in.at[part], tiles.at[part], sems.at[p])
    copies[INNER[0]].start()
    for c in own_copies:
        c.start()
    for p in (INNER + EDGE)[1:]:
        copies[p].start()
    zero = jnp.zeros((TILE, TILE), bf16)

    def build(p, out):
        out[:TILE, TILE:] = zero
        out[BAND * TILE :, :TILE] = zero
        for q in range(2):
            for o in range(BAND):
                slot = p * 2 * BAND + q * BAND + o
                at = (q + o) * TILE
                out[at : at + TILE, q * TILE : (q + 1) * TILE] = jnp.where(
                    index[1, slot] == 1, tiles[slot], zero
                )

    for p in INNER:
        copies[p].wait()
        if p == INNER[0]:
            for c in own_copies:
                c.wait()
        build(p, weights)
        window = own[:, (2 * p - HB) * TILE : (2 * p + HB + 2) * TILE]
        fitted = jnp.dot(window, weights[...], preferred_element_type=f32).astype(bf16)
        columns = slice(p * 2 * TILE, (p + 1) * 2 * TILE)
        a[:, columns] = fitted[:ROWS]
        b[:, columns] = fitted[ROWS:]
    for n, p in enumerate(EDGE):
        copies[p].wait()
        build(p, edge.at[n])


def fit_edge_kernel(left, right, own, edge, _, __, a, b, ext):
    ext[:, :HALO] = left[...]
    ext[:, HALO : 3 * HALO] = own[:, : 2 * HALO]
    ext[:, 3 * HALO : 5 * HALO] = own[:, AUX - 2 * HALO :]
    ext[:, 5 * HALO :] = right[...]
    for n, p in enumerate(EDGE):
        at = (0, 2, 12, 14)[n] * TILE
        window = ext[:, at : at + (BAND + 1) * TILE]
        fitted = jnp.dot(window, edge[n], preferred_element_type=f32).astype(bf16)
        columns = slice(p * 2 * TILE, (p + 1) * 2 * TILE)
        a[:, columns] = fitted[:ROWS]
        b[:, columns] = fitted[ROWS:]


def fit(index, own, tiles, left, right):
    banded = ((BAND + 1) * TILE, 2 * TILE)
    a, b, own, edge = call(
        fit_inner_kernel,
        [(index, SMEM), (own, ANY), (tiles, ANY)],
        [vmem((ROWS, AUX)), vmem((ROWS, AUX)), vmem((2 * ROWS, AUX)), vmem((4, *banded))],
        [pltpu.VMEM(tiles.shape, bf16), pltpu.VMEM(banded, bf16), DMA((2,)), DMA((10,))],
        name="fit_inner",
        mib=56,
    )
    return call(
        fit_edge_kernel,
        [(v, VMEM) for v in (left, right, own, edge, a, b)],
        [vmem((ROWS, AUX))] * 2,
        [pltpu.VMEM((2 * ROWS, 6 * HALO), bf16)],
        name="fit_edge",
        aliases={4: 0, 5: 1},
    )


def ends_kernel(own, last, first, sems):
    copies = [
        pltpu.make_async_copy(own.at[:, pl.ds(AUX - HALO, HALO)], last, sems.at[0]),
        pltpu.make_async_copy(own.at[:, pl.ds(0, HALO)], first, sems.at[1]),
    ]
    for c in copies:
        c.start()
    for c in copies:
        c.wait()


def ends(own):
    outs = [vmem((2 * ROWS, HALO))] * 2
    return call(ends_kernel, [(own, ANY)], outs, [DMA((2,))], name="ends", mib=60)


def cut(parts, after=(), name=None):
    def kernel(*refs):
        ins, outs, sems = refs[: len(parts)], refs[-1 - len(parts) : -1], refs[-1]
        copies = [
            pltpu.make_async_copy(i.at[pl.ds(r, n)], o, sems.at[j])
            for j, (i, o, (_, r, n)) in enumerate(zip(ins, outs, parts))
        ]
        for c in copies:
            c.start()
        for c in copies:
            c.wait()

    return pl.pallas_call(
        kernel,
        in_specs=[ANY] * (len(parts) + len(after)),
        out_specs=[ANY] * len(parts),
        out_shape=[hbm((n, AUX)) for _, _, n in parts],
        scratch_shapes=[DMA((len(parts),))],
        compiler_params=params(),
        cost_estimate=cost(),
        name=name,
    )(*[p[0] for p in parts], *after)


def arrive(parts, after):
    n = len(parts)
    return pl.pallas_call(
        lambda *refs: None,
        in_specs=[ANY] * (n + len(after)),
        out_specs=[ANY] * n,
        out_shape=[hbm(v.shape, v.dtype) for v in parts],
        input_output_aliases={i: i for i in range(n)},
        compiler_params=params(),
        cost_estimate=cost(),
        name="arrive",
    )(*parts, *after)


def row_copies(moves, out, sems):
    return [
        [
            pltpu.make_async_copy(
                v.at[pl.ds(r, n), pl.ds(h * K2, K2)],
                out.at[pl.ds(at, n), pl.ds(h * K2, K2)],
                sems.at[i, h],
            )
            for i, (v, r, n, at) in enumerate(moves)
        ]
        for h in range(2)
    ]


def b_moves(parts, at=0):
    moves = []
    for p in parts:
        moves.append((p, 0, p.shape[0], at))
        at += p.shape[0]
    return moves


def products(acat, bcat, rows, copies):
    for half in copies:
        for c in half:
            c.start()
    total = None
    for h in range(2):
        for c in copies[h]:
            c.wait()
        columns = slice(h * K2, (h + 1) * K2)
        part = lax.dot_general(
            acat[:, columns], bcat[rows, columns], (((1,), (1,)), ((), ())),
            preferred_element_type=f32,
        )
        total = part if total is None else total + part
    return total


def pair_early_kernel(own, ax, am, ad, *refs):
    b_refs = refs[:7]
    total, bcat, acat, a_sems, b_sems = refs[7:]
    a_moves = [
        (own, 0, ROWS, 0),
        (ax, 0, HALF, ROWS),
        (ax, HALF, HALF, 2 * ROWS),
        (am, 0, HALF, 2 * ROWS + HALF),
        (am, HALF, HALF, ROWS + HALF),
        (ad, 0, ROWS, 3 * ROWS),
    ]
    a_copies = row_copies(a_moves, acat, a_sems)
    b_copies = row_copies(b_moves(b_refs), bcat, b_sems)
    copies = [x + y for x, y in zip(a_copies, b_copies)]
    total[...] = products(acat, bcat, slice(0, 7 * ROWS), copies)


def pair_early(a_parts, b_parts):
    return call(
        pair_early_kernel,
        [(v, ANY) for v in (*a_parts, *b_parts)],
        [vmem((WIDE, 7 * ROWS), f32), vmem((2 * WIDE, AUX)), vmem((WIDE, AUX))],
        [DMA((6, 2)), DMA((7, 2))],
        name="pair_early",
    )


def pair_late_kernel(acat, early, bcat_in, *refs):
    b_refs = refs[:3]
    keep, send, bcat, sems = refs[3:]
    copies = row_copies(b_moves(b_refs, 7 * ROWS), bcat, sems)
    late = products(acat, bcat, slice(7 * ROWS, 8 * ROWS), copies)
    core = position()[1]
    split = 3 * ROWS

    @pl.when(core == 0)
    def _():
        keep[...] = early[:, :WIDE]
        send[:, :split] = early[:, WIDE:].astype(bf16)
        send[:, split:] = late.astype(bf16)

    @pl.when(core == 1)
    def _():
        send[...] = early[:, :WIDE].astype(bf16)
        keep[:, :split] = early[:, WIDE:]
        keep[:, split:] = late


def pair_late(acat, early, bcat, b_parts):
    return call(
        pair_late_kernel,
        [(acat, VMEM), (early, VMEM), (bcat, VMEM)] + [(v, ANY) for v in b_parts],
        [vmem((WIDE, WIDE), f32), hbm((WIDE, WIDE)), vmem((2 * WIDE, AUX))],
        [DMA((3, 2))],
        name="pair_late",
        aliases={2: 2},
    )


def core_sum_kernel(keep, got_in, own, s1, s2, s3, got, sem):
    copy = pltpu.make_async_copy(got_in, got, sem)
    copy.start()
    copy.wait()
    high = position()[0]
    for step, out in enumerate((own, s1, s2, s3)):
        for wave in range(2):
            at = pl.multiple_of((1 - wave) * 2 * ROWS + ((high + step) % 4) * SHARE, SHARE)
            value = keep[pl.ds(at, SHARE)] + got[pl.ds(at, SHARE)].astype(f32)
            out[wave * SHARE : (wave + 1) * SHARE] = value.astype(out.dtype)


def core_sum(keep, got):
    share = (2 * SHARE, WIDE)
    return call(
        core_sum_kernel,
        [(keep, VMEM), (got, ANY)],
        [vmem(share, f32)] + [hbm(share)] * 3,
        [pltpu.VMEM(got.shape, bf16), DMA(())],
        name="core_sum",
    )


BLOCKS = (((0, 0), (3, 0), (1, 0), (0, 1)), ((3, 1), (2, 0), (1, 1), (2, 1)))


def amplitude_kernel(vir, occ, chosen, own, *refs):
    arrived, outs, got, sems = refs[:3], refs[3:5], refs[5], refs[6]
    copies = [
        pltpu.make_async_copy(r, got.at[i], sems.at[i]) for i, r in enumerate(arrived)
    ]
    for c in copies:
        c.start()
    high, core, y, x, z = position()
    occ_total = occ[chosen[0]] + occ[chosen[1]]
    lane = lax.broadcasted_iota(jnp.int32, (SHARE, ROWS), 1)
    row = lax.broadcasted_iota(jnp.int32, (SHARE, ROWS), 0)

    def row_energy(shift, second):
        block = vir[pl.ds((y * 4 + (x + shift) % 4) * 2 + z, 1), :]
        own_lane = lane == row + second * SHARE
        return jnp.sum(jnp.where(own_lane, block, 0.0), axis=1, keepdims=True)

    rows = (
        row_energy(
            jnp.where(high == 0, 1, jnp.where(high == 1, 3, 2)),
            jnp.where((high == 0) | (high == 3), 1, 0),
        ),
        row_energy(jnp.where(high < 2, 0, 2 * high - 3), high % 2),
    )
    places = []
    for first, last in zip(*BLOCKS):
        step = jnp.where(core == 0, first[0], last[0])
        away = jnp.where(core == 0, first[1], last[1])
        places.append((((y + step) % 4) * 4 + x) * 2 + jnp.where(away == 1, 1 - z, z))
    columns = jnp.concatenate([vir[pl.ds(at, 1), :] for at in places], axis=1)
    for c in copies:
        c.wait()
    for wave, out in enumerate(outs):
        part = slice(wave * SHARE, (wave + 1) * SHARE)
        total = own[part]
        for i in range(3):
            total = total + got[i, part].astype(f32)
        denominator = (rows[wave] + columns) - occ_total
        out[...] = (total / denominator).astype(bf16)


def amplitude(vir, occ, chosen, own, arrived):
    return call(
        amplitude_kernel,
        [(vir, VMEM), (occ, SMEM), (chosen, SMEM), (own, VMEM)]
        + [(v, ANY) for v in arrived],
        [hbm((SHARE, WIDE))] * 2,
        [pltpu.VMEM((3, *own.shape), bf16), DMA((3,))],
        name="amplitude",
    )


def gather_rows(mine, other, tcat, sems):
    high, core = position()[:2]
    copies = []
    for k in range(4):
        rows = pl.ds(pl.multiple_of(((high - k + 4) % 4) * SHARE, SHARE), SHARE)
        for i, (v, of) in enumerate(((mine[k], core), (other[k], 1 - core))):
            columns = pl.ds(pl.multiple_of(of * WIDE, WIDE), WIDE)
            copies.append(pltpu.make_async_copy(v, tcat.at[rows, columns], sems.at[k, i]))
    for c in copies:
        c.start()
    return copies


def product(tcat, bcat, half):
    columns = slice(half * K2, (half + 1) * K2)
    return jnp.dot(tcat[...], bcat[:, columns], preferred_element_type=f32)


TCAT = (2 * ROWS, 2 * WIDE)


def density_first_kernel(*refs):
    mine, other, bcat = refs[:4], refs[4:8], refs[8]
    outs, tcat, sems = refs[-6:-2], refs[-2], refs[-1]
    for c in gather_rows(mine, other, tcat, sems):
        c.wait()
    for half in range(2):
        columns = slice(half * K2, (half + 1) * K2)
        value = product(tcat, bcat, half).astype(bf16)
        for i, out in enumerate(outs):
            out[:, columns] = value[i * HALF : (i + 1) * HALF]


def density_first(mine, other, bcat, after):
    return call(
        density_first_kernel,
        [(v, ANY) for v in (*mine, *other)] + [(bcat, VMEM)] + [(v, ANY) for v in after],
        [hbm((HALF, AUX))] * 4,
        [pltpu.VMEM(TCAT, bf16), DMA((4, 2))],
        name="density_first",
    )


def density_second_kernel(*refs):
    mine, other, (bcat, from_m, from_x) = refs[:4], refs[4:8], refs[8:11]
    x1, m2, own, tcat, got_m, got_x, row_sems, sems = refs[11:]
    rows_copies = gather_rows(mine, other, tcat, row_sems)
    copies = [
        pltpu.make_async_copy(from_m, got_m, sems.at[0]),
        pltpu.make_async_copy(from_x, got_x, sems.at[1]),
    ]
    for c in copies:
        c.start()
    for c in rows_copies:
        c.wait()
    for half in range(2):
        columns = slice(half * K2, (half + 1) * K2)
        value = product(tcat, bcat, half)
        if half == 0:
            for c in copies:
                c.wait()
        x = value[ROWS : ROWS + HALF] + got_m[:, columns].astype(f32)
        m = value[ROWS + HALF :] + got_x[:, columns].astype(f32)
        x1[:, columns] = x.astype(bf16)
        m2[:, columns] = m.astype(bf16)
        own[:, columns] = value[:ROWS]


def density_second(mine, other, bcat, from_m, from_x):
    return call(
        density_second_kernel,
        [(v, ANY) for v in (*mine, *other)]
        + [(bcat, VMEM), (from_m, ANY), (from_x, ANY)],
        [hbm((HALF, AUX))] * 2 + [vmem((ROWS, AUX), f32)],
        [pltpu.VMEM(TCAT, bf16)]
        + [pltpu.VMEM((HALF, AUX), bf16)] * 2
        + [DMA((4, 2)), DMA((2,))],
        name="density_second",
    )


def total_kernel(own, x1, m1, x2, m2, out, got, sems):
    copies = [
        pltpu.make_async_copy(v, got.at[i], sems.at[i]) for i, v in enumerate((x1, m1, x2, m2))
    ]
    for c in copies:
        c.start()
    for h in range(2):
        rows = slice(h * HALF, (h + 1) * HALF)
        for c in copies[2 * h : 2 * h + 2]:
            c.wait()
        value = own[rows] + got[2 * h].astype(f32) + got[2 * h + 1].astype(f32)
        out[rows] = value.astype(bf16)


def total(own, x1, m1, x2, m2):
    return call(
        total_kernel,
        [(own, VMEM)] + [(v, ANY) for v in (x1, m1, x2, m2)],
        [hbm((ROWS, AUX))],
        [pltpu.VMEM((4, HALF, AUX), bf16), DMA((4,))],
        name="total",
    )[0]


def local(integrals, tiles, tile_index, vir_energy, occ_energy, pair_index):
    window = integrals.reshape(2 * ROWS, AUX)
    vir = vir_energy.reshape(-1, ROWS)
    up = [(g, g + 1) for g in range(7)]
    down = [(g + 1, g) for g in range(7)]
    last, first = ends(window)
    left = lax.ppermute(last, "grp", up)
    right = lax.ppermute(first, "grp", down)
    a, b = fit(tile_index.T, window, tiles, left, right)

    with jax.named_scope("first"):
        bm = send_y(b, 1)
        bp = send_y(b, -1)
        bo = send_z(b)
        ax = send_x(a, -1)
        am = send_x(a, 1)
    bo, bp, ax = arrive((bo, bp, ax), (bm, am, vir))
    with jax.named_scope("second"):
        bom = send_y(bo, 1)
        b2 = send_y(bp, -1)
        bop = send_z(bp)
        ad = send_x(ax, -1)
    c1, c2, c3 = cut([(b2, 0, 64), (bom, 64, 48), (bop, 112, 48)], name="cut_b")
    with jax.named_scope("third"):
        c1 = send_z(c1)
        c2 = send_y(c2, 1)
        c3 = send_y(c3, -1)
    early, bcat, acat = pair_early((a, ax, am, ad), (b, bm, bp, bo, bom, b2, bop))
    keep, send, bcat = pair_late(acat, early, bcat, (c1, c2, c3))
    with jax.named_scope("core"):
        own, *s = core_sum(keep, send_core(send))
    with jax.named_scope("shares"):
        arrived = [send_high(v, k + 1) for k, v in enumerate(s)]
    mine = amplitude(vir, occ_energy, pair_index, own, arrived)

    def spread(wave):
        with jax.named_scope(f"spread_{wave}"):
            return [mine[wave]] + [send_high(mine[wave], k) for k in (1, 2, 3)]

    def other_core(wave, mine):
        with jax.named_scope(f"other_{wave}"):
            return [send_core(v) for v in mine]

    mine0, mine1 = spread(0), spread(1)
    other0 = other_core(0, mine0)
    other1 = other_core(1, mine1)
    x2, m1, to_d1, to_d2 = density_first(mine0, other0, bcat, (mine1[2],))
    with jax.named_scope("out"):
        from_m = send_x(to_d1, 1)
        from_x = send_x(to_d2, -1)
        got_x2 = send_x(x2, 1)
        got_m1 = send_x(m1, -1)
    x1, m2, own = density_second(mine1, other1, bcat, from_m, from_x)
    with jax.named_scope("out"):
        got_x1 = send_x(x1, 1)
        got_m2 = send_x(m2, -1)
    return total(own, got_x1, got_m1, got_x2, got_m2)


def solution(mesh):
    in_specs = (P(None, "blk", "grp"), P("grp", None, None), P("grp", None), P(), P(), P())
    return jax.shard_map(
        local, mesh=mesh, in_specs=in_specs, out_specs=P("blk", "grp"), check_vma=False
    )
```

```python
import functools

import jax
import jax.numpy as jnp
from jax import lax
from jax.experimental import pallas as pl
from jax.experimental.pallas import tpu as pltpu
from jax.sharding import PartitionSpec as P

TILE = 128
HB = 4
BAND = 2 * HB + 1
ROWS = 160
AUX = 2560
HALO = HB * TILE
bf16 = jnp.bfloat16
f32 = jnp.float32
MIB = 1 << 20


def blk_index(y, x, z):
    return ((y % 4) * 4 + x % 4) * 2 + z


PLACES = [(y, x, z) for y in range(4) for x in range(4) for z in range(2)]


def send_y(v, step):
    pairs = [(blk_index(y, x, z), blk_index(y + step, x, z)) for y, x, z in PLACES]
    return lax.ppermute(v, "blk", pairs)


def send_x(v, step):
    pairs = [(blk_index(y, x, z), blk_index(y, x + step, z)) for y, x, z in PLACES]
    return lax.ppermute(v, "blk", pairs)


def send_z(v):
    pairs = [(blk_index(y, x, z), blk_index(y, x, 1 - z)) for y, x, z in PLACES]
    return lax.ppermute(v, "blk", pairs)


def send_core(v):
    return lax.ppermute(v, "grp", [(g, g ^ 1) for g in range(8)])


def send_high(v, step):
    return lax.ppermute(v, "grp", [(g, (g + 2 * step) % 8) for g in range(8)])


def params(mib=28):
    return pltpu.CompilerParams(vmem_limit_bytes=mib * MIB)


def cost():
    return pl.CostEstimate(flops=1000, bytes_accessed=1000, transcendentals=0)


def position():
    group = lax.axis_index("grp").astype(jnp.int32)
    me = lax.axis_index("blk").astype(jnp.int32)
    return group // 2, group % 2, me // 8, (me // 2) % 4, me % 2


ANY = pl.BlockSpec(memory_space=pl.ANY)
VMEM = pl.BlockSpec(memory_space=pltpu.VMEM)
SMEM = pl.BlockSpec(memory_space=pltpu.SMEM)
DMA = pltpu.SemaphoreType.DMA
HALF = ROWS // 2
SHARE = ROWS // 2
WIDE = 4 * ROWS
K2 = AUX // 2
K4 = AUX // 4


def hbm(shape, dtype=bf16):
    return jax.ShapeDtypeStruct(shape, dtype)


def vmem(shape, dtype=bf16):
    return pltpu.VMEM(shape, dtype)


def call(kernel, args, outs, scratch=(), name=None, aliases=None, mib=28):
    return pl.pallas_call(
        kernel,
        in_specs=[spec for _, spec in args],
        out_specs=[VMEM] * len(outs),
        out_shape=list(outs),
        scratch_shapes=list(scratch),
        input_output_aliases=aliases or {},
        compiler_params=params(mib),
        cost_estimate=cost(),
        name=name,
    )(*[a for a, _ in args])


INNER = (2, 3, 4, 5, 6, 7)
EDGE = (0, 1, 8, 9)


def fit_inner_kernel(index, own_in, tiles_in, a, b, own, edge, tiles, weights, own_sem, sems):
    own_copies = [
        pltpu.make_async_copy(
            own_in.at[pl.ds(i * ROWS, ROWS)], own.at[pl.ds(i * ROWS, ROWS)], own_sem.at[i]
        )
        for i in range(2)
    ]
    copies = {}
    for p in INNER + EDGE:
        part = pl.ds(p * 2 * BAND, 2 * BAND)
        copies[p] = pltpu.make_async_copy(tiles_in.at[part], tiles.at[part], sems.at[p])
    copies[INNER[0]].start()
    for c in own_copies:
        c.start()
    for p in (INNER + EDGE)[1:]:
        copies[p].start()
    zero = jnp.zeros((TILE, TILE), bf16)

    def build(p, out):
        out[:TILE, TILE:] = zero
        out[BAND * TILE :, :TILE] = zero
        for q in range(2):
            for o in range(BAND):
                slot = p * 2 * BAND + q * BAND + o
                at = (q + o) * TILE
                out[at : at + TILE, q * TILE : (q + 1) * TILE] = jnp.where(
                    index[1, slot] == 1, tiles[slot], zero
                )

    for p in INNER:
        copies[p].wait()
        if p == INNER[0]:
            for c in own_copies:
                c.wait()
        build(p, weights)
        window = own[:, (2 * p - HB) * TILE : (2 * p + HB + 2) * TILE]
        fitted = jnp.dot(window, weights[...], preferred_element_type=f32).astype(bf16)
        columns = slice(p * 2 * TILE, (p + 1) * 2 * TILE)
        a[:, columns] = fitted[:ROWS]
        b[:, columns] = fitted[ROWS:]
    for n, p in enumerate(EDGE):
        copies[p].wait()
        build(p, edge.at[n])


def fit_edge_kernel(left, right, own, edge, _, __, a, b, ext):
    ext[:, :HALO] = left[...]
    ext[:, HALO : 3 * HALO] = own[:, : 2 * HALO]
    ext[:, 3 * HALO : 5 * HALO] = own[:, AUX - 2 * HALO :]
    ext[:, 5 * HALO :] = right[...]
    for n, p in enumerate(EDGE):
        at = (0, 2, 12, 14)[n] * TILE
        window = ext[:, at : at + (BAND + 1) * TILE]
        fitted = jnp.dot(window, edge[n], preferred_element_type=f32).astype(bf16)
        columns = slice(p * 2 * TILE, (p + 1) * 2 * TILE)
        a[:, columns] = fitted[:ROWS]
        b[:, columns] = fitted[ROWS:]


def fit(index, own, tiles, left, right):
    banded = ((BAND + 1) * TILE, 2 * TILE)
    a, b, own, edge = call(
        fit_inner_kernel,
        [(index, SMEM), (own, ANY), (tiles, ANY)],
        [vmem((ROWS, AUX)), vmem((ROWS, AUX)), vmem((2 * ROWS, AUX)), vmem((4, *banded))],
        [pltpu.VMEM(tiles.shape, bf16), pltpu.VMEM(banded, bf16), DMA((2,)), DMA((10,))],
        name="fit_inner",
        mib=56,
    )
    return call(
        fit_edge_kernel,
        [(v, VMEM) for v in (left, right, own, edge, a, b)],
        [vmem((ROWS, AUX))] * 2,
        [pltpu.VMEM((2 * ROWS, 6 * HALO), bf16)],
        name="fit_edge",
        aliases={4: 0, 5: 1},
    )


def ends_kernel(own, last, first, sems):
    copies = [
        pltpu.make_async_copy(own.at[:, pl.ds(AUX - HALO, HALO)], last, sems.at[0]),
        pltpu.make_async_copy(own.at[:, pl.ds(0, HALO)], first, sems.at[1]),
    ]
    for c in copies:
        c.start()
    for c in copies:
        c.wait()


def ends(own):
    outs = [vmem((2 * ROWS, HALO))] * 2
    return call(ends_kernel, [(own, ANY)], outs, [DMA((2,))], name="ends", mib=60)


def cut(parts, after=(), name=None):
    def kernel(*refs):
        ins, outs, sems = refs[: len(parts)], refs[-1 - len(parts) : -1], refs[-1]
        copies = [
            pltpu.make_async_copy(i.at[pl.ds(r, n)], o, sems.at[j])
            for j, (i, o, (_, r, n)) in enumerate(zip(ins, outs, parts))
        ]
        for c in copies:
            c.start()
        for c in copies:
            c.wait()

    return pl.pallas_call(
        kernel,
        in_specs=[ANY] * (len(parts) + len(after)),
        out_specs=[ANY] * len(parts),
        out_shape=[hbm((n, AUX)) for _, _, n in parts],
        scratch_shapes=[DMA((len(parts),))],
        compiler_params=params(),
        cost_estimate=cost(),
        name=name,
    )(*[p[0] for p in parts], *after)


def arrive(parts, after):
    n = len(parts)
    return pl.pallas_call(
        lambda *refs: None,
        in_specs=[ANY] * (n + len(after)),
        out_specs=[ANY] * n,
        out_shape=[hbm(v.shape, v.dtype) for v in parts],
        input_output_aliases={i: i for i in range(n)},
        compiler_params=params(),
        cost_estimate=cost(),
        name="arrive",
    )(*parts, *after)


def row_copies(moves, out, sems, part):
    columns = pl.ds(pl.multiple_of(part * K4, K4), K4)
    return [
        pltpu.make_async_copy(
            v.at[pl.ds(r, n), columns], out.at[pl.ds(at, n), columns], sems.at[i, part]
        )
        for i, (v, r, n, at) in enumerate(moves)
    ]


def b_moves(parts, at=0):
    moves = []
    for p in parts:
        moves.append((p, 0, p.shape[0], at))
        at += p.shape[0]
    return moves


def products(copies, acat, bcat, wanted):
    for part in range(4):
        for c in copies(part):
            c.start()

    @pl.loop(0, 4)
    def _(part):
        for c in copies(part):
            c.wait()
        columns = pl.ds(pl.multiple_of(part * K4, K4), K4)
        for a_rows, b_rows, total in wanted:
            value = lax.dot_general(
                acat[a_rows, columns], bcat[b_rows, columns], (((1,), (1,)), ((), ())),
                preferred_element_type=f32,
            )

            @pl.when(part == 0)
            def _():
                total[...] = value

            @pl.when(part > 0)
            def _():
                total[...] += value


def pair_first_kernel(own, ax, am, *refs):
    b_refs = refs[:4]
    total, bcat, acat, a_sems, b_sems = refs[4:]
    a_moves = [
        (own, 0, ROWS, 0),
        (ax, 0, HALF, ROWS),
        (ax, HALF, HALF, 2 * ROWS),
        (am, 0, HALF, 2 * ROWS + HALF),
        (am, HALF, HALF, ROWS + HALF),
    ]
    rows = slice(0, 3 * ROWS)
    products(
        lambda part: row_copies(a_moves, acat, a_sems, part)
        + row_copies(b_moves(b_refs), bcat, b_sems, part),
        acat, bcat, [(rows, slice(0, WIDE), total.at[rows])],
    )


def pair_first(a_parts, b_parts):
    return call(
        pair_first_kernel,
        [(v, ANY) for v in (*a_parts, *b_parts)],
        [vmem((WIDE, WIDE), f32), vmem((2 * WIDE, AUX)), vmem((WIDE, AUX))],
        [DMA((5, 4)), DMA((4, 4))],
        name="pair_first",
    )


def pair_early_kernel(first_in, bcat_in, acat_in, ad, *refs):
    b_refs = refs[:3]
    first, bcat, acat, early, a_sems, b_sems = refs[3:]
    rows = slice(3 * ROWS, WIDE)
    products(
        lambda part: row_copies([(ad, 0, ROWS, 3 * ROWS)], acat, a_sems, part)
        + row_copies(b_moves(b_refs, WIDE), bcat, b_sems, part),
        acat, bcat,
        [
            (rows, slice(0, WIDE), first.at[rows]),
            (slice(0, WIDE), slice(WIDE, 7 * ROWS), early),
        ],
    )


def pair_early(first, bcat, acat, ad, b_parts):
    return call(
        pair_early_kernel,
        [(v, VMEM) for v in (first, bcat, acat)] + [(v, ANY) for v in (ad, *b_parts)],
        [
            vmem((WIDE, WIDE), f32),
            vmem((2 * WIDE, AUX)),
            vmem((WIDE, AUX)),
            vmem((WIDE, 3 * ROWS), f32),
        ],
        [DMA((1, 4)), DMA((3, 4))],
        name="pair_early",
        aliases={0: 0, 1: 1, 2: 2},
    )


def pair_late_kernel(first, early, acat, bcat_in, *refs):
    b_refs = refs[:3]
    keep, send, bcat, late, sems = refs[3:]
    products(
        lambda part: row_copies(b_moves(b_refs, 7 * ROWS), bcat, sems, part),
        acat, bcat, [(slice(0, WIDE), slice(7 * ROWS, 8 * ROWS), late)],
    )
    core = position()[1]
    split = 3 * ROWS

    @pl.when(core == 0)
    def _():
        keep[...] = first[...]
        send[:, :split] = early[...].astype(bf16)
        send[:, split:] = late[...].astype(bf16)

    @pl.when(core == 1)
    def _():
        send[...] = first[...].astype(bf16)
        keep[:, :split] = early[...]
        keep[:, split:] = late[...]


def pair_late(first, early, acat, bcat, b_parts):
    return call(
        pair_late_kernel,
        [(v, VMEM) for v in (first, early, acat, bcat)] + [(v, ANY) for v in b_parts],
        [vmem((WIDE, WIDE), f32), hbm((WIDE, WIDE)), vmem((2 * WIDE, AUX))],
        [pltpu.VMEM((WIDE, ROWS), f32), DMA((3, 4))],
        name="pair_late",
        aliases={3: 2},
    )


def core_sum_kernel(keep, got_in, own, s1, s2, s3, got, sem):
    copy = pltpu.make_async_copy(got_in, got, sem)
    copy.start()
    copy.wait()
    high = position()[0]
    for step, out in enumerate((own, s1, s2, s3)):
        for wave in range(2):
            at = pl.multiple_of((1 - wave) * 2 * ROWS + ((high + step) % 4) * SHARE, SHARE)
            value = keep[pl.ds(at, SHARE)] + got[pl.ds(at, SHARE)].astype(f32)
            out[wave * SHARE : (wave + 1) * SHARE] = value.astype(out.dtype)


def core_sum(keep, got):
    share = (2 * SHARE, WIDE)
    return call(
        core_sum_kernel,
        [(keep, VMEM), (got, ANY)],
        [vmem(share, f32)] + [hbm(share)] * 3,
        [pltpu.VMEM(got.shape, bf16), DMA(())],
        name="core_sum",
    )


BLOCKS = (((0, 0), (3, 0), (1, 0), (0, 1)), ((3, 1), (2, 0), (1, 1), (2, 1)))


def amplitude_kernel(vir, occ, chosen, own, *refs):
    arrived, outs, got, sems = refs[:3], refs[3:5], refs[5], refs[6]
    copies = [
        pltpu.make_async_copy(r, got.at[i], sems.at[i]) for i, r in enumerate(arrived)
    ]
    for c in copies:
        c.start()
    high, core, y, x, z = position()
    occ_total = occ[chosen[0]] + occ[chosen[1]]
    lane = lax.broadcasted_iota(jnp.int32, (SHARE, ROWS), 1)
    row = lax.broadcasted_iota(jnp.int32, (SHARE, ROWS), 0)

    def row_energy(shift, second):
        block = vir[pl.ds((y * 4 + (x + shift) % 4) * 2 + z, 1), :]
        own_lane = lane == row + second * SHARE
        return jnp.sum(jnp.where(own_lane, block, 0.0), axis=1, keepdims=True)

    rows = (
        row_energy(
            jnp.where(high == 0, 1, jnp.where(high == 1, 3, 2)),
            jnp.where((high == 0) | (high == 3), 1, 0),
        ),
        row_energy(jnp.where(high < 2, 0, 2 * high - 3), high % 2),
    )
    places = []
    for first, last in zip(*BLOCKS):
        step = jnp.where(core == 0, first[0], last[0])
        away = jnp.where(core == 0, first[1], last[1])
        places.append((((y + step) % 4) * 4 + x) * 2 + jnp.where(away == 1, 1 - z, z))
    columns = jnp.concatenate([vir[pl.ds(at, 1), :] for at in places], axis=1)
    for c in copies:
        c.wait()
    for wave, out in enumerate(outs):
        part = slice(wave * SHARE, (wave + 1) * SHARE)
        total = own[part]
        for i in range(3):
            total = total + got[i, part].astype(f32)
        denominator = (rows[wave] + columns) - occ_total
        out[...] = (total / denominator).astype(bf16)


def amplitude(vir, occ, chosen, own, arrived):
    return call(
        amplitude_kernel,
        [(vir, VMEM), (occ, SMEM), (chosen, SMEM), (own, VMEM)]
        + [(v, ANY) for v in arrived],
        [hbm((SHARE, WIDE))] * 2,
        [pltpu.VMEM((3, *own.shape), bf16), DMA((3,))],
        name="amplitude",
    )


def gather_rows(mine, other, tcat, sems):
    high, core = position()[:2]
    copies = []
    for k in range(4):
        rows = pl.ds(pl.multiple_of(((high - k + 4) % 4) * SHARE, SHARE), SHARE)
        for i, (v, of) in enumerate(((mine[k], core), (other[k], 1 - core))):
            columns = pl.ds(pl.multiple_of(of * WIDE, WIDE), WIDE)
            copies.append(pltpu.make_async_copy(v, tcat.at[rows, columns], sems.at[k, i]))
    for c in copies:
        c.start()
    return copies


def product(tcat, bcat, half):
    columns = pl.ds(pl.multiple_of(half * K2, K2), K2)
    return columns, jnp.dot(tcat[...], bcat[:, columns], preferred_element_type=f32)


TCAT = (2 * ROWS, 2 * WIDE)


def density_first_kernel(*refs):
    mine, other, bcat = refs[:4], refs[4:8], refs[8]
    outs, tcat, sems = refs[-6:-2], refs[-2], refs[-1]
    for c in gather_rows(mine, other, tcat, sems):
        c.wait()

    @pl.loop(0, 2)
    def _(half):
        columns, value = product(tcat, bcat, half)
        for i, out in enumerate(outs):
            out[:, columns] = value[i * HALF : (i + 1) * HALF].astype(bf16)


def density_first(mine, other, bcat, after):
    return call(
        density_first_kernel,
        [(v, ANY) for v in (*mine, *other)] + [(bcat, VMEM)] + [(v, ANY) for v in after],
        [hbm((HALF, AUX))] * 4,
        [pltpu.VMEM(TCAT, bf16), DMA((4, 2))],
        name="density_first",
    )


def density_second_kernel(*refs):
    mine, other, (bcat, from_m, from_x) = refs[:4], refs[4:8], refs[8:11]
    x1, m2, own, tcat, got_m, got_x, row_sems, sems = refs[11:]
    rows_copies = gather_rows(mine, other, tcat, row_sems)
    copies = [
        pltpu.make_async_copy(from_m, got_m, sems.at[0]),
        pltpu.make_async_copy(from_x, got_x, sems.at[1]),
    ]
    for c in copies:
        c.start()
    for c in rows_copies + copies:
        c.wait()

    @pl.loop(0, 2)
    def _(half):
        columns, value = product(tcat, bcat, half)
        x = value[ROWS : ROWS + HALF] + got_m[:, columns].astype(f32)
        m = value[ROWS + HALF :] + got_x[:, columns].astype(f32)
        x1[:, columns] = x.astype(bf16)
        m2[:, columns] = m.astype(bf16)
        own[:, columns] = value[:ROWS]


def density_second(mine, other, bcat, from_m, from_x):
    return call(
        density_second_kernel,
        [(v, ANY) for v in (*mine, *other)]
        + [(bcat, VMEM), (from_m, ANY), (from_x, ANY)],
        [hbm((HALF, AUX))] * 2 + [vmem((ROWS, AUX), f32)],
        [pltpu.VMEM(TCAT, bf16)]
        + [pltpu.VMEM((HALF, AUX), bf16)] * 2
        + [DMA((4, 2)), DMA((2,))],
        name="density_second",
    )


def add_kernel(own, one, two, out, got, sems):
    copies = [
        pltpu.make_async_copy(v, got.at[pl.ds(i * HALF, HALF)], sems.at[i])
        for i, v in enumerate((one, two))
    ]
    for c in copies:
        c.start()
    for c in copies:
        c.wait()
    out[...] = (own[...] + got[...].astype(f32)).astype(out.dtype)


def add(own, one, two, out):
    return call(
        add_kernel,
        [(own, VMEM), (one, ANY), (two, ANY)],
        [out],
        [pltpu.VMEM((ROWS, AUX), bf16), DMA((2,))],
        name="add",
    )[0]


def local(integrals, tiles, tile_index, vir_energy, occ_energy, pair_index):
    window = integrals.reshape(2 * ROWS, AUX)
    vir = vir_energy.reshape(-1, ROWS)
    up = [(g, g + 1) for g in range(7)]
    down = [(g + 1, g) for g in range(7)]
    last, first = ends(window)
    left = lax.ppermute(last, "grp", up)
    right = lax.ppermute(first, "grp", down)
    a, b = fit(tile_index.T, window, tiles, left, right)

    with jax.named_scope("first"):
        bm = send_y(b, 1)
        bp = send_y(b, -1)
        bo = send_z(b)
        ax = send_x(a, -1)
        am = send_x(a, 1)
    bo, bp, ax = arrive((bo, bp, ax), (bm, am, vir))
    with jax.named_scope("second"):
        bom = send_y(bo, 1)
        b2 = send_y(bp, -1)
        bop = send_z(bp)
        ad = send_x(ax, -1)
    early_sums, bcat, acat = pair_first((a, ax, am), (b, bm, bp, bo))
    c1, c2, c3 = cut([(b2, 0, 64), (bom, 64, 48), (bop, 112, 48)], (early_sums,), name="cut_b")
    with jax.named_scope("third"):
        c1 = send_z(c1)
        c2 = send_y(c2, 1)
        c3 = send_y(c3, -1)
    early_sums, bcat, acat, early = pair_early(early_sums, bcat, acat, ad, (bom, b2, bop))
    keep, send, bcat = pair_late(early_sums, early, acat, bcat, (c1, c2, c3))
    with jax.named_scope("core"):
        own, *s = core_sum(keep, send_core(send))
    with jax.named_scope("shares"):
        arrived = [send_high(v, k + 1) for k, v in enumerate(s)]
    mine = amplitude(vir, occ_energy, pair_index, own, arrived)

    def spread(wave):
        with jax.named_scope(f"spread_{wave}"):
            return [mine[wave]] + [send_high(mine[wave], k) for k in (1, 2, 3)]

    def other_core(wave, mine):
        with jax.named_scope(f"other_{wave}"):
            return [send_core(v) for v in mine]

    mine0, mine1 = spread(0), spread(1)
    other0 = other_core(0, mine0)
    other1 = other_core(1, mine1)
    x2, m1, to_d1, to_d2 = density_first(mine0, other0, bcat, (mine1[2],))
    with jax.named_scope("out"):
        from_m = send_x(to_d1, 1)
        from_x = send_x(to_d2, -1)
        got_x2 = send_x(x2, 1)
        got_m1 = send_x(m1, -1)
    x1, m2, own = density_second(mine1, other1, bcat, from_m, from_x)
    with jax.named_scope("out"):
        got_x1 = send_x(x1, 1)
        got_m2 = send_x(m2, -1)
    own = add(own, got_m1, got_x2, vmem((ROWS, AUX), f32))
    return add(own, got_x1, got_m2, hbm((ROWS, AUX)))


def solution(mesh):
    in_specs = (P(None, "blk", "grp"), P("grp", None, None), P("grp", None), P(), P(), P())
    return jax.shard_map(
        local, mesh=mesh, in_specs=in_specs, out_specs=P("blk", "grp"), check_vma=False
    )
```

```python
import functools

import jax
import jax.numpy as jnp
from jax import lax
from jax.experimental import pallas as pl
from jax.experimental.pallas import tpu as pltpu
from jax.sharding import PartitionSpec as P

TILE = 128
HB = 4
BAND = 2 * HB + 1
ROWS = 160
AUX = 2560
HALO = HB * TILE
bf16 = jnp.bfloat16
f32 = jnp.float32
MIB = 1 << 20


def blk_index(y, x, z):
    return ((y % 4) * 4 + x % 4) * 2 + z


PLACES = [(y, x, z) for y in range(4) for x in range(4) for z in range(2)]


def send_y(v, step):
    pairs = [(blk_index(y, x, z), blk_index(y + step, x, z)) for y, x, z in PLACES]
    return lax.ppermute(v, "blk", pairs)


def send_x(v, step):
    pairs = [(blk_index(y, x, z), blk_index(y, x + step, z)) for y, x, z in PLACES]
    return lax.ppermute(v, "blk", pairs)


def send_z(v):
    pairs = [(blk_index(y, x, z), blk_index(y, x, 1 - z)) for y, x, z in PLACES]
    return lax.ppermute(v, "blk", pairs)


def send_core(v):
    return lax.ppermute(v, "grp", [(g, g ^ 1) for g in range(8)])


def send_high(v, step):
    return lax.ppermute(v, "grp", [(g, (g + 2 * step) % 8) for g in range(8)])


def params(mib=28):
    return pltpu.CompilerParams(vmem_limit_bytes=mib * MIB)


def cost():
    return pl.CostEstimate(flops=1000, bytes_accessed=1000, transcendentals=0)


def position():
    group = lax.axis_index("grp").astype(jnp.int32)
    me = lax.axis_index("blk").astype(jnp.int32)
    return group // 2, group % 2, me // 8, (me // 2) % 4, me % 2


ANY = pl.BlockSpec(memory_space=pl.ANY)
VMEM = pl.BlockSpec(memory_space=pltpu.VMEM)
SMEM = pl.BlockSpec(memory_space=pltpu.SMEM)
DMA = pltpu.SemaphoreType.DMA
HALF = ROWS // 2
SHARE = ROWS // 2
WIDE = 4 * ROWS
K2 = AUX // 2
K4 = AUX // 4


def hbm(shape, dtype=bf16):
    return jax.ShapeDtypeStruct(shape, dtype)


def vmem(shape, dtype=bf16):
    return pltpu.VMEM(shape, dtype)


def call(kernel, args, outs, scratch=(), name=None, aliases=None, mib=28):
    return pl.pallas_call(
        kernel,
        in_specs=[spec for _, spec in args],
        out_specs=[VMEM] * len(outs),
        out_shape=list(outs),
        scratch_shapes=list(scratch),
        input_output_aliases=aliases or {},
        compiler_params=params(mib),
        cost_estimate=cost(),
        name=name,
    )(*[a for a, _ in args])


INNER = (2, 3, 4, 5, 6, 7)
EDGE = (0, 1, 8, 9)


def fit_inner_kernel(index, own_in, tiles_in, a, b, own, edge, tiles, weights, own_sem, sems):
    own_copies = [
        pltpu.make_async_copy(
            own_in.at[pl.ds(i * ROWS, ROWS)], own.at[pl.ds(i * ROWS, ROWS)], own_sem.at[i]
        )
        for i in range(2)
    ]
    copies = {}
    for p in INNER + EDGE:
        part = pl.ds(p * 2 * BAND, 2 * BAND)
        copies[p] = pltpu.make_async_copy(tiles_in.at[part], tiles.at[part], sems.at[p])
    copies[INNER[0]].start()
    for c in own_copies:
        c.start()
    for p in (INNER + EDGE)[1:]:
        copies[p].start()
    zero = jnp.zeros((TILE, TILE), bf16)

    def build(p, out):
        out[:TILE, TILE:] = zero
        out[BAND * TILE :, :TILE] = zero
        for q in range(2):
            for o in range(BAND):
                slot = p * 2 * BAND + q * BAND + o
                at = (q + o) * TILE
                out[at : at + TILE, q * TILE : (q + 1) * TILE] = jnp.where(
                    index[1, slot] == 1, tiles[slot], zero
                )

    for p in INNER:
        copies[p].wait()
        if p == INNER[0]:
            for c in own_copies:
                c.wait()
        build(p, weights)
        window = own[:, (2 * p - HB) * TILE : (2 * p + HB + 2) * TILE]
        fitted = jnp.dot(window, weights[...], preferred_element_type=f32).astype(bf16)
        columns = slice(p * 2 * TILE, (p + 1) * 2 * TILE)
        a[:, columns] = fitted[:ROWS]
        b[:, columns] = fitted[ROWS:]
    for n, p in enumerate(EDGE):
        copies[p].wait()
        build(p, edge.at[n])


def fit_edge_kernel(left, right, own, edge, _, __, a, b, ext):
    ext[:, :HALO] = left[...]
    ext[:, HALO : 3 * HALO] = own[:, : 2 * HALO]
    ext[:, 3 * HALO : 5 * HALO] = own[:, AUX - 2 * HALO :]
    ext[:, 5 * HALO :] = right[...]
    for n, p in enumerate(EDGE):
        at = (0, 2, 12, 14)[n] * TILE
        window = ext[:, at : at + (BAND + 1) * TILE]
        fitted = jnp.dot(window, edge[n], preferred_element_type=f32).astype(bf16)
        columns = slice(p * 2 * TILE, (p + 1) * 2 * TILE)
        a[:, columns] = fitted[:ROWS]
        b[:, columns] = fitted[ROWS:]


def fit(index, own, tiles, left, right):
    banded = ((BAND + 1) * TILE, 2 * TILE)
    a, b, own, edge = call(
        fit_inner_kernel,
        [(index, SMEM), (own, ANY), (tiles, ANY)],
        [vmem((ROWS, AUX)), vmem((ROWS, AUX)), vmem((2 * ROWS, AUX)), vmem((4, *banded))],
        [pltpu.VMEM(tiles.shape, bf16), pltpu.VMEM(banded, bf16), DMA((2,)), DMA((10,))],
        name="fit_inner",
        mib=56,
    )
    return call(
        fit_edge_kernel,
        [(v, VMEM) for v in (left, right, own, edge, a, b)],
        [vmem((ROWS, AUX))] * 2,
        [pltpu.VMEM((2 * ROWS, 6 * HALO), bf16)],
        name="fit_edge",
        aliases={4: 0, 5: 1},
    )


def ends_kernel(own, last, first, sems):
    copies = [
        pltpu.make_async_copy(own.at[:, pl.ds(AUX - HALO, HALO)], last, sems.at[0]),
        pltpu.make_async_copy(own.at[:, pl.ds(0, HALO)], first, sems.at[1]),
    ]
    for c in copies:
        c.start()
    for c in copies:
        c.wait()


def ends(own):
    outs = [vmem((2 * ROWS, HALO))] * 2
    return call(ends_kernel, [(own, ANY)], outs, [DMA((2,))], name="ends", mib=60)


def cut(parts, after=(), name=None):
    def kernel(*refs):
        ins, outs, sems = refs[: len(parts)], refs[-1 - len(parts) : -1], refs[-1]
        copies = [
            pltpu.make_async_copy(i.at[pl.ds(r, n)], o, sems.at[j])
            for j, (i, o, (_, r, n)) in enumerate(zip(ins, outs, parts))
        ]
        for c in copies:
            c.start()
        for c in copies:
            c.wait()

    return pl.pallas_call(
        kernel,
        in_specs=[ANY] * (len(parts) + len(after)),
        out_specs=[ANY] * len(parts),
        out_shape=[hbm((n, AUX)) for _, _, n in parts],
        scratch_shapes=[DMA((len(parts),))],
        compiler_params=params(),
        cost_estimate=cost(),
        name=name,
    )(*[p[0] for p in parts], *after)


def arrive(parts, after):
    n = len(parts)
    return pl.pallas_call(
        lambda *refs: None,
        in_specs=[ANY] * (n + len(after)),
        out_specs=[ANY] * n,
        out_shape=[hbm(v.shape, v.dtype) for v in parts],
        input_output_aliases={i: i for i in range(n)},
        compiler_params=params(),
        cost_estimate=cost(),
        name="arrive",
    )(*parts, *after)


def row_copies(moves, out, sems, part):
    columns = pl.ds(pl.multiple_of(part * K4, K4), K4)
    return [
        pltpu.make_async_copy(
            v.at[pl.ds(r, n), columns], out.at[pl.ds(at, n), columns], sems.at[i, part]
        )
        for i, (v, r, n, at) in enumerate(moves)
    ]


def b_moves(parts, at=0):
    moves = []
    for p in parts:
        moves.append((p, 0, p.shape[0], at))
        at += p.shape[0]
    return moves


def products(copies, acat, bcat, wanted):
    for part in range(4):
        for c in copies(part):
            c.start()

    @pl.loop(0, 4)
    def _(part):
        for c in copies(part):
            c.wait()
        columns = pl.ds(pl.multiple_of(part * K4, K4), K4)
        for a_rows, b_rows, total in wanted:
            value = lax.dot_general(
                acat[a_rows, columns], bcat[b_rows, columns], (((1,), (1,)), ((), ())),
                preferred_element_type=f32,
            )

            @pl.when(part == 0)
            def _():
                total[...] = value

            @pl.when(part > 0)
            def _():
                total[...] += value


def pair_first_kernel(own, ax, am, *refs):
    b_refs = refs[:4]
    total, bcat, acat, a_sems, b_sems = refs[4:]
    a_moves = [
        (own, 0, ROWS, 0),
        (ax, 0, HALF, ROWS),
        (ax, HALF, HALF, 2 * ROWS),
        (am, 0, HALF, 2 * ROWS + HALF),
        (am, HALF, HALF, ROWS + HALF),
    ]
    rows = slice(0, 3 * ROWS)
    products(
        lambda part: row_copies(a_moves, acat, a_sems, part)
        + row_copies(b_moves(b_refs), bcat, b_sems, part),
        acat, bcat, [(rows, slice(0, WIDE), total.at[rows])],
    )


def pair_first(a_parts, b_parts):
    return call(
        pair_first_kernel,
        [(v, ANY) for v in (*a_parts, *b_parts)],
        [vmem((WIDE, WIDE), f32), vmem((2 * WIDE, AUX)), vmem((WIDE, AUX))],
        [DMA((5, 4)), DMA((4, 4))],
        name="pair_first",
    )


def pair_early_kernel(first_in, bcat_in, acat_in, ad, *refs):
    b_refs = refs[:3]
    first, bcat, acat, early, a_sems, b_sems = refs[3:]
    rows = slice(3 * ROWS, WIDE)
    products(
        lambda part: row_copies([(ad, 0, ROWS, 3 * ROWS)], acat, a_sems, part)
        + row_copies(b_moves(b_refs, WIDE), bcat, b_sems, part),
        acat, bcat,
        [
            (rows, slice(0, WIDE), first.at[rows]),
            (slice(0, WIDE), slice(WIDE, 7 * ROWS), early),
        ],
    )


def pair_early(first, bcat, acat, ad, b_parts):
    return call(
        pair_early_kernel,
        [(v, VMEM) for v in (first, bcat, acat)] + [(v, ANY) for v in (ad, *b_parts)],
        [
            vmem((WIDE, WIDE), f32),
            vmem((2 * WIDE, AUX)),
            vmem((WIDE, AUX)),
            vmem((WIDE, 3 * ROWS), f32),
        ],
        [DMA((1, 4)), DMA((3, 4))],
        name="pair_early",
        aliases={0: 0, 1: 1, 2: 2},
    )


def pair_late_kernel(first, early, acat, bcat_in, *refs):
    b_refs = refs[:3]
    keep, send, bcat, late, sems = refs[3:]
    products(
        lambda part: row_copies(b_moves(b_refs, 7 * ROWS), bcat, sems, part),
        acat, bcat, [(slice(0, WIDE), slice(7 * ROWS, 8 * ROWS), late)],
    )
    core = position()[1]
    split = 3 * ROWS

    @pl.when(core == 0)
    def _():
        keep[...] = first[...]
        send[:, :split] = early[...].astype(bf16)
        send[:, split:] = late[...].astype(bf16)

    @pl.when(core == 1)
    def _():
        send[...] = first[...].astype(bf16)
        keep[:, :split] = early[...]
        keep[:, split:] = late[...]


def pair_late(first, early, acat, bcat, b_parts):
    return call(
        pair_late_kernel,
        [(v, VMEM) for v in (first, early, acat, bcat)] + [(v, ANY) for v in b_parts],
        [vmem((WIDE, WIDE), f32), hbm((WIDE, WIDE)), vmem((2 * WIDE, AUX))],
        [pltpu.VMEM((WIDE, ROWS), f32), DMA((3, 4))],
        name="pair_late",
        aliases={3: 2},
    )


def core_sum_kernel(keep, got_in, own, s1, s2, s3, got, sem):
    copy = pltpu.make_async_copy(got_in, got, sem)
    copy.start()
    copy.wait()
    high = position()[0]
    for step, out in enumerate((own, s1, s2, s3)):
        for wave in range(2):
            at = pl.multiple_of((1 - wave) * 2 * ROWS + ((high + step) % 4) * SHARE, SHARE)
            value = keep[pl.ds(at, SHARE)] + got[pl.ds(at, SHARE)].astype(f32)
            out[wave * SHARE : (wave + 1) * SHARE] = value.astype(out.dtype)


def core_sum(keep, got):
    share = (2 * SHARE, WIDE)
    return call(
        core_sum_kernel,
        [(keep, VMEM), (got, ANY)],
        [vmem(share, f32)] + [hbm(share)] * 3,
        [pltpu.VMEM(got.shape, bf16), DMA(())],
        name="core_sum",
    )


BLOCKS = (((0, 0), (3, 0), (1, 0), (0, 1)), ((3, 1), (2, 0), (1, 1), (2, 1)))


def amplitude_kernel(vir, occ, chosen, own, *refs):
    arrived, outs, got, sems = refs[:3], refs[3:5], refs[5], refs[6]
    copies = [
        pltpu.make_async_copy(r, got.at[i], sems.at[i]) for i, r in enumerate(arrived)
    ]
    for c in copies:
        c.start()
    high, core, y, x, z = position()
    occ_total = occ[chosen[0]] + occ[chosen[1]]
    lane = lax.broadcasted_iota(jnp.int32, (SHARE, ROWS), 1)
    row = lax.broadcasted_iota(jnp.int32, (SHARE, ROWS), 0)

    def row_energy(shift, second):
        block = vir[pl.ds((y * 4 + (x + shift) % 4) * 2 + z, 1), :]
        own_lane = lane == row + second * SHARE
        return jnp.sum(jnp.where(own_lane, block, 0.0), axis=1, keepdims=True)

    rows = (
        row_energy(
            jnp.where(high == 0, 1, jnp.where(high == 1, 3, 2)),
            jnp.where((high == 0) | (high == 3), 1, 0),
        ),
        row_energy(jnp.where(high < 2, 0, 2 * high - 3), high % 2),
    )
    places = []
    for first, last in zip(*BLOCKS):
        step = jnp.where(core == 0, first[0], last[0])
        away = jnp.where(core == 0, first[1], last[1])
        places.append((((y + step) % 4) * 4 + x) * 2 + jnp.where(away == 1, 1 - z, z))
    columns = jnp.concatenate([vir[pl.ds(at, 1), :] for at in places], axis=1)
    for c in copies:
        c.wait()
    for wave, out in enumerate(outs):
        part = slice(wave * SHARE, (wave + 1) * SHARE)
        total = own[part]
        for i in range(3):
            total = total + got[i, part].astype(f32)
        denominator = (rows[wave] + columns) - occ_total
        out[...] = (total / denominator).astype(bf16)


def amplitude(vir, occ, chosen, own, arrived):
    return call(
        amplitude_kernel,
        [(vir, VMEM), (occ, SMEM), (chosen, SMEM), (own, VMEM)]
        + [(v, ANY) for v in arrived],
        [hbm((SHARE, WIDE))] * 2,
        [pltpu.VMEM((3, *own.shape), bf16), DMA((3,))],
        name="amplitude",
    )


def gather_rows(mine, other, tcat, sems):
    high, core = position()[:2]
    copies = []
    for k in range(4):
        rows = pl.ds(pl.multiple_of(((high - k + 4) % 4) * SHARE, SHARE), SHARE)
        for i, (v, of) in enumerate(((mine[k], core), (other[k], 1 - core))):
            columns = pl.ds(pl.multiple_of(of * WIDE, WIDE), WIDE)
            copies.append(pltpu.make_async_copy(v, tcat.at[rows, columns], sems.at[k, i]))
    for c in copies:
        c.start()
    return copies


def product(tcat, bcat, half):
    columns = pl.ds(pl.multiple_of(half * K2, K2), K2)
    return columns, jnp.dot(tcat[...], bcat[:, columns], preferred_element_type=f32)


TCAT = (2 * ROWS, 2 * WIDE)


def density_first_kernel(*refs):
    mine, other, bcat = refs[:4], refs[4:8], refs[8]
    outs, tcat, sems = refs[9:11], refs[11], refs[12]
    for c in gather_rows(mine, other, tcat, sems):
        c.wait()

    @pl.loop(0, 2)
    def _(half):
        columns, value = product(tcat, bcat, half)
        value = value.astype(bf16)
        for i, out in enumerate(outs):
            out[:HALF, columns] = value[i * HALF : (i + 1) * HALF]
            out[HALF:, columns] = value[(i + 2) * HALF : (i + 3) * HALF]


def density_first(mine, other, bcat):
    return call(
        density_first_kernel,
        [(v, ANY) for v in (*mine, *other)] + [(bcat, VMEM)],
        [hbm((ROWS, AUX))] * 2,
        [pltpu.VMEM(TCAT, bf16), DMA((4, 2))],
        name="density_first",
    )


def density_second_kernel(*refs):
    mine, other, (bcat, from_m, from_x) = refs[:4], refs[4:8], refs[8:11]
    x1, m2, own, tcat, got_m, got_x, row_sems, sems = refs[11:]
    rows_copies = gather_rows(mine, other, tcat, row_sems)
    copies = [
        pltpu.make_async_copy(from_m, got_m, sems.at[0]),
        pltpu.make_async_copy(from_x, got_x, sems.at[1]),
    ]
    for c in copies:
        c.start()
    for c in rows_copies + copies:
        c.wait()

    @pl.loop(0, 2)
    def _(half):
        columns, value = product(tcat, bcat, half)
        x = value[ROWS : ROWS + HALF] + got_m[HALF:, columns].astype(f32)
        m = value[ROWS + HALF :] + got_x[HALF:, columns].astype(f32)
        x1[:, columns] = x.astype(bf16)
        m2[:, columns] = m.astype(bf16)
        own[:HALF, columns] = value[:HALF] + got_x[:HALF, columns].astype(f32)
        own[HALF:, columns] = value[HALF:ROWS] + got_m[:HALF, columns].astype(f32)


def density_second(mine, other, bcat, from_m, from_x):
    return call(
        density_second_kernel,
        [(v, ANY) for v in (*mine, *other)]
        + [(bcat, VMEM), (from_m, ANY), (from_x, ANY)],
        [hbm((HALF, AUX))] * 2 + [vmem((ROWS, AUX), f32)],
        [pltpu.VMEM(TCAT, bf16)]
        + [pltpu.VMEM((ROWS, AUX), bf16)] * 2
        + [DMA((4, 2)), DMA((2,))],
        name="density_second",
    )


def add_kernel(own, one, two, out, got, sems):
    copies = [
        pltpu.make_async_copy(v, got.at[pl.ds(i * HALF, HALF)], sems.at[i])
        for i, v in enumerate((one, two))
    ]
    for c in copies:
        c.start()
    for c in copies:
        c.wait()
    out[...] = (own[...] + got[...].astype(f32)).astype(out.dtype)


def add(own, one, two):
    return call(
        add_kernel,
        [(own, VMEM), (one, ANY), (two, ANY)],
        [hbm((ROWS, AUX))],
        [pltpu.VMEM((ROWS, AUX), bf16), DMA((2,))],
        name="add",
    )[0]


def local(integrals, tiles, tile_index, vir_energy, occ_energy, pair_index):
    window = integrals.reshape(2 * ROWS, AUX)
    vir = vir_energy.reshape(-1, ROWS)
    up = [(g, g + 1) for g in range(7)]
    down = [(g + 1, g) for g in range(7)]
    last, first = ends(window)
    left = lax.ppermute(last, "grp", up)
    right = lax.ppermute(first, "grp", down)
    a, b = fit(tile_index.T, window, tiles, left, right)

    with jax.named_scope("first"):
        bm = send_y(b, 1)
        bp = send_y(b, -1)
        bo = send_z(b)
        ax = send_x(a, -1)
        am = send_x(a, 1)
    bo, bp, ax = arrive((bo, bp, ax), (bm, am, vir))
    with jax.named_scope("second"):
        bom = send_y(bo, 1)
        b2 = send_y(bp, -1)
        bop = send_z(bp)
        ad = send_x(ax, -1)
    early_sums, bcat, acat = pair_first((a, ax, am), (b, bm, bp, bo))
    c1, c2, c3 = cut([(b2, 0, 64), (bom, 64, 48), (bop, 112, 48)], (early_sums,), name="cut_b")
    with jax.named_scope("third"):
        c1 = send_z(c1)
        c2 = send_y(c2, 1)
        c3 = send_y(c3, -1)
    early_sums, bcat, acat, early = pair_early(early_sums, bcat, acat, ad, (bom, b2, bop))
    keep, send, bcat = pair_late(early_sums, early, acat, bcat, (c1, c2, c3))
    with jax.named_scope("core"):
        own, *s = core_sum(keep, send_core(send))
    with jax.named_scope("shares"):
        arrived = [send_high(v, k + 1) for k, v in enumerate(s)]
    mine = amplitude(vir, occ_energy, pair_index, own, arrived)

    def spread(wave):
        with jax.named_scope(f"spread_{wave}"):
            return [mine[wave]] + [send_high(mine[wave], k) for k in (1, 2, 3)]

    def other_core(wave, mine):
        with jax.named_scope(f"other_{wave}"):
            return [send_core(v) for v in mine]

    mine0, mine1 = spread(0), spread(1)
    other0 = other_core(0, mine0)
    other1 = other_core(1, mine1)
    x2_d1, m1_d2 = density_first(mine0, other0, bcat)
    with jax.named_scope("out"):
        from_m = send_x(x2_d1, 1)
        from_x = send_x(m1_d2, -1)
    x1, m2, own = density_second(mine1, other1, bcat, from_m, from_x)
    with jax.named_scope("out"):
        got_x1 = send_x(x1, 1)
        got_m2 = send_x(m2, -1)
    return add(own, got_x1, got_m2)


def solution(mesh):
    in_specs = (P(None, "blk", "grp"), P("grp", None, None), P("grp", None), P(), P(), P())
    return jax.shard_map(
        local, mesh=mesh, in_specs=in_specs, out_specs=P("blk", "grp"), check_vma=False
    )
```

```python
import functools

import jax
import jax.numpy as jnp
from jax import lax
from jax.experimental import pallas as pl
from jax.experimental.pallas import tpu as pltpu
from jax.sharding import PartitionSpec as P

TILE = 128
HB = 4
BAND = 2 * HB + 1
ROWS = 160
AUX = 2560
HALO = HB * TILE
bf16 = jnp.bfloat16
f32 = jnp.float32
MIB = 1 << 20


def blk_index(y, x, z):
    return ((y % 4) * 4 + x % 4) * 2 + z


PLACES = [(y, x, z) for y in range(4) for x in range(4) for z in range(2)]


def send_y(v, step):
    pairs = [(blk_index(y, x, z), blk_index(y + step, x, z)) for y, x, z in PLACES]
    return lax.ppermute(v, "blk", pairs)


def send_x(v, step):
    pairs = [(blk_index(y, x, z), blk_index(y, x + step, z)) for y, x, z in PLACES]
    return lax.ppermute(v, "blk", pairs)


def send_z(v):
    pairs = [(blk_index(y, x, z), blk_index(y, x, 1 - z)) for y, x, z in PLACES]
    return lax.ppermute(v, "blk", pairs)


def send_core(v):
    return lax.ppermute(v, "grp", [(g, g ^ 1) for g in range(8)])


def send_high(v, step):
    return lax.ppermute(v, "grp", [(g, (g + 2 * step) % 8) for g in range(8)])


def params(mib=28):
    return pltpu.CompilerParams(vmem_limit_bytes=mib * MIB)


def cost():
    return pl.CostEstimate(flops=1000, bytes_accessed=1000, transcendentals=0)


def position():
    group = lax.axis_index("grp").astype(jnp.int32)
    me = lax.axis_index("blk").astype(jnp.int32)
    return group // 2, group % 2, me // 8, (me // 2) % 4, me % 2


ANY = pl.BlockSpec(memory_space=pl.ANY)
VMEM = pl.BlockSpec(memory_space=pltpu.VMEM)
SMEM = pl.BlockSpec(memory_space=pltpu.SMEM)
DMA = pltpu.SemaphoreType.DMA
HALF = ROWS // 2
SHARE = ROWS // 2
WIDE = 4 * ROWS
K2 = AUX // 2
K4 = AUX // 4


def hbm(shape, dtype=bf16):
    return jax.ShapeDtypeStruct(shape, dtype)


def vmem(shape, dtype=bf16):
    return pltpu.VMEM(shape, dtype)


def call(kernel, args, outs, scratch=(), name=None, aliases=None, mib=28):
    return pl.pallas_call(
        kernel,
        in_specs=[spec for _, spec in args],
        out_specs=[VMEM] * len(outs),
        out_shape=list(outs),
        scratch_shapes=list(scratch),
        input_output_aliases=aliases or {},
        compiler_params=params(mib),
        cost_estimate=cost(),
        name=name,
    )(*[a for a, _ in args])


INNER = (2, 3, 4, 5, 6, 7)
EDGE = (0, 1, 8, 9)


def fit_inner_kernel(index, own_in, tiles_in, a, b, own, edge, tiles, weights, own_sem, sems):
    own_copies = [
        pltpu.make_async_copy(
            own_in.at[pl.ds(i * ROWS, ROWS)], own.at[pl.ds(i * ROWS, ROWS)], own_sem.at[i]
        )
        for i in range(2)
    ]
    copies = {}
    for p in INNER + EDGE:
        part = pl.ds(p * 2 * BAND, 2 * BAND)
        copies[p] = pltpu.make_async_copy(tiles_in.at[part], tiles.at[part], sems.at[p])
    copies[INNER[0]].start()
    for c in own_copies:
        c.start()
    for p in (INNER + EDGE)[1:]:
        copies[p].start()
    zero = jnp.zeros((TILE, TILE), bf16)

    def build(p, out):
        out[:TILE, TILE:] = zero
        out[BAND * TILE :, :TILE] = zero
        for q in range(2):
            for o in range(BAND):
                slot = p * 2 * BAND + q * BAND + o
                at = (q + o) * TILE
                out[at : at + TILE, q * TILE : (q + 1) * TILE] = jnp.where(
                    index[1, slot] == 1, tiles[slot], zero
                )

    for p in INNER:
        copies[p].wait()
        if p == INNER[0]:
            for c in own_copies:
                c.wait()
        build(p, weights)
        window = own[:, (2 * p - HB) * TILE : (2 * p + HB + 2) * TILE]
        fitted = jnp.dot(window, weights[...], preferred_element_type=f32).astype(bf16)
        columns = slice(p * 2 * TILE, (p + 1) * 2 * TILE)
        a[:, columns] = fitted[:ROWS]
        b[:, columns] = fitted[ROWS:]
    for n, p in enumerate(EDGE):
        copies[p].wait()
        build(p, edge.at[n])


def fit_edge_kernel(left, right, own, edge, _, __, a, b, ext):
    ext[:, :HALO] = left[...]
    ext[:, HALO : 3 * HALO] = own[:, : 2 * HALO]
    ext[:, 3 * HALO : 5 * HALO] = own[:, AUX - 2 * HALO :]
    ext[:, 5 * HALO :] = right[...]
    for n, p in enumerate(EDGE):
        at = (0, 2, 12, 14)[n] * TILE
        window = ext[:, at : at + (BAND + 1) * TILE]
        fitted = jnp.dot(window, edge[n], preferred_element_type=f32).astype(bf16)
        columns = slice(p * 2 * TILE, (p + 1) * 2 * TILE)
        a[:, columns] = fitted[:ROWS]
        b[:, columns] = fitted[ROWS:]


def fit(index, own, tiles, left, right):
    banded = ((BAND + 1) * TILE, 2 * TILE)
    a, b, own, edge = call(
        fit_inner_kernel,
        [(index, SMEM), (own, ANY), (tiles, ANY)],
        [vmem((ROWS, AUX)), vmem((ROWS, AUX)), vmem((2 * ROWS, AUX)), vmem((4, *banded))],
        [pltpu.VMEM(tiles.shape, bf16), pltpu.VMEM(banded, bf16), DMA((2,)), DMA((10,))],
        name="fit_inner",
        mib=56,
    )
    return call(
        fit_edge_kernel,
        [(v, VMEM) for v in (left, right, own, edge, a, b)],
        [vmem((ROWS, AUX))] * 2,
        [pltpu.VMEM((2 * ROWS, 6 * HALO), bf16)],
        name="fit_edge",
        aliases={4: 0, 5: 1},
    )


def ends_kernel(own, last, first, sems):
    copies = [
        pltpu.make_async_copy(own.at[:, pl.ds(AUX - HALO, HALO)], last, sems.at[0]),
        pltpu.make_async_copy(own.at[:, pl.ds(0, HALO)], first, sems.at[1]),
    ]
    for c in copies:
        c.start()
    for c in copies:
        c.wait()


def ends(own):
    outs = [vmem((2 * ROWS, HALO))] * 2
    return call(ends_kernel, [(own, ANY)], outs, [DMA((2,))], name="ends", mib=60)


def cut(parts, after=(), name=None):
    def kernel(*refs):
        ins, outs, sems = refs[: len(parts)], refs[-1 - len(parts) : -1], refs[-1]
        copies = [
            pltpu.make_async_copy(i.at[pl.ds(r, n)], o, sems.at[j])
            for j, (i, o, (_, r, n)) in enumerate(zip(ins, outs, parts))
        ]
        for c in copies:
            c.start()
        for c in copies:
            c.wait()

    return pl.pallas_call(
        kernel,
        in_specs=[ANY] * (len(parts) + len(after)),
        out_specs=[ANY] * len(parts),
        out_shape=[hbm((n, AUX)) for _, _, n in parts],
        scratch_shapes=[DMA((len(parts),))],
        compiler_params=params(),
        cost_estimate=cost(),
        name=name,
    )(*[p[0] for p in parts], *after)


def arrive(parts, after):
    n = len(parts)
    return pl.pallas_call(
        lambda *refs: None,
        in_specs=[ANY] * (n + len(after)),
        out_specs=[ANY] * n,
        out_shape=[hbm(v.shape, v.dtype) for v in parts],
        input_output_aliases={i: i for i in range(n)},
        compiler_params=params(),
        cost_estimate=cost(),
        name="arrive",
    )(*parts, *after)


def row_copies(moves, out, sems, part):
    columns = pl.ds(pl.multiple_of(part * K4, K4), K4)
    return [
        pltpu.make_async_copy(
            v.at[pl.ds(r, n), columns], out.at[pl.ds(at, n), columns], sems.at[i, part]
        )
        for i, (v, r, n, at) in enumerate(moves)
    ]


def b_moves(parts, at=0):
    moves = []
    for p in parts:
        moves.append((p, 0, p.shape[0], at))
        at += p.shape[0]
    return moves


def products(copies, acat, bcat, wanted, unroll=False):
    for part in range(4):
        for c in copies(part):
            c.start()

    if unroll:
        for c in (c for part in range(4) for c in copies(part)):
            c.wait()
        for a_rows, b_rows, total in wanted:
            total[...] = lax.dot_general(
                acat[a_rows], bcat[b_rows], (((1,), (1,)), ((), ())),
                preferred_element_type=f32,
            )
        return

    @pl.loop(0, 4)
    def _(part):
        for c in copies(part):
            c.wait()
        columns = pl.ds(pl.multiple_of(part * K4, K4), K4)
        for a_rows, b_rows, total in wanted:
            value = lax.dot_general(
                acat[a_rows, columns], bcat[b_rows, columns], (((1,), (1,)), ((), ())),
                preferred_element_type=f32,
            )

            @pl.when(part == 0)
            def _():
                total[...] = value

            @pl.when(part > 0)
            def _():
                total[...] += value


def pair_first_kernel(own, ax, am, *refs):
    b_refs = refs[:4]
    total, bcat, acat, a_sems, b_sems = refs[4:]
    a_moves = [
        (own, 0, ROWS, 0),
        (ax, 0, HALF, ROWS),
        (ax, HALF, HALF, 2 * ROWS),
        (am, 0, HALF, 2 * ROWS + HALF),
        (am, HALF, HALF, ROWS + HALF),
    ]
    rows = slice(0, 3 * ROWS)
    products(
        lambda part: row_copies(a_moves, acat, a_sems, part)
        + row_copies(b_moves(b_refs), bcat, b_sems, part),
        acat, bcat, [(rows, slice(0, WIDE), total.at[rows])],
    )


def pair_first(a_parts, b_parts):
    return call(
        pair_first_kernel,
        [(v, ANY) for v in (*a_parts, *b_parts)],
        [vmem((WIDE, WIDE), f32), vmem((2 * WIDE, AUX)), vmem((WIDE, AUX))],
        [DMA((5, 4)), DMA((4, 4))],
        name="pair_first",
    )


def pair_early_kernel(first_in, bcat_in, acat_in, ad, *refs):
    b_refs = refs[:3]
    first, bcat, acat, early, a_sems, b_sems = refs[3:]
    rows = slice(3 * ROWS, WIDE)
    products(
        lambda part: row_copies([(ad, 0, ROWS, 3 * ROWS)], acat, a_sems, part)
        + row_copies(b_moves(b_refs, WIDE), bcat, b_sems, part),
        acat, bcat,
        [
            (rows, slice(0, WIDE), first.at[rows]),
            (slice(0, WIDE), slice(WIDE, 7 * ROWS), early),
        ],
    )


def pair_early(first, bcat, acat, ad, b_parts):
    return call(
        pair_early_kernel,
        [(v, VMEM) for v in (first, bcat, acat)] + [(v, ANY) for v in (ad, *b_parts)],
        [
            vmem((WIDE, WIDE), f32),
            vmem((2 * WIDE, AUX)),
            vmem((WIDE, AUX)),
            vmem((WIDE, 3 * ROWS), f32),
        ],
        [DMA((1, 4)), DMA((3, 4))],
        name="pair_early",
        aliases={0: 0, 1: 1, 2: 2},
    )


def pair_late_kernel(first, early, acat, bcat_in, *refs):
    b_refs = refs[:3]
    keep, send, bcat, late, sems = refs[3:]
    products(
        lambda part: row_copies(b_moves(b_refs, 7 * ROWS), bcat, sems, part),
        acat, bcat, [(slice(0, WIDE), slice(7 * ROWS, 8 * ROWS), late)], unroll=True,
    )
    core = position()[1]
    split = 3 * ROWS

    @pl.when(core == 0)
    def _():
        keep[...] = first[...]
        send[:, :split] = early[...].astype(bf16)
        send[:, split:] = late[...].astype(bf16)

    @pl.when(core == 1)
    def _():
        send[...] = first[...].astype(bf16)
        keep[:, :split] = early[...]
        keep[:, split:] = late[...]


def pair_late(first, early, acat, bcat, b_parts):
    return call(
        pair_late_kernel,
        [(v, VMEM) for v in (first, early, acat, bcat)] + [(v, ANY) for v in b_parts],
        [vmem((WIDE, WIDE), f32), hbm((WIDE, WIDE)), vmem((2 * WIDE, AUX))],
        [pltpu.VMEM((WIDE, ROWS), f32), DMA((3, 4))],
        name="pair_late",
        aliases={3: 2},
    )


def core_sum_kernel(keep, got_in, own, s1, s2, s3, got, sem):
    copy = pltpu.make_async_copy(got_in, got, sem)
    copy.start()
    copy.wait()
    high = position()[0]
    for step, out in enumerate((own, s1, s2, s3)):
        for wave in range(2):
            at = pl.multiple_of((1 - wave) * 2 * ROWS + ((high + step) % 4) * SHARE, SHARE)
            value = keep[pl.ds(at, SHARE)] + got[pl.ds(at, SHARE)].astype(f32)
            out[wave * SHARE : (wave + 1) * SHARE] = value.astype(out.dtype)


def core_sum(keep, got):
    share = (2 * SHARE, WIDE)
    return call(
        core_sum_kernel,
        [(keep, VMEM), (got, ANY)],
        [vmem(share, f32)] + [hbm(share)] * 3,
        [pltpu.VMEM(got.shape, bf16), DMA(())],
        name="core_sum",
    )


BLOCKS = (((0, 0), (3, 0), (1, 0), (0, 1)), ((3, 1), (2, 0), (1, 1), (2, 1)))


def amplitude_kernel(vir, occ, chosen, own, *refs):
    arrived, outs, got, sems = refs[:3], refs[3:5], refs[5], refs[6]
    copies = [
        pltpu.make_async_copy(r, got.at[i], sems.at[i]) for i, r in enumerate(arrived)
    ]
    for c in copies:
        c.start()
    high, core, y, x, z = position()
    occ_total = occ[chosen[0]] + occ[chosen[1]]
    lane = lax.broadcasted_iota(jnp.int32, (SHARE, ROWS), 1)
    row = lax.broadcasted_iota(jnp.int32, (SHARE, ROWS), 0)

    def row_energy(shift, second):
        block = vir[pl.ds((y * 4 + (x + shift) % 4) * 2 + z, 1), :]
        own_lane = lane == row + second * SHARE
        return jnp.sum(jnp.where(own_lane, block, 0.0), axis=1, keepdims=True)

    rows = (
        row_energy(
            jnp.where(high == 0, 1, jnp.where(high == 1, 3, 2)),
            jnp.where((high == 0) | (high == 3), 1, 0),
        ),
        row_energy(jnp.where(high < 2, 0, 2 * high - 3), high % 2),
    )
    places = []
    for first, last in zip(*BLOCKS):
        step = jnp.where(core == 0, first[0], last[0])
        away = jnp.where(core == 0, first[1], last[1])
        places.append((((y + step) % 4) * 4 + x) * 2 + jnp.where(away == 1, 1 - z, z))
    columns = jnp.concatenate([vir[pl.ds(at, 1), :] for at in places], axis=1)
    for c in copies:
        c.wait()
    for wave, out in enumerate(outs):
        part = slice(wave * SHARE, (wave + 1) * SHARE)
        total = own[part]
        for i in range(3):
            total = total + got[i, part].astype(f32)
        denominator = (rows[wave] + columns) - occ_total
        out[...] = (total / denominator).astype(bf16)


def amplitude(vir, occ, chosen, own, arrived):
    return call(
        amplitude_kernel,
        [(vir, VMEM), (occ, SMEM), (chosen, SMEM), (own, VMEM)]
        + [(v, ANY) for v in arrived],
        [hbm((SHARE, WIDE))] * 2,
        [pltpu.VMEM((3, *own.shape), bf16), DMA((3,))],
        name="amplitude",
    )


def gather_rows(mine, other, tcat, sems):
    high, core = position()[:2]
    copies = []
    for k in range(4):
        rows = pl.ds(pl.multiple_of(((high - k + 4) % 4) * SHARE, SHARE), SHARE)
        for i, (v, of) in enumerate(((mine[k], core), (other[k], 1 - core))):
            columns = pl.ds(pl.multiple_of(of * WIDE, WIDE), WIDE)
            copies.append(pltpu.make_async_copy(v, tcat.at[rows, columns], sems.at[k, i]))
    for c in copies:
        c.start()
    return copies


def product(tcat, bcat, half):
    columns = pl.ds(pl.multiple_of(half * K2, K2), K2)
    return columns, jnp.dot(tcat[...], bcat[:, columns], preferred_element_type=f32)


TCAT = (2 * ROWS, 2 * WIDE)


def density_first_kernel(*refs):
    mine, other, bcat = refs[:4], refs[4:8], refs[8]
    outs, tcat, sems = refs[9:11], refs[11], refs[12]
    for c in gather_rows(mine, other, tcat, sems):
        c.wait()

    @pl.loop(0, 2)
    def _(half):
        columns, value = product(tcat, bcat, half)
        value = value.astype(bf16)
        for i, out in enumerate(outs):
            out[:HALF, columns] = value[i * HALF : (i + 1) * HALF]
            out[HALF:, columns] = value[(i + 2) * HALF : (i + 3) * HALF]


def density_first(mine, other, bcat):
    return call(
        density_first_kernel,
        [(v, ANY) for v in (*mine, *other)] + [(bcat, VMEM)],
        [hbm((ROWS, AUX))] * 2,
        [pltpu.VMEM(TCAT, bf16), DMA((4, 2))],
        name="density_first",
    )


def density_second_kernel(*refs):
    mine, other, (bcat, from_m, from_x) = refs[:4], refs[4:8], refs[8:11]
    x1, m2, own, tcat, got_m, got_x, row_sems, sems = refs[11:]
    rows_copies = gather_rows(mine, other, tcat, row_sems)
    copies = [
        pltpu.make_async_copy(from_m, got_m, sems.at[0]),
        pltpu.make_async_copy(from_x, got_x, sems.at[1]),
    ]
    for c in copies:
        c.start()
    for c in rows_copies + copies:
        c.wait()

    @pl.loop(0, 2)
    def _(half):
        columns, value = product(tcat, bcat, half)
        x = value[ROWS : ROWS + HALF] + got_m[HALF:, columns].astype(f32)
        m = value[ROWS + HALF :] + got_x[HALF:, columns].astype(f32)
        x1[:, columns] = x.astype(bf16)
        m2[:, columns] = m.astype(bf16)
        own[:HALF, columns] = value[:HALF] + got_x[:HALF, columns].astype(f32)
        own[HALF:, columns] = value[HALF:ROWS] + got_m[:HALF, columns].astype(f32)


def density_second(mine, other, bcat, from_m, from_x):
    return call(
        density_second_kernel,
        [(v, ANY) for v in (*mine, *other)]
        + [(bcat, VMEM), (from_m, ANY), (from_x, ANY)],
        [hbm((HALF, AUX))] * 2 + [vmem((ROWS, AUX), f32)],
        [pltpu.VMEM(TCAT, bf16)]
        + [pltpu.VMEM((ROWS, AUX), bf16)] * 2
        + [DMA((4, 2)), DMA((2,))],
        name="density_second",
    )


def add_kernel(own, one, two, out, got, sems):
    copies = [
        pltpu.make_async_copy(v, got.at[pl.ds(i * HALF, HALF)], sems.at[i])
        for i, v in enumerate((one, two))
    ]
    for c in copies:
        c.start()
    for c in copies:
        c.wait()
    out[...] = (own[...] + got[...].astype(f32)).astype(out.dtype)


def add(own, one, two):
    return call(
        add_kernel,
        [(own, VMEM), (one, ANY), (two, ANY)],
        [hbm((ROWS, AUX))],
        [pltpu.VMEM((ROWS, AUX), bf16), DMA((2,))],
        name="add",
    )[0]


def local(integrals, tiles, tile_index, vir_energy, occ_energy, pair_index):
    window = integrals.reshape(2 * ROWS, AUX)
    vir = vir_energy.reshape(-1, ROWS)
    up = [(g, g + 1) for g in range(7)]
    down = [(g + 1, g) for g in range(7)]
    last, first = ends(window)
    left = lax.ppermute(last, "grp", up)
    right = lax.ppermute(first, "grp", down)
    a, b = fit(tile_index.T, window, tiles, left, right)

    with jax.named_scope("first"):
        ax = send_x(a, -1)
        am = send_x(a, 1)
        bo = send_z(b)
        bp = send_y(b, -1)
        bm = send_y(b, 1)
    bo, bp = arrive((bo, bp), (bm, vir))
    with jax.named_scope("second"):
        bom = send_y(bo, 1)
        b2 = send_y(bp, -1)
        bop = send_z(bp)
        ad = send_x(ax, -1)
    early_sums, bcat, acat = pair_first((a, ax, am), (b, bm, bp, bo))
    c1, c2, c3 = cut([(b2, 0, 64), (bom, 64, 48), (bop, 112, 48)], (early_sums,), name="cut_b")
    with jax.named_scope("third"):
        c1 = send_z(c1)
        c2 = send_y(c2, 1)
        c3 = send_y(c3, -1)
    early_sums, bcat, acat, early = pair_early(early_sums, bcat, acat, ad, (bom, b2, bop))
    keep, send, bcat = pair_late(early_sums, early, acat, bcat, (c1, c2, c3))
    with jax.named_scope("core"):
        own, *s = core_sum(keep, send_core(send))
    with jax.named_scope("shares"):
        arrived = [send_high(s[k - 1], k) for k in (2, 1, 3)]
    mine = amplitude(vir, occ_energy, pair_index, own, arrived)

    def spread(wave):
        with jax.named_scope(f"spread_{wave}"):
            sent = {k: send_high(mine[wave], k) for k in (1, 3, 2)}
            return [mine[wave]] + [sent[k] for k in (1, 2, 3)]

    def other_core(wave, mine):
        with jax.named_scope(f"other_{wave}"):
            return [send_core(v) for v in mine]

    mine0, mine1 = spread(0), spread(1)
    other0 = other_core(0, mine0)
    other1 = other_core(1, mine1)
    x2_d1, m1_d2 = density_first(mine0, other0, bcat)
    with jax.named_scope("out"):
        from_m = send_x(x2_d1, 1)
        from_x = send_x(m1_d2, -1)
    x1, m2, own = density_second(mine1, other1, bcat, from_m, from_x)
    with jax.named_scope("out"):
        got_x1 = send_x(x1, 1)
        got_m2 = send_x(m2, -1)
    return add(own, got_x1, got_m2)


def solution(mesh):
    in_specs = (P(None, "blk", "grp"), P("grp", None, None), P("grp", None), P(), P(), P())
    return jax.shard_map(
        local, mesh=mesh, in_specs=in_specs, out_specs=P("blk", "grp"), check_vma=False
    )
```

```python
import functools

import jax
import jax.numpy as jnp
from jax import lax
from jax.experimental import pallas as pl
from jax.experimental.pallas import tpu as pltpu
from jax.sharding import PartitionSpec as P

TILE = 128
HB = 4
BAND = 2 * HB + 1
ROWS = 160
AUX = 2560
HALO = HB * TILE
bf16 = jnp.bfloat16
f32 = jnp.float32
MIB = 1 << 20


def blk_index(y, x, z):
    return ((y % 4) * 4 + x % 4) * 2 + z


PLACES = [(y, x, z) for y in range(4) for x in range(4) for z in range(2)]


def send_y(v, step):
    pairs = [(blk_index(y, x, z), blk_index(y + step, x, z)) for y, x, z in PLACES]
    return lax.ppermute(v, "blk", pairs)


def send_x(v, step):
    pairs = [(blk_index(y, x, z), blk_index(y, x + step, z)) for y, x, z in PLACES]
    return lax.ppermute(v, "blk", pairs)


def send_z(v):
    pairs = [(blk_index(y, x, z), blk_index(y, x, 1 - z)) for y, x, z in PLACES]
    return lax.ppermute(v, "blk", pairs)


def send_core(v):
    return lax.ppermute(v, "grp", [(g, g ^ 1) for g in range(8)])


def send_high(v, step):
    return lax.ppermute(v, "grp", [(g, (g + 2 * step) % 8) for g in range(8)])


def params(mib=28):
    return pltpu.CompilerParams(vmem_limit_bytes=mib * MIB)


def cost():
    return pl.CostEstimate(flops=1000, bytes_accessed=1000, transcendentals=0)


def position():
    group = lax.axis_index("grp").astype(jnp.int32)
    me = lax.axis_index("blk").astype(jnp.int32)
    return group // 2, group % 2, me // 8, (me // 2) % 4, me % 2


ANY = pl.BlockSpec(memory_space=pl.ANY)
VMEM = pl.BlockSpec(memory_space=pltpu.VMEM)
SMEM = pl.BlockSpec(memory_space=pltpu.SMEM)
DMA = pltpu.SemaphoreType.DMA
HALF = ROWS // 2
SHARE = ROWS // 2
WIDE = 4 * ROWS
K2 = AUX // 2
K4 = AUX // 4


def hbm(shape, dtype=bf16):
    return jax.ShapeDtypeStruct(shape, dtype)


def vmem(shape, dtype=bf16):
    return pltpu.VMEM(shape, dtype)


def call(kernel, args, outs, scratch=(), name=None, aliases=None, mib=28):
    return pl.pallas_call(
        kernel,
        in_specs=[spec for _, spec in args],
        out_specs=[VMEM] * len(outs),
        out_shape=list(outs),
        scratch_shapes=list(scratch),
        input_output_aliases=aliases or {},
        compiler_params=params(mib),
        cost_estimate=cost(),
        name=name,
    )(*[a for a, _ in args])


INNER = (2, 3, 4, 5, 6, 7)
EDGE = (0, 1, 8, 9)


def fit_inner_kernel(index, own_in, tiles_in, a, b, own, edge, tiles, weights, own_sem, sems):
    own_copies = [
        pltpu.make_async_copy(
            own_in.at[pl.ds(i * ROWS, ROWS)], own.at[pl.ds(i * ROWS, ROWS)], own_sem.at[i]
        )
        for i in range(2)
    ]
    copies = {}
    for p in INNER + EDGE:
        part = pl.ds(p * 2 * BAND, 2 * BAND)
        copies[p] = pltpu.make_async_copy(tiles_in.at[part], tiles.at[part], sems.at[p])
    copies[INNER[0]].start()
    for c in own_copies:
        c.start()
    for p in (INNER + EDGE)[1:]:
        copies[p].start()
    zero = jnp.zeros((TILE, TILE), bf16)

    def build(p, out):
        out[:TILE, TILE:] = zero
        out[BAND * TILE :, :TILE] = zero
        for q in range(2):
            for o in range(BAND):
                slot = p * 2 * BAND + q * BAND + o
                at = (q + o) * TILE
                out[at : at + TILE, q * TILE : (q + 1) * TILE] = jnp.where(
                    index[1, slot] == 1, tiles[slot], zero
                )

    for p in INNER:
        copies[p].wait()
        if p == INNER[0]:
            for c in own_copies:
                c.wait()
        build(p, weights)
        window = own[:, (2 * p - HB) * TILE : (2 * p + HB + 2) * TILE]
        fitted = jnp.dot(window, weights[...], preferred_element_type=f32).astype(bf16)
        columns = slice(p * 2 * TILE, (p + 1) * 2 * TILE)
        a[:, columns] = fitted[:ROWS]
        b[:, columns] = fitted[ROWS:]
    for n, p in enumerate(EDGE):
        copies[p].wait()
        build(p, edge.at[n])


def fit_edge_kernel(left, right, own, edge, _, __, a, b, ext):
    ext[:, :HALO] = left[...]
    ext[:, HALO : 3 * HALO] = own[:, : 2 * HALO]
    ext[:, 3 * HALO : 5 * HALO] = own[:, AUX - 2 * HALO :]
    ext[:, 5 * HALO :] = right[...]
    for n, p in enumerate(EDGE):
        at = (0, 2, 12, 14)[n] * TILE
        window = ext[:, at : at + (BAND + 1) * TILE]
        fitted = jnp.dot(window, edge[n], preferred_element_type=f32).astype(bf16)
        columns = slice(p * 2 * TILE, (p + 1) * 2 * TILE)
        a[:, columns] = fitted[:ROWS]
        b[:, columns] = fitted[ROWS:]


def fit(index, own, tiles, left, right):
    banded = ((BAND + 1) * TILE, 2 * TILE)
    a, b, own, edge = call(
        fit_inner_kernel,
        [(index, SMEM), (own, ANY), (tiles, ANY)],
        [vmem((ROWS, AUX)), vmem((ROWS, AUX)), vmem((2 * ROWS, AUX)), vmem((4, *banded))],
        [pltpu.VMEM(tiles.shape, bf16), pltpu.VMEM(banded, bf16), DMA((2,)), DMA((10,))],
        name="fit_inner",
        mib=56,
    )
    return call(
        fit_edge_kernel,
        [(v, VMEM) for v in (left, right, own, edge, a, b)],
        [vmem((ROWS, AUX))] * 2,
        [pltpu.VMEM((2 * ROWS, 6 * HALO), bf16)],
        name="fit_edge",
        aliases={4: 0, 5: 1},
    )


def ends_kernel(own, last, first, sems):
    copies = [
        pltpu.make_async_copy(own.at[:, pl.ds(AUX - HALO, HALO)], last, sems.at[0]),
        pltpu.make_async_copy(own.at[:, pl.ds(0, HALO)], first, sems.at[1]),
    ]
    for c in copies:
        c.start()
    for c in copies:
        c.wait()


def ends(own):
    outs = [vmem((2 * ROWS, HALO))] * 2
    return call(ends_kernel, [(own, ANY)], outs, [DMA((2,))], name="ends", mib=60)


def cut(parts, after=(), name=None):
    def kernel(*refs):
        ins, outs, sems = refs[: len(parts)], refs[-1 - len(parts) : -1], refs[-1]
        copies = [
            pltpu.make_async_copy(i.at[pl.ds(r, n)], o, sems.at[j])
            for j, (i, o, (_, r, n)) in enumerate(zip(ins, outs, parts))
        ]
        for c in copies:
            c.start()
        for c in copies:
            c.wait()

    return pl.pallas_call(
        kernel,
        in_specs=[ANY] * (len(parts) + len(after)),
        out_specs=[ANY] * len(parts),
        out_shape=[hbm((n, AUX)) for _, _, n in parts],
        scratch_shapes=[DMA((len(parts),))],
        compiler_params=params(),
        cost_estimate=cost(),
        name=name,
    )(*[p[0] for p in parts], *after)


def arrive(parts, after):
    n = len(parts)
    return pl.pallas_call(
        lambda *refs: None,
        in_specs=[ANY] * (n + len(after)),
        out_specs=[ANY] * n,
        out_shape=[hbm(v.shape, v.dtype) for v in parts],
        input_output_aliases={i: i for i in range(n)},
        compiler_params=params(),
        cost_estimate=cost(),
        name="arrive",
    )(*parts, *after)


def row_copies(moves, out, sems, part):
    columns = pl.ds(pl.multiple_of(part * K4, K4), K4)
    return [
        pltpu.make_async_copy(
            v.at[pl.ds(r, n), columns], out.at[pl.ds(at, n), columns], sems.at[i, part]
        )
        for i, (v, r, n, at) in enumerate(moves)
    ]


def b_moves(parts, at=0):
    moves = []
    for p in parts:
        moves.append((p, 0, p.shape[0], at))
        at += p.shape[0]
    return moves


def products(copies, acat, bcat, wanted, unroll=False):
    for part in range(4):
        for c in copies(part):
            c.start()

    if unroll:
        for c in (c for part in range(4) for c in copies(part)):
            c.wait()
        for a_rows, b_rows, total in wanted:
            total[...] = lax.dot_general(
                acat[a_rows], bcat[b_rows], (((1,), (1,)), ((), ())),
                preferred_element_type=f32,
            )
        return

    @pl.loop(0, 4)
    def _(part):
        for c in copies(part):
            c.wait()
        columns = pl.ds(pl.multiple_of(part * K4, K4), K4)
        for a_rows, b_rows, total in wanted:
            value = lax.dot_general(
                acat[a_rows, columns], bcat[b_rows, columns], (((1,), (1,)), ((), ())),
                preferred_element_type=f32,
            )

            @pl.when(part == 0)
            def _():
                total[...] = value

            @pl.when(part > 0)
            def _():
                total[...] += value


def pair_first_kernel(own, ax, am, *refs):
    b_refs = refs[:4]
    total, bcat, acat, a_sems, b_sems = refs[4:]
    a_moves = [
        (own, 0, ROWS, 0),
        (ax, 0, HALF, ROWS),
        (ax, HALF, HALF, 2 * ROWS),
        (am, 0, HALF, 2 * ROWS + HALF),
        (am, HALF, HALF, ROWS + HALF),
    ]
    rows = slice(0, 3 * ROWS)
    products(
        lambda part: row_copies(a_moves, acat, a_sems, part)
        + row_copies(b_moves(b_refs), bcat, b_sems, part),
        acat, bcat, [(rows, slice(0, WIDE), total.at[rows])],
    )


def pair_first(a_parts, b_parts):
    return call(
        pair_first_kernel,
        [(v, ANY) for v in (*a_parts, *b_parts)],
        [vmem((WIDE, WIDE), f32), vmem((2 * WIDE, AUX)), vmem((WIDE, AUX))],
        [DMA((5, 4)), DMA((4, 4))],
        name="pair_first",
    )


def pair_early_kernel(first_in, bcat_in, acat_in, ad, *refs):
    b_refs = refs[:3]
    first, bcat, acat, early, a_sems, b_sems = refs[3:]
    rows = slice(3 * ROWS, WIDE)
    products(
        lambda part: row_copies([(ad, 0, ROWS, 3 * ROWS)], acat, a_sems, part)
        + row_copies(b_moves(b_refs, WIDE), bcat, b_sems, part),
        acat, bcat,
        [
            (rows, slice(0, WIDE), first.at[rows]),
            (slice(0, WIDE), slice(WIDE, 7 * ROWS), early),
        ],
        unroll=True,
    )


def pair_early(first, bcat, acat, ad, b_parts):
    return call(
        pair_early_kernel,
        [(v, VMEM) for v in (first, bcat, acat)] + [(v, ANY) for v in (ad, *b_parts)],
        [
            vmem((WIDE, WIDE), f32),
            vmem((2 * WIDE, AUX)),
            vmem((WIDE, AUX)),
            vmem((WIDE, 3 * ROWS), f32),
        ],
        [DMA((1, 4)), DMA((3, 4))],
        name="pair_early",
        aliases={0: 0, 1: 1, 2: 2},
    )


def pair_late_kernel(first, early, acat, bcat_in, *refs):
    b_refs = refs[:3]
    keep, send, bcat, late, sems = refs[3:]
    products(
        lambda part: row_copies(b_moves(b_refs, 7 * ROWS), bcat, sems, part),
        acat, bcat, [(slice(0, WIDE), slice(7 * ROWS, 8 * ROWS), late)], unroll=True,
    )
    core = position()[1]
    split = 3 * ROWS

    @pl.when(core == 0)
    def _():
        keep[...] = first[...]
        send[:, :split] = early[...].astype(bf16)
        send[:, split:] = late[...].astype(bf16)

    @pl.when(core == 1)
    def _():
        send[...] = first[...].astype(bf16)
        keep[:, :split] = early[...]
        keep[:, split:] = late[...]


def pair_late(first, early, acat, bcat, b_parts):
    return call(
        pair_late_kernel,
        [(v, VMEM) for v in (first, early, acat, bcat)] + [(v, ANY) for v in b_parts],
        [vmem((WIDE, WIDE), f32), hbm((WIDE, WIDE)), vmem((2 * WIDE, AUX))],
        [pltpu.VMEM((WIDE, ROWS), f32), DMA((3, 4))],
        name="pair_late",
        aliases={3: 2},
    )


def core_sum_kernel(keep, got, own, s1, s2, s3):
    high = position()[0]
    for step, out in enumerate((own, s1, s2, s3)):
        for wave in range(2):
            at = pl.multiple_of((1 - wave) * 2 * ROWS + ((high + step) % 4) * SHARE, SHARE)
            value = keep[pl.ds(at, SHARE)] + got[pl.ds(at, SHARE)].astype(f32)
            out[wave * SHARE : (wave + 1) * SHARE] = value.astype(out.dtype)


def core_sum(keep, got):
    share = (2 * SHARE, WIDE)
    return call(
        core_sum_kernel,
        [(keep, VMEM), (got, VMEM)],
        [vmem(share, f32)] + [hbm(share)] * 3,
        name="core_sum",
    )


BLOCKS = (((0, 0), (3, 0), (1, 0), (0, 1)), ((3, 1), (2, 0), (1, 1), (2, 1)))


def amplitude_kernel(vir, occ, chosen, own, *refs):
    arrived, outs = refs[:3], refs[3:5]
    high, core, y, x, z = position()
    occ_total = occ[chosen[0]] + occ[chosen[1]]
    lane = lax.broadcasted_iota(jnp.int32, (SHARE, ROWS), 1)
    row = lax.broadcasted_iota(jnp.int32, (SHARE, ROWS), 0)

    def row_energy(shift, second):
        block = vir[pl.ds((y * 4 + (x + shift) % 4) * 2 + z, 1), :]
        own_lane = lane == row + second * SHARE
        return jnp.sum(jnp.where(own_lane, block, 0.0), axis=1, keepdims=True)

    rows = (
        row_energy(
            jnp.where(high == 0, 1, jnp.where(high == 1, 3, 2)),
            jnp.where((high == 0) | (high == 3), 1, 0),
        ),
        row_energy(jnp.where(high < 2, 0, 2 * high - 3), high % 2),
    )
    places = []
    for first, last in zip(*BLOCKS):
        step = jnp.where(core == 0, first[0], last[0])
        away = jnp.where(core == 0, first[1], last[1])
        places.append((((y + step) % 4) * 4 + x) * 2 + jnp.where(away == 1, 1 - z, z))
    columns = jnp.concatenate([vir[pl.ds(at, 1), :] for at in places], axis=1)
    for wave, out in enumerate(outs):
        part = slice(wave * SHARE, (wave + 1) * SHARE)
        total = own[part]
        for r in arrived:
            total = total + r[part].astype(f32)
        denominator = (rows[wave] + columns) - occ_total
        out[...] = (total / denominator).astype(bf16)


def amplitude(vir, occ, chosen, own, arrived):
    return call(
        amplitude_kernel,
        [(vir, VMEM), (occ, SMEM), (chosen, SMEM), (own, VMEM)]
        + [(v, VMEM) for v in arrived],
        [hbm((SHARE, WIDE))] * 2,
        name="amplitude",
    )


def gather_rows(mine, other, tcat):
    high, core = position()[:2]
    for k in range(4):
        rows = pl.ds(pl.multiple_of(((high - k + 4) % 4) * SHARE, SHARE), SHARE)
        for v, of in ((mine[k], core), (other[k], 1 - core)):
            tcat[rows, pl.ds(pl.multiple_of(of * WIDE, WIDE), WIDE)] = v[...]


def product(tcat, bcat, half):
    columns = pl.ds(pl.multiple_of(half * K2, K2), K2)
    return columns, jnp.dot(tcat[...], bcat[:, columns], preferred_element_type=f32)


TCAT = (2 * ROWS, 2 * WIDE)


def density_first_kernel(*refs):
    mine, other, bcat = refs[:4], refs[4:8], refs[8]
    outs, tcat = refs[9:11], refs[11]
    gather_rows(mine, other, tcat)

    @pl.loop(0, 2)
    def _(half):
        columns, value = product(tcat, bcat, half)
        value = value.astype(bf16)
        for i, out in enumerate(outs):
            out[:HALF, columns] = value[i * HALF : (i + 1) * HALF]
            out[HALF:, columns] = value[(i + 2) * HALF : (i + 3) * HALF]


def density_first(mine, other, bcat):
    return call(
        density_first_kernel,
        [(v, VMEM) for v in (*mine, *other, bcat)],
        [hbm((ROWS, AUX))] * 2,
        [pltpu.VMEM(TCAT, bf16)],
        name="density_first",
    )


def density_second_kernel(*refs):
    mine, other, (bcat, got_m, got_x) = refs[:4], refs[4:8], refs[8:11]
    x1, m2, own, tcat = refs[11:]
    gather_rows(mine, other, tcat)

    @pl.loop(0, 2)
    def _(half):
        columns, value = product(tcat, bcat, half)
        x = value[ROWS : ROWS + HALF] + got_m[HALF:, columns].astype(f32)
        m = value[ROWS + HALF :] + got_x[HALF:, columns].astype(f32)
        x1[:, columns] = x.astype(bf16)
        m2[:, columns] = m.astype(bf16)
        own[:HALF, columns] = value[:HALF] + got_x[:HALF, columns].astype(f32)
        own[HALF:, columns] = value[HALF:ROWS] + got_m[:HALF, columns].astype(f32)


def density_second(mine, other, bcat, from_m, from_x):
    return call(
        density_second_kernel,
        [(v, VMEM) for v in (*mine, *other, bcat, from_m, from_x)],
        [hbm((HALF, AUX))] * 2 + [vmem((ROWS, AUX), f32)],
        [pltpu.VMEM(TCAT, bf16)],
        name="density_second",
    )


def add_kernel(own, one, two, out):
    out[:HALF] = (own[:HALF] + one[...].astype(f32)).astype(bf16)
    out[HALF:] = (own[HALF:] + two[...].astype(f32)).astype(bf16)


def add(own, one, two):
    return call(
        add_kernel,
        [(own, VMEM), (one, VMEM), (two, VMEM)],
        [hbm((ROWS, AUX))],
        name="add",
    )[0]


def local(integrals, tiles, tile_index, vir_energy, occ_energy, pair_index):
    window = integrals.reshape(2 * ROWS, AUX)
    vir = vir_energy.reshape(-1, ROWS)
    up = [(g, g + 1) for g in range(7)]
    down = [(g + 1, g) for g in range(7)]
    last, first = ends(window)
    left = lax.ppermute(last, "grp", up)
    right = lax.ppermute(first, "grp", down)
    a, b = fit(tile_index.T, window, tiles, left, right)

    with jax.named_scope("first"):
        ax = send_x(a, -1)
        am = send_x(a, 1)
        bo = send_z(b)
        bp = send_y(b, -1)
        bm = send_y(b, 1)
    bo, bp = arrive((bo, bp), (bm, vir))
    with jax.named_scope("second"):
        bom = send_y(bo, 1)
        b2 = send_y(bp, -1)
        bop = send_z(bp)
        ad = send_x(ax, -1)
    early_sums, bcat, acat = pair_first((a, ax, am), (b, bm, bp, bo))
    c1, c2, c3 = cut([(b2, 0, 64), (bom, 64, 48), (bop, 112, 48)], (early_sums,), name="cut_b")
    with jax.named_scope("third"):
        c1 = send_z(c1)
        c2 = send_y(c2, 1)
        c3 = send_y(c3, -1)
    early_sums, bcat, acat, early = pair_early(early_sums, bcat, acat, ad, (bom, b2, bop))
    keep, send, bcat = pair_late(early_sums, early, acat, bcat, (c1, c2, c3))
    with jax.named_scope("core"):
        own, *s = core_sum(keep, send_core(send))
    with jax.named_scope("shares"):
        arrived = [send_high(s[k - 1], k) for k in (2, 1, 3)]
    mine = amplitude(vir, occ_energy, pair_index, own, arrived)

    def spread(wave):
        with jax.named_scope(f"spread_{wave}"):
            sent = {k: send_high(mine[wave], k) for k in (1, 3, 2)}
            return [mine[wave]] + [sent[k] for k in (1, 2, 3)]

    def other_core(wave, mine):
        with jax.named_scope(f"other_{wave}"):
            return [send_core(v) for v in mine]

    mine0, mine1 = spread(0), spread(1)
    other0 = other_core(0, mine0)
    other1 = other_core(1, mine1)
    x2_d1, m1_d2 = density_first(mine0, other0, bcat)
    with jax.named_scope("out"):
        from_m = send_x(x2_d1, 1)
        from_x = send_x(m1_d2, -1)
    x1, m2, own = density_second(mine1, other1, bcat, from_m, from_x)
    with jax.named_scope("out"):
        got_x1 = send_x(x1, 1)
        got_m2 = send_x(m2, -1)
    return add(own, got_x1, got_m2)


def solution(mesh):
    in_specs = (P(None, "blk", "grp"), P("grp", None, None), P("grp", None), P(), P(), P())
    return jax.shard_map(
        local, mesh=mesh, in_specs=in_specs, out_specs=P("blk", "grp"), check_vma=False
    )
```

```python
import functools

import jax
import jax.numpy as jnp
from jax import lax
from jax.experimental import pallas as pl
from jax.experimental.pallas import tpu as pltpu
from jax.sharding import PartitionSpec as P

TILE = 128
HB = 4
BAND = 2 * HB + 1
ROWS = 160
AUX = 2560
HALO = HB * TILE
bf16 = jnp.bfloat16
f32 = jnp.float32
MIB = 1 << 20


def blk_index(y, x, z):
    return ((y % 4) * 4 + x % 4) * 2 + z


PLACES = [(y, x, z) for y in range(4) for x in range(4) for z in range(2)]


def send_y(v, step):
    pairs = [(blk_index(y, x, z), blk_index(y + step, x, z)) for y, x, z in PLACES]
    return lax.ppermute(v, "blk", pairs)


def send_x(v, step):
    pairs = [(blk_index(y, x, z), blk_index(y, x + step, z)) for y, x, z in PLACES]
    return lax.ppermute(v, "blk", pairs)


def send_z(v):
    pairs = [(blk_index(y, x, z), blk_index(y, x, 1 - z)) for y, x, z in PLACES]
    return lax.ppermute(v, "blk", pairs)


def send_core(v):
    return lax.ppermute(v, "grp", [(g, g ^ 1) for g in range(8)])


def send_high(v, step):
    return lax.ppermute(v, "grp", [(g, (g + 2 * step) % 8) for g in range(8)])


def params(mib=28):
    return pltpu.CompilerParams(vmem_limit_bytes=mib * MIB)


def cost():
    return pl.CostEstimate(flops=1000, bytes_accessed=1000, transcendentals=0)


def position():
    group = lax.axis_index("grp").astype(jnp.int32)
    me = lax.axis_index("blk").astype(jnp.int32)
    return group // 2, group % 2, me // 8, (me // 2) % 4, me % 2


ANY = pl.BlockSpec(memory_space=pl.ANY)
VMEM = pl.BlockSpec(memory_space=pltpu.VMEM)
SMEM = pl.BlockSpec(memory_space=pltpu.SMEM)
DMA = pltpu.SemaphoreType.DMA
HALF = ROWS // 2
SHARE = ROWS // 2
WIDE = 4 * ROWS
K2 = AUX // 2
K4 = AUX // 4


def hbm(shape, dtype=bf16):
    return jax.ShapeDtypeStruct(shape, dtype)


def vmem(shape, dtype=bf16):
    return pltpu.VMEM(shape, dtype)


def call(kernel, args, outs, scratch=(), name=None, aliases=None, mib=28):
    return pl.pallas_call(
        kernel,
        in_specs=[spec for _, spec in args],
        out_specs=[VMEM] * len(outs),
        out_shape=list(outs),
        scratch_shapes=list(scratch),
        input_output_aliases=aliases or {},
        compiler_params=params(mib),
        cost_estimate=cost(),
        name=name,
    )(*[a for a, _ in args])


INNER = (2, 3, 4, 5, 6, 7)
EDGE = (0, 1, 8, 9)


def fit_inner_kernel(index, own_in, tiles_in, a, b, own, edge, tiles, weights, own_sem, sems):
    own_copies = [
        pltpu.make_async_copy(
            own_in.at[pl.ds(i * ROWS, ROWS)], own.at[pl.ds(i * ROWS, ROWS)], own_sem.at[i]
        )
        for i in range(2)
    ]
    copies = {}
    for p in INNER + EDGE:
        part = pl.ds(p * 2 * BAND, 2 * BAND)
        copies[p] = pltpu.make_async_copy(tiles_in.at[part], tiles.at[part], sems.at[p])
    copies[INNER[0]].start()
    for c in own_copies:
        c.start()
    for p in (INNER + EDGE)[1:]:
        copies[p].start()
    zero = jnp.zeros((TILE, TILE), bf16)

    def build(p, out):
        out[:TILE, TILE:] = zero
        out[BAND * TILE :, :TILE] = zero
        for q in range(2):
            for o in range(BAND):
                slot = p * 2 * BAND + q * BAND + o
                at = (q + o) * TILE
                out[at : at + TILE, q * TILE : (q + 1) * TILE] = jnp.where(
                    index[1, slot] == 1, tiles[slot], zero
                )

    for p in INNER:
        copies[p].wait()
        if p == INNER[0]:
            for c in own_copies:
                c.wait()
        build(p, weights)
        window = own[:, (2 * p - HB) * TILE : (2 * p + HB + 2) * TILE]
        fitted = jnp.dot(window, weights[...], preferred_element_type=f32).astype(bf16)
        columns = slice(p * 2 * TILE, (p + 1) * 2 * TILE)
        a[:, columns] = fitted[:ROWS]
        b[:, columns] = fitted[ROWS:]
    for n, p in enumerate(EDGE):
        copies[p].wait()
        build(p, edge.at[n])


def fit_edge_kernel(left, right, own, edge, _, __, a, b, ext):
    ext[:, :HALO] = left[...]
    ext[:, HALO : 3 * HALO] = own[:, : 2 * HALO]
    ext[:, 3 * HALO : 5 * HALO] = own[:, AUX - 2 * HALO :]
    ext[:, 5 * HALO :] = right[...]
    for n, p in enumerate(EDGE):
        at = (0, 2, 12, 14)[n] * TILE
        window = ext[:, at : at + (BAND + 1) * TILE]
        fitted = jnp.dot(window, edge[n], preferred_element_type=f32).astype(bf16)
        columns = slice(p * 2 * TILE, (p + 1) * 2 * TILE)
        a[:, columns] = fitted[:ROWS]
        b[:, columns] = fitted[ROWS:]


def fit(index, own, tiles, left, right):
    banded = ((BAND + 1) * TILE, 2 * TILE)
    a, b, own, edge = call(
        fit_inner_kernel,
        [(index, SMEM), (own, ANY), (tiles, ANY)],
        [vmem((ROWS, AUX)), vmem((ROWS, AUX)), vmem((2 * ROWS, AUX)), vmem((4, *banded))],
        [pltpu.VMEM(tiles.shape, bf16), pltpu.VMEM(banded, bf16), DMA((2,)), DMA((10,))],
        name="fit_inner",
        mib=56,
    )
    return call(
        fit_edge_kernel,
        [(v, VMEM) for v in (left, right, own, edge, a, b)],
        [vmem((ROWS, AUX))] * 2,
        [pltpu.VMEM((2 * ROWS, 6 * HALO), bf16)],
        name="fit_edge",
        aliases={4: 0, 5: 1},
    )


def ends_kernel(own, last, first, sems):
    copies = [
        pltpu.make_async_copy(own.at[:, pl.ds(AUX - HALO, HALO)], last, sems.at[0]),
        pltpu.make_async_copy(own.at[:, pl.ds(0, HALO)], first, sems.at[1]),
    ]
    for c in copies:
        c.start()
    for c in copies:
        c.wait()


def ends(own):
    outs = [vmem((2 * ROWS, HALO))] * 2
    return call(ends_kernel, [(own, ANY)], outs, [DMA((2,))], name="ends", mib=60)


def cut(parts, after=(), name=None):
    def kernel(*refs):
        ins, outs, sems = refs[: len(parts)], refs[-1 - len(parts) : -1], refs[-1]
        copies = [
            pltpu.make_async_copy(i.at[pl.ds(r, n)], o, sems.at[j])
            for j, (i, o, (_, r, n)) in enumerate(zip(ins, outs, parts))
        ]
        for c in copies:
            c.start()
        for c in copies:
            c.wait()

    return pl.pallas_call(
        kernel,
        in_specs=[ANY] * (len(parts) + len(after)),
        out_specs=[ANY] * len(parts),
        out_shape=[hbm((n, AUX)) for _, _, n in parts],
        scratch_shapes=[DMA((len(parts),))],
        compiler_params=params(),
        cost_estimate=cost(),
        name=name,
    )(*[p[0] for p in parts], *after)


def arrive(parts, after):
    n = len(parts)
    return pl.pallas_call(
        lambda *refs: None,
        in_specs=[ANY] * (n + len(after)),
        out_specs=[ANY] * n,
        out_shape=[hbm(v.shape, v.dtype) for v in parts],
        input_output_aliases={i: i for i in range(n)},
        compiler_params=params(),
        cost_estimate=cost(),
        name="arrive",
    )(*parts, *after)


def row_copies(moves, out, sems, part):
    columns = pl.ds(pl.multiple_of(part * K4, K4), K4)
    return [
        pltpu.make_async_copy(
            v.at[pl.ds(r, n), columns], out.at[pl.ds(at, n), columns], sems.at[i, part]
        )
        for i, (v, r, n, at) in enumerate(moves)
    ]


def b_moves(parts, at=0):
    moves = []
    for p in parts:
        moves.append((p, 0, p.shape[0], at))
        at += p.shape[0]
    return moves


def products(copies, acat, bcat, wanted, unroll=False):
    for part in range(4):
        for c in copies(part):
            c.start()

    if unroll:
        for c in (c for part in range(4) for c in copies(part)):
            c.wait()
        for a_rows, b_rows, total in wanted:
            total[...] = lax.dot_general(
                acat[a_rows], bcat[b_rows], (((1,), (1,)), ((), ())),
                preferred_element_type=f32,
            )
        return

    @pl.loop(0, 4)
    def _(part):
        for c in copies(part):
            c.wait()
        columns = pl.ds(pl.multiple_of(part * K4, K4), K4)
        for a_rows, b_rows, total in wanted:
            value = lax.dot_general(
                acat[a_rows, columns], bcat[b_rows, columns], (((1,), (1,)), ((), ())),
                preferred_element_type=f32,
            )

            @pl.when(part == 0)
            def _():
                total[...] = value

            @pl.when(part > 0)
            def _():
                total[...] += value


def pair_first_kernel(own, ax, am, *refs):
    b_refs = refs[:4]
    total, bcat, acat, a_sems, b_sems = refs[4:]
    a_moves = [
        (own, 0, ROWS, 0),
        (ax, 0, HALF, ROWS),
        (ax, HALF, HALF, 2 * ROWS),
        (am, 0, HALF, 2 * ROWS + HALF),
        (am, HALF, HALF, ROWS + HALF),
    ]
    rows = slice(0, 3 * ROWS)
    products(
        lambda part: row_copies(a_moves, acat, a_sems, part)
        + row_copies(b_moves(b_refs), bcat, b_sems, part),
        acat, bcat, [(rows, slice(0, WIDE), total.at[rows])],
    )


def pair_first(a_parts, b_parts):
    return call(
        pair_first_kernel,
        [(v, ANY) for v in (*a_parts, *b_parts)],
        [vmem((WIDE, WIDE), f32), vmem((2 * WIDE, AUX)), vmem((WIDE, AUX))],
        [DMA((5, 4)), DMA((4, 4))],
        name="pair_first",
    )


def pair_early_kernel(first_in, bcat_in, acat_in, ad, *refs):
    b_refs = refs[:3]
    first, bcat, acat, keep, send, early, a_sems, b_sems = refs[3:]
    rows = slice(3 * ROWS, WIDE)
    products(
        lambda part: row_copies([(ad, 0, ROWS, 3 * ROWS)], acat, a_sems, part)
        + row_copies(b_moves(b_refs, WIDE), bcat, b_sems, part),
        acat, bcat,
        [
            (rows, slice(0, WIDE), first.at[rows]),
            (slice(0, WIDE), slice(WIDE, 7 * ROWS), early),
        ],
        unroll=True,
    )
    core = position()[1]
    split = 3 * ROWS

    @pl.when(core == 0)
    def _():
        keep[...] = first[...]
        send[:, :split] = early[...].astype(bf16)

    @pl.when(core == 1)
    def _():
        send[...] = first[...].astype(bf16)
        keep[:, :split] = early[...]


def pair_early(first, bcat, acat, ad, b_parts):
    return call(
        pair_early_kernel,
        [(v, VMEM) for v in (first, bcat, acat)] + [(v, ANY) for v in (ad, *b_parts)],
        [
            vmem((WIDE, WIDE), f32),
            vmem((2 * WIDE, AUX)),
            vmem((WIDE, AUX)),
            vmem((WIDE, WIDE), f32),
            vmem((WIDE, WIDE)),
        ],
        [pltpu.VMEM((WIDE, 3 * ROWS), f32), DMA((1, 4)), DMA((3, 4))],
        name="pair_early",
        aliases={0: 0, 1: 1, 2: 2},
    )


def pair_late_kernel(keep_in, send_in, acat, bcat_in, *refs):
    b_refs = refs[:3]
    keep, send, bcat, late, sems = refs[3:]
    products(
        lambda part: row_copies(b_moves(b_refs, 7 * ROWS), bcat, sems, part),
        acat, bcat, [(slice(0, WIDE), slice(7 * ROWS, 8 * ROWS), late)], unroll=True,
    )
    core = position()[1]
    columns = slice(3 * ROWS, WIDE)

    @pl.when(core == 0)
    def _():
        send[:, columns] = late[...].astype(bf16)

    @pl.when(core == 1)
    def _():
        keep[:, columns] = late[...]


def pair_late(keep, send, acat, bcat, b_parts):
    return call(
        pair_late_kernel,
        [(v, VMEM) for v in (keep, send, acat, bcat)] + [(v, ANY) for v in b_parts],
        [vmem((WIDE, WIDE), f32), vmem((WIDE, WIDE)), vmem((2 * WIDE, AUX))],
        [pltpu.VMEM((WIDE, ROWS), f32), DMA((3, 4))],
        name="pair_late",
        aliases={0: 0, 1: 1, 3: 2},
    )


def core_sum_kernel(keep, got, own, s1, s2, s3):
    high = position()[0]
    for step, out in enumerate((own, s1, s2, s3)):
        for wave in range(2):
            at = pl.multiple_of((1 - wave) * 2 * ROWS + ((high + step) % 4) * SHARE, SHARE)
            value = keep[pl.ds(at, SHARE)] + got[pl.ds(at, SHARE)].astype(f32)
            out[wave * SHARE : (wave + 1) * SHARE] = value.astype(out.dtype)


def core_sum(keep, got):
    share = (2 * SHARE, WIDE)
    return call(
        core_sum_kernel,
        [(keep, VMEM), (got, VMEM)],
        [vmem(share, f32)] + [hbm(share)] * 3,
        name="core_sum",
    )


BLOCKS = (((0, 0), (3, 0), (1, 0), (0, 1)), ((3, 1), (2, 0), (1, 1), (2, 1)))


def amplitude_kernel(vir, occ, chosen, own, *refs):
    arrived, outs = refs[:3], refs[3:5]
    high, core, y, x, z = position()
    occ_total = occ[chosen[0]] + occ[chosen[1]]
    lane = lax.broadcasted_iota(jnp.int32, (SHARE, ROWS), 1)
    row = lax.broadcasted_iota(jnp.int32, (SHARE, ROWS), 0)

    def row_energy(shift, second):
        block = vir[pl.ds((y * 4 + (x + shift) % 4) * 2 + z, 1), :]
        own_lane = lane == row + second * SHARE
        return jnp.sum(jnp.where(own_lane, block, 0.0), axis=1, keepdims=True)

    rows = (
        row_energy(
            jnp.where(high == 0, 1, jnp.where(high == 1, 3, 2)),
            jnp.where((high == 0) | (high == 3), 1, 0),
        ),
        row_energy(jnp.where(high < 2, 0, 2 * high - 3), high % 2),
    )
    places = []
    for first, last in zip(*BLOCKS):
        step = jnp.where(core == 0, first[0], last[0])
        away = jnp.where(core == 0, first[1], last[1])
        places.append((((y + step) % 4) * 4 + x) * 2 + jnp.where(away == 1, 1 - z, z))
    columns = jnp.concatenate([vir[pl.ds(at, 1), :] for at in places], axis=1)
    for wave, out in enumerate(outs):
        part = slice(wave * SHARE, (wave + 1) * SHARE)
        total = own[part]
        for r in arrived:
            total = total + r[part].astype(f32)
        denominator = (rows[wave] + columns) - occ_total
        out[...] = (total / denominator).astype(bf16)


def amplitude(vir, occ, chosen, own, arrived):
    return call(
        amplitude_kernel,
        [(vir, VMEM), (occ, SMEM), (chosen, SMEM), (own, VMEM)]
        + [(v, VMEM) for v in arrived],
        [hbm((SHARE, WIDE))] * 2,
        name="amplitude",
    )


def gather_rows(mine, other, tcat):
    high, core = position()[:2]
    for k in range(4):
        rows = pl.ds(pl.multiple_of(((high - k + 4) % 4) * SHARE, SHARE), SHARE)
        for v, of in ((mine[k], core), (other[k], 1 - core)):
            tcat[rows, pl.ds(pl.multiple_of(of * WIDE, WIDE), WIDE)] = v[...]


def product(tcat, bcat, half):
    columns = pl.ds(pl.multiple_of(half * K2, K2), K2)
    return columns, jnp.dot(tcat[...], bcat[:, columns], preferred_element_type=f32)


TCAT = (2 * ROWS, 2 * WIDE)


def density_first_kernel(*refs):
    mine, other, bcat = refs[:4], refs[4:8], refs[8]
    outs, tcat = refs[9:11], refs[11]
    gather_rows(mine, other, tcat)

    @pl.loop(0, 2)
    def _(half):
        columns, value = product(tcat, bcat, half)
        value = value.astype(bf16)
        for i, out in enumerate(outs):
            out[:HALF, columns] = value[i * HALF : (i + 1) * HALF]
            out[HALF:, columns] = value[(i + 2) * HALF : (i + 3) * HALF]


def density_first(mine, other, bcat):
    return call(
        density_first_kernel,
        [(v, VMEM) for v in (*mine, *other, bcat)],
        [hbm((ROWS, AUX))] * 2,
        [pltpu.VMEM(TCAT, bf16)],
        name="density_first",
    )


def density_second_kernel(*refs):
    mine, other, (bcat, got_m, got_x) = refs[:4], refs[4:8], refs[8:11]
    x1, m2, own_rows, tcat = refs[11:]
    gather_rows(mine, other, tcat)
    own_rows[...] = tcat[:ROWS]

    @pl.loop(0, 2)
    def _(half):
        columns, value = product(tcat.at[ROWS:], bcat, half)
        x = value[:HALF] + got_m[HALF:, columns].astype(f32)
        m = value[HALF:] + got_x[HALF:, columns].astype(f32)
        x1[:, columns] = x.astype(bf16)
        m2[:, columns] = m.astype(bf16)


def density_second(mine, other, bcat, from_m, from_x):
    return call(
        density_second_kernel,
        [(v, VMEM) for v in (*mine, *other, bcat, from_m, from_x)],
        [hbm((HALF, AUX))] * 2 + [vmem((ROWS, 2 * WIDE))],
        [pltpu.VMEM(TCAT, bf16)],
        name="density_second",
    )


def density_own_kernel(rows, bcat, got_m, got_x, own):
    @pl.loop(0, 2)
    def _(half):
        columns, value = product(rows, bcat, half)
        own[:HALF, columns] = value[:HALF] + got_x[:HALF, columns].astype(f32)
        own[HALF:, columns] = value[HALF:] + got_m[:HALF, columns].astype(f32)


def density_own(rows, bcat, from_m, from_x):
    return call(
        density_own_kernel,
        [(v, VMEM) for v in (rows, bcat, from_m, from_x)],
        [vmem((ROWS, AUX), f32)],
        name="density_own",
    )[0]


def add_kernel(own, one, two, out):
    out[:HALF] = (own[:HALF] + one[...].astype(f32)).astype(bf16)
    out[HALF:] = (own[HALF:] + two[...].astype(f32)).astype(bf16)


def add(own, one, two):
    return call(
        add_kernel,
        [(own, VMEM), (one, VMEM), (two, VMEM)],
        [hbm((ROWS, AUX))],
        name="add",
    )[0]


def local(integrals, tiles, tile_index, vir_energy, occ_energy, pair_index):
    window = integrals.reshape(2 * ROWS, AUX)
    vir = vir_energy.reshape(-1, ROWS)
    up = [(g, g + 1) for g in range(7)]
    down = [(g + 1, g) for g in range(7)]
    last, first = ends(window)
    left = lax.ppermute(last, "grp", up)
    right = lax.ppermute(first, "grp", down)
    a, b = fit(tile_index.T, window, tiles, left, right)

    with jax.named_scope("first"):
        ax = send_x(a, -1)
        am = send_x(a, 1)
        bo = send_z(b)
        bp = send_y(b, -1)
        bm = send_y(b, 1)
    bo, bp = arrive((bo, bp), (bm, vir))
    with jax.named_scope("second"):
        bom = send_y(bo, 1)
        b2 = send_y(bp, -1)
        bop = send_z(bp)
        ad = send_x(ax, -1)
    early_sums, bcat, acat = pair_first((a, ax, am), (b, bm, bp, bo))
    c1, c2, c3 = cut([(b2, 0, 64), (bom, 64, 48), (bop, 112, 48)], (early_sums,), name="cut_b")
    with jax.named_scope("third"):
        c1 = send_z(c1)
        c2 = send_y(c2, 1)
        c3 = send_y(c3, -1)
    _, bcat, acat, keep, send = pair_early(early_sums, bcat, acat, ad, (bom, b2, bop))
    keep, send, bcat = pair_late(keep, send, acat, bcat, (c1, c2, c3))
    with jax.named_scope("core"):
        own, *s = core_sum(keep, send_core(send))
    with jax.named_scope("shares"):
        arrived = [send_high(s[k - 1], k) for k in (2, 1, 3)]
    mine = amplitude(vir, occ_energy, pair_index, own, arrived)

    def spread(wave):
        with jax.named_scope(f"spread_{wave}"):
            sent = {k: send_high(mine[wave], k) for k in (1, 3, 2)}
            return [mine[wave]] + [sent[k] for k in (1, 2, 3)]

    def other_core(wave, mine):
        with jax.named_scope(f"other_{wave}"):
            return [send_core(v) for v in mine]

    mine0, mine1 = spread(0), spread(1)
    other0 = other_core(0, mine0)
    other1 = other_core(1, mine1)
    x2_d1, m1_d2 = density_first(mine0, other0, bcat)
    with jax.named_scope("out"):
        from_m = send_x(x2_d1, 1)
        from_x = send_x(m1_d2, -1)
    x1, m2, own_rows = density_second(mine1, other1, bcat, from_m, from_x)
    with jax.named_scope("out"):
        got_x1 = send_x(x1, 1)
        got_m2 = send_x(m2, -1)
    own = density_own(own_rows, bcat, from_m, from_x)
    return add(own, got_x1, got_m2)


def solution(mesh):
    in_specs = (P(None, "blk", "grp"), P("grp", None, None), P("grp", None), P(), P(), P())
    return jax.shard_map(
        local, mesh=mesh, in_specs=in_specs, out_specs=P("blk", "grp"), check_vma=False
    )
```

```python
import functools

import jax
import jax.numpy as jnp
from jax import lax
from jax.experimental import pallas as pl
from jax.experimental.pallas import tpu as pltpu
from jax.sharding import PartitionSpec as P

TILE = 128
HB = 4
BAND = 2 * HB + 1
ROWS = 160
AUX = 2560
HALO = HB * TILE
bf16 = jnp.bfloat16
f32 = jnp.float32
MIB = 1 << 20


def blk_index(y, x, z):
    return ((y % 4) * 4 + x % 4) * 2 + z


PLACES = [(y, x, z) for y in range(4) for x in range(4) for z in range(2)]


def send_y(v, step):
    pairs = [(blk_index(y, x, z), blk_index(y + step, x, z)) for y, x, z in PLACES]
    return lax.ppermute(v, "blk", pairs)


def send_x(v, step):
    pairs = [(blk_index(y, x, z), blk_index(y, x + step, z)) for y, x, z in PLACES]
    return lax.ppermute(v, "blk", pairs)


def send_z(v):
    pairs = [(blk_index(y, x, z), blk_index(y, x, 1 - z)) for y, x, z in PLACES]
    return lax.ppermute(v, "blk", pairs)


def send_core(v):
    return lax.ppermute(v, "grp", [(g, g ^ 1) for g in range(8)])


def send_high(v, step):
    return lax.ppermute(v, "grp", [(g, (g + 2 * step) % 8) for g in range(8)])


def params(mib=28):
    return pltpu.CompilerParams(vmem_limit_bytes=mib * MIB)


def cost():
    return pl.CostEstimate(flops=1000, bytes_accessed=1000, transcendentals=0)


def position():
    group = lax.axis_index("grp").astype(jnp.int32)
    me = lax.axis_index("blk").astype(jnp.int32)
    return group // 2, group % 2, me // 8, (me // 2) % 4, me % 2


ANY = pl.BlockSpec(memory_space=pl.ANY)
VMEM = pl.BlockSpec(memory_space=pltpu.VMEM)
SMEM = pl.BlockSpec(memory_space=pltpu.SMEM)
DMA = pltpu.SemaphoreType.DMA
HALF = ROWS // 2
SHARE = ROWS // 2
WIDE = 4 * ROWS
K2 = AUX // 2
K4 = AUX // 4


def hbm(shape, dtype=bf16):
    return jax.ShapeDtypeStruct(shape, dtype)


def vmem(shape, dtype=bf16):
    return pltpu.VMEM(shape, dtype)


def call(kernel, args, outs, scratch=(), name=None, aliases=None, mib=28):
    return pl.pallas_call(
        kernel,
        in_specs=[spec for _, spec in args],
        out_specs=[VMEM] * len(outs),
        out_shape=list(outs),
        scratch_shapes=list(scratch),
        input_output_aliases=aliases or {},
        compiler_params=params(mib),
        cost_estimate=cost(),
        name=name,
    )(*[a for a, _ in args])


INNER = (2, 3, 4, 5, 6, 7)
EDGE = (0, 1, 8, 9)


def fit_inner_kernel(index, own_in, tiles_in, a, b, own, edge, tiles, weights, own_sem, sems):
    own_copies = [
        pltpu.make_async_copy(
            own_in.at[pl.ds(i * ROWS, ROWS)], own.at[pl.ds(i * ROWS, ROWS)], own_sem.at[i]
        )
        for i in range(2)
    ]
    copies = {}
    for p in INNER + EDGE:
        part = pl.ds(p * 2 * BAND, 2 * BAND)
        copies[p] = pltpu.make_async_copy(tiles_in.at[part], tiles.at[part], sems.at[p])
    copies[INNER[0]].start()
    for c in own_copies:
        c.start()
    for p in (INNER + EDGE)[1:]:
        copies[p].start()
    zero = jnp.zeros((TILE, TILE), bf16)

    def build(p, out):
        out[:TILE, TILE:] = zero
        out[BAND * TILE :, :TILE] = zero
        for q in range(2):
            for o in range(BAND):
                slot = p * 2 * BAND + q * BAND + o
                at = (q + o) * TILE
                out[at : at + TILE, q * TILE : (q + 1) * TILE] = jnp.where(
                    index[1, slot] == 1, tiles[slot], zero
                )

    for p in INNER:
        copies[p].wait()
        if p == INNER[0]:
            for c in own_copies:
                c.wait()
        build(p, weights)
        window = own[:, (2 * p - HB) * TILE : (2 * p + HB + 2) * TILE]
        fitted = jnp.dot(window, weights[...], preferred_element_type=f32).astype(bf16)
        columns = slice(p * 2 * TILE, (p + 1) * 2 * TILE)
        a[:, columns] = fitted[:ROWS]
        b[:, columns] = fitted[ROWS:]
    for n, p in enumerate(EDGE):
        copies[p].wait()
        build(p, edge.at[n])


def fit_edge_kernel(left, right, own, edge, _, __, a, b, ext):
    ext[:, :HALO] = left[...]
    ext[:, HALO : 3 * HALO] = own[:, : 2 * HALO]
    ext[:, 3 * HALO : 5 * HALO] = own[:, AUX - 2 * HALO :]
    ext[:, 5 * HALO :] = right[...]
    for n, p in enumerate(EDGE):
        at = (0, 2, 12, 14)[n] * TILE
        window = ext[:, at : at + (BAND + 1) * TILE]
        fitted = jnp.dot(window, edge[n], preferred_element_type=f32).astype(bf16)
        columns = slice(p * 2 * TILE, (p + 1) * 2 * TILE)
        a[:, columns] = fitted[:ROWS]
        b[:, columns] = fitted[ROWS:]


def fit(index, own, tiles, left, right):
    banded = ((BAND + 1) * TILE, 2 * TILE)
    a, b, own, edge = call(
        fit_inner_kernel,
        [(index, SMEM), (own, ANY), (tiles, ANY)],
        [vmem((ROWS, AUX)), vmem((ROWS, AUX)), vmem((2 * ROWS, AUX)), vmem((4, *banded))],
        [pltpu.VMEM(tiles.shape, bf16), pltpu.VMEM(banded, bf16), DMA((2,)), DMA((10,))],
        name="fit_inner",
        mib=56,
    )
    return call(
        fit_edge_kernel,
        [(v, VMEM) for v in (left, right, own, edge, a, b)],
        [vmem((ROWS, AUX))] * 2,
        [pltpu.VMEM((2 * ROWS, 6 * HALO), bf16)],
        name="fit_edge",
        aliases={4: 0, 5: 1},
    )


def ends_kernel(own, last, first, sems):
    copies = [
        pltpu.make_async_copy(own.at[:, pl.ds(AUX - HALO, HALO)], last, sems.at[0]),
        pltpu.make_async_copy(own.at[:, pl.ds(0, HALO)], first, sems.at[1]),
    ]
    for c in copies:
        c.start()
    for c in copies:
        c.wait()


def ends(own):
    outs = [vmem((2 * ROWS, HALO))] * 2
    return call(ends_kernel, [(own, ANY)], outs, [DMA((2,))], name="ends", mib=60)


def cut(parts, after=(), name=None):
    def kernel(*refs):
        for i, o, (_, r, n) in zip(refs, refs[len(parts) + len(after) :], parts):
            o[...] = i[r : r + n]

    return call(
        kernel,
        [(p[0], VMEM) for p in parts] + [(v, ANY) for v in after],
        [hbm((n, AUX)) for _, _, n in parts],
        name=name,
    )


def arrive(parts, after):
    n = len(parts)
    return pl.pallas_call(
        lambda *refs: None,
        in_specs=[ANY] * (n + len(after)),
        out_specs=[ANY] * n,
        out_shape=[hbm(v.shape, v.dtype) for v in parts],
        input_output_aliases={i: i for i in range(n)},
        compiler_params=params(),
        cost_estimate=cost(),
        name="arrive",
    )(*parts, *after)


def row_copies(moves, out, sems, part):
    columns = pl.ds(pl.multiple_of(part * K4, K4), K4)
    return [
        pltpu.make_async_copy(
            v.at[pl.ds(r, n), columns], out.at[pl.ds(at, n), columns], sems.at[i, part]
        )
        for i, (v, r, n, at) in enumerate(moves)
    ]


def b_moves(parts, at=0):
    moves = []
    for p in parts:
        moves.append((p, 0, p.shape[0], at))
        at += p.shape[0]
    return moves


def products(copies, acat, bcat, wanted, unroll=False):
    for part in range(4):
        for c in copies(part):
            c.start()

    if unroll:
        for c in (c for part in range(4) for c in copies(part)):
            c.wait()
        for a_rows, b_rows, total in wanted:
            total[...] = lax.dot_general(
                acat[a_rows], bcat[b_rows], (((1,), (1,)), ((), ())),
                preferred_element_type=f32,
            )
        return

    @pl.loop(0, 4)
    def _(part):
        for c in copies(part):
            c.wait()
        columns = pl.ds(pl.multiple_of(part * K4, K4), K4)
        for a_rows, b_rows, total in wanted:
            value = lax.dot_general(
                acat[a_rows, columns], bcat[b_rows, columns], (((1,), (1,)), ((), ())),
                preferred_element_type=f32,
            )

            @pl.when(part == 0)
            def _():
                total[...] = value

            @pl.when(part > 0)
            def _():
                total[...] += value


def pair_first_kernel(own, ax, am, *refs):
    b_refs = refs[:4]
    total, bcat, acat, a_sems, b_sems = refs[4:]
    a_moves = [
        (own, 0, ROWS, 0),
        (ax, 0, HALF, ROWS),
        (ax, HALF, HALF, 2 * ROWS),
        (am, 0, HALF, 2 * ROWS + HALF),
        (am, HALF, HALF, ROWS + HALF),
    ]
    rows = slice(0, 3 * ROWS)
    products(
        lambda part: row_copies(a_moves, acat, a_sems, part)
        + row_copies(b_moves(b_refs), bcat, b_sems, part),
        acat, bcat, [(rows, slice(0, WIDE), total.at[rows])],
    )


def pair_first(a_parts, b_parts):
    return call(
        pair_first_kernel,
        [(v, ANY) for v in (*a_parts, *b_parts)],
        [vmem((WIDE, WIDE), f32), vmem((2 * WIDE, AUX)), vmem((WIDE, AUX))],
        [DMA((5, 4)), DMA((4, 4))],
        name="pair_first",
    )


def pair_early_kernel(first_in, bcat_in, acat_in, ad, *refs):
    b_refs = refs[:3]
    first, bcat, acat, keep, send, early, a_sems, b_sems = refs[3:]
    rows = slice(3 * ROWS, WIDE)
    products(
        lambda part: row_copies([(ad, 0, ROWS, 3 * ROWS)], acat, a_sems, part)
        + row_copies(b_moves(b_refs, WIDE), bcat, b_sems, part),
        acat, bcat,
        [
            (rows, slice(0, WIDE), first.at[rows]),
            (slice(0, WIDE), slice(WIDE, 7 * ROWS), early),
        ],
        unroll=True,
    )
    core = position()[1]
    split = 3 * ROWS

    @pl.when(core == 0)
    def _():
        keep[...] = first[...]
        send[:, :split] = early[...].astype(bf16)

    @pl.when(core == 1)
    def _():
        send[...] = first[...].astype(bf16)
        keep[:, :split] = early[...]


def pair_early(first, bcat, acat, ad, b_parts):
    return call(
        pair_early_kernel,
        [(v, VMEM) for v in (first, bcat, acat)] + [(v, ANY) for v in (ad, *b_parts)],
        [
            vmem((WIDE, WIDE), f32),
            vmem((2 * WIDE, AUX)),
            vmem((WIDE, AUX)),
            vmem((WIDE, WIDE), f32),
            vmem((WIDE, WIDE)),
        ],
        [pltpu.VMEM((WIDE, 3 * ROWS), f32), DMA((1, 4)), DMA((3, 4))],
        name="pair_early",
        aliases={0: 0, 1: 1, 2: 2},
    )


def pair_late_kernel(keep_in, send_in, acat, bcat_in, *refs):
    b_refs = refs[:3]
    keep, send, bcat = refs[3:]
    at = 7 * ROWS
    for v in b_refs:
        bcat[at : at + v.shape[0]] = v[...]
        at += v.shape[0]
    late = lax.dot_general(
        acat[...], bcat[7 * ROWS :], (((1,), (1,)), ((), ())), preferred_element_type=f32
    )
    core = position()[1]
    columns = slice(3 * ROWS, WIDE)

    @pl.when(core == 0)
    def _():
        send[:, columns] = late.astype(bf16)

    @pl.when(core == 1)
    def _():
        keep[:, columns] = late


def pair_late(keep, send, acat, bcat, b_parts):
    return call(
        pair_late_kernel,
        [(v, VMEM) for v in (keep, send, acat, bcat, *b_parts)],
        [vmem((WIDE, WIDE), f32), vmem((WIDE, WIDE)), vmem((2 * WIDE, AUX))],
        name="pair_late",
        aliases={0: 0, 1: 1, 3: 2},
    )


def core_sum_kernel(keep, got, own, s1, s2, s3):
    high = position()[0]
    for step, out in enumerate((own, s1, s2, s3)):
        for wave in range(2):
            at = pl.multiple_of((1 - wave) * 2 * ROWS + ((high + step) % 4) * SHARE, SHARE)
            value = keep[pl.ds(at, SHARE)] + got[pl.ds(at, SHARE)].astype(f32)
            out[wave * SHARE : (wave + 1) * SHARE] = value.astype(out.dtype)


def core_sum(keep, got):
    share = (2 * SHARE, WIDE)
    return call(
        core_sum_kernel,
        [(keep, VMEM), (got, VMEM)],
        [vmem(share, f32)] + [hbm(share)] * 3,
        name="core_sum",
    )


BLOCKS = (((0, 0), (3, 0), (1, 0), (0, 1)), ((3, 1), (2, 0), (1, 1), (2, 1)))


def amplitude_kernel(vir, occ, chosen, own, *refs):
    arrived, outs = refs[:3], refs[3:5]
    high, core, y, x, z = position()
    occ_total = occ[chosen[0]] + occ[chosen[1]]
    lane = lax.broadcasted_iota(jnp.int32, (SHARE, ROWS), 1)
    row = lax.broadcasted_iota(jnp.int32, (SHARE, ROWS), 0)

    def row_energy(shift, second):
        block = vir[pl.ds((y * 4 + (x + shift) % 4) * 2 + z, 1), :]
        own_lane = lane == row + second * SHARE
        return jnp.sum(jnp.where(own_lane, block, 0.0), axis=1, keepdims=True)

    rows = (
        row_energy(
            jnp.where(high == 0, 1, jnp.where(high == 1, 3, 2)),
            jnp.where((high == 0) | (high == 3), 1, 0),
        ),
        row_energy(jnp.where(high < 2, 0, 2 * high - 3), high % 2),
    )
    places = []
    for first, last in zip(*BLOCKS):
        step = jnp.where(core == 0, first[0], last[0])
        away = jnp.where(core == 0, first[1], last[1])
        places.append((((y + step) % 4) * 4 + x) * 2 + jnp.where(away == 1, 1 - z, z))
    columns = jnp.concatenate([vir[pl.ds(at, 1), :] for at in places], axis=1)
    for wave, out in enumerate(outs):
        part = slice(wave * SHARE, (wave + 1) * SHARE)
        total = own[part]
        for r in arrived:
            total = total + r[part].astype(f32)
        denominator = (rows[wave] + columns) - occ_total
        out[...] = (total / denominator).astype(bf16)


def amplitude(vir, occ, chosen, own, arrived):
    return call(
        amplitude_kernel,
        [(vir, VMEM), (occ, SMEM), (chosen, SMEM), (own, VMEM)]
        + [(v, VMEM) for v in arrived],
        [hbm((SHARE, WIDE))] * 2,
        name="amplitude",
    )


def gather_rows(mine, other, tcat):
    high, core = position()[:2]
    for k in range(4):
        rows = pl.ds(pl.multiple_of(((high - k + 4) % 4) * SHARE, SHARE), SHARE)
        for v, of in ((mine[k], core), (other[k], 1 - core)):
            tcat[rows, pl.ds(pl.multiple_of(of * WIDE, WIDE), WIDE)] = v[...]


def product(tcat, bcat, half):
    columns = pl.ds(pl.multiple_of(half * K2, K2), K2)
    return columns, jnp.dot(tcat[...], bcat[:, columns], preferred_element_type=f32)


TCAT = (2 * ROWS, 2 * WIDE)


def density_first_kernel(*refs):
    mine, other, bcat = refs[:4], refs[4:8], refs[8]
    outs, tcat = refs[9:11], refs[11]
    gather_rows(mine, other, tcat)

    @pl.loop(0, 2)
    def _(half):
        columns, value = product(tcat, bcat, half)
        value = value.astype(bf16)
        for i, out in enumerate(outs):
            out[:HALF, columns] = value[i * HALF : (i + 1) * HALF]
            out[HALF:, columns] = value[(i + 2) * HALF : (i + 3) * HALF]


def density_first(mine, other, bcat):
    return call(
        density_first_kernel,
        [(v, VMEM) for v in (*mine, *other, bcat)],
        [hbm((ROWS, AUX))] * 2,
        [pltpu.VMEM(TCAT, bf16)],
        name="density_first",
    )


def density_second_kernel(*refs):
    mine, other, (bcat, got_m, got_x) = refs[:4], refs[4:8], refs[8:11]
    x1, m2, own_rows, tcat = refs[11:]
    gather_rows(mine, other, tcat)
    own_rows[...] = tcat[:ROWS]

    @pl.loop(0, 2)
    def _(half):
        columns, value = product(tcat.at[ROWS:], bcat, half)
        x = value[:HALF] + got_m[HALF:, columns].astype(f32)
        m = value[HALF:] + got_x[HALF:, columns].astype(f32)
        x1[:, columns] = x.astype(bf16)
        m2[:, columns] = m.astype(bf16)


def density_second(mine, other, bcat, from_m, from_x):
    return call(
        density_second_kernel,
        [(v, VMEM) for v in (*mine, *other, bcat, from_m, from_x)],
        [hbm((HALF, AUX))] * 2 + [vmem((ROWS, 2 * WIDE))],
        [pltpu.VMEM(TCAT, bf16)],
        name="density_second",
    )


def density_own_kernel(rows, bcat, got_m, got_x, own):
    @pl.loop(0, 2)
    def _(half):
        columns, value = product(rows, bcat, half)
        own[:HALF, columns] = value[:HALF] + got_x[:HALF, columns].astype(f32)
        own[HALF:, columns] = value[HALF:] + got_m[:HALF, columns].astype(f32)


def density_own(rows, bcat, from_m, from_x):
    return call(
        density_own_kernel,
        [(v, VMEM) for v in (rows, bcat, from_m, from_x)],
        [vmem((ROWS, AUX), f32)],
        name="density_own",
    )[0]


def add_kernel(own, one, two, out):
    out[:HALF] = (own[:HALF] + one[...].astype(f32)).astype(bf16)
    out[HALF:] = (own[HALF:] + two[...].astype(f32)).astype(bf16)


def add(own, one, two):
    return call(
        add_kernel,
        [(own, VMEM), (one, VMEM), (two, VMEM)],
        [hbm((ROWS, AUX))],
        name="add",
    )[0]


def local(integrals, tiles, tile_index, vir_energy, occ_energy, pair_index):
    window = integrals.reshape(2 * ROWS, AUX)
    vir = vir_energy.reshape(-1, ROWS)
    up = [(g, g + 1) for g in range(7)]
    down = [(g + 1, g) for g in range(7)]
    last, first = ends(window)
    left = lax.ppermute(last, "grp", up)
    right = lax.ppermute(first, "grp", down)
    a, b = fit(tile_index.T, window, tiles, left, right)

    with jax.named_scope("first"):
        ax = send_x(a, -1)
        am = send_x(a, 1)
        bo = send_z(b)
        bp = send_y(b, -1)
        bm = send_y(b, 1)
    bo, bp = arrive((bo, bp), (bm, vir))
    with jax.named_scope("second"):
        bom = send_y(bo, 1)
        b2 = send_y(bp, -1)
        bop = send_z(bp)
        ad = send_x(ax, -1)
    early_sums, bcat, acat = pair_first((a, ax, am), (b, bm, bp, bo))
    c1, c2, c3 = cut([(b2, 0, 64), (bom, 64, 48), (bop, 112, 48)], (early_sums,), name="cut_b")
    with jax.named_scope("third"):
        c1 = send_z(c1)
        c2 = send_y(c2, 1)
        c3 = send_y(c3, -1)
    _, bcat, acat, keep, send = pair_early(early_sums, bcat, acat, ad, (bom, b2, bop))
    keep, send, bcat = pair_late(keep, send, acat, bcat, (c1, c2, c3))
    with jax.named_scope("core"):
        own, *s = core_sum(keep, send_core(send))
    with jax.named_scope("shares"):
        arrived = [send_high(s[k - 1], k) for k in (2, 1, 3)]
    mine = amplitude(vir, occ_energy, pair_index, own, arrived)

    def spread(wave):
        with jax.named_scope(f"spread_{wave}"):
            sent = {k: send_high(mine[wave], k) for k in (1, 3, 2)}
            return [mine[wave]] + [sent[k] for k in (1, 2, 3)]

    def other_core(wave, mine):
        with jax.named_scope(f"other_{wave}"):
            return [send_core(v) for v in mine]

    mine0, mine1 = spread(0), spread(1)
    other0 = other_core(0, mine0)
    other1 = other_core(1, mine1)
    x2_d1, m1_d2 = density_first(mine0, other0, bcat)
    with jax.named_scope("out"):
        from_m = send_x(x2_d1, 1)
        from_x = send_x(m1_d2, -1)
    x1, m2, own_rows = density_second(mine1, other1, bcat, from_m, from_x)
    with jax.named_scope("out"):
        got_x1 = send_x(x1, 1)
        got_m2 = send_x(m2, -1)
    own = density_own(own_rows, bcat, from_m, from_x)
    return add(own, got_x1, got_m2)


def solution(mesh):
    in_specs = (P(None, "blk", "grp"), P("grp", None, None), P("grp", None), P(), P(), P())
    return jax.shard_map(
        local, mesh=mesh, in_specs=in_specs, out_specs=P("blk", "grp"), check_vma=False
    )
```

```python
import functools

import jax
import jax.numpy as jnp
from jax import lax
from jax.experimental import pallas as pl
from jax.experimental.pallas import tpu as pltpu
from jax.sharding import PartitionSpec as P

TILE = 128
HB = 4
BAND = 2 * HB + 1
ROWS = 160
AUX = 2560
HALO = HB * TILE
bf16 = jnp.bfloat16
f32 = jnp.float32
MIB = 1 << 20


def blk_index(y, x, z):
    return ((y % 4) * 4 + x % 4) * 2 + z


PLACES = [(y, x, z) for y in range(4) for x in range(4) for z in range(2)]


def send_y(v, step):
    pairs = [(blk_index(y, x, z), blk_index(y + step, x, z)) for y, x, z in PLACES]
    return lax.ppermute(v, "blk", pairs)


def send_x(v, step):
    pairs = [(blk_index(y, x, z), blk_index(y, x + step, z)) for y, x, z in PLACES]
    return lax.ppermute(v, "blk", pairs)


def send_z(v):
    pairs = [(blk_index(y, x, z), blk_index(y, x, 1 - z)) for y, x, z in PLACES]
    return lax.ppermute(v, "blk", pairs)


def send_core(v):
    return lax.ppermute(v, "grp", [(g, g ^ 1) for g in range(8)])


def send_high(v, step):
    return lax.ppermute(v, "grp", [(g, (g + 2 * step) % 8) for g in range(8)])


def params(mib=28):
    return pltpu.CompilerParams(vmem_limit_bytes=mib * MIB)


def cost():
    return pl.CostEstimate(flops=1000, bytes_accessed=1000, transcendentals=0)


def position():
    group = lax.axis_index("grp").astype(jnp.int32)
    me = lax.axis_index("blk").astype(jnp.int32)
    return group // 2, group % 2, me // 8, (me // 2) % 4, me % 2


ANY = pl.BlockSpec(memory_space=pl.ANY)
VMEM = pl.BlockSpec(memory_space=pltpu.VMEM)
SMEM = pl.BlockSpec(memory_space=pltpu.SMEM)
DMA = pltpu.SemaphoreType.DMA
HALF = ROWS // 2
SHARE = ROWS // 2
WIDE = 4 * ROWS
K2 = AUX // 2
K4 = AUX // 4


def hbm(shape, dtype=bf16):
    return jax.ShapeDtypeStruct(shape, dtype)


def vmem(shape, dtype=bf16):
    return pltpu.VMEM(shape, dtype)


def call(kernel, args, outs, scratch=(), name=None, aliases=None, mib=28):
    return pl.pallas_call(
        kernel,
        in_specs=[spec for _, spec in args],
        out_specs=[VMEM] * len(outs),
        out_shape=list(outs),
        scratch_shapes=list(scratch),
        input_output_aliases=aliases or {},
        compiler_params=params(mib),
        cost_estimate=cost(),
        name=name,
    )(*[a for a, _ in args])


INNER = (2, 3, 4, 5, 6, 7)
EDGE = (0, 1, 8, 9)


def fit_inner_kernel(index, own_in, tiles_in, a, b, own, edge, tiles, weights, own_sem, sems):
    own_copies = [
        pltpu.make_async_copy(
            own_in.at[pl.ds(i * ROWS, ROWS)], own.at[pl.ds(i * ROWS, ROWS)], own_sem.at[i]
        )
        for i in range(2)
    ]
    copies = {}
    for p in INNER + EDGE:
        part = pl.ds(p * 2 * BAND, 2 * BAND)
        copies[p] = pltpu.make_async_copy(tiles_in.at[part], tiles.at[part], sems.at[p])
    copies[INNER[0]].start()
    for c in own_copies:
        c.start()
    for p in (INNER + EDGE)[1:]:
        copies[p].start()
    zero = jnp.zeros((TILE, TILE), bf16)

    def build(p, out):
        out[:TILE, TILE:] = zero
        out[BAND * TILE :, :TILE] = zero
        for q in range(2):
            for o in range(BAND):
                slot = p * 2 * BAND + q * BAND + o
                at = (q + o) * TILE
                out[at : at + TILE, q * TILE : (q + 1) * TILE] = jnp.where(
                    index[1, slot] == 1, tiles[slot], zero
                )

    for p in INNER:
        copies[p].wait()
        if p == INNER[0]:
            for c in own_copies:
                c.wait()
        build(p, weights)
        window = own[:, (2 * p - HB) * TILE : (2 * p + HB + 2) * TILE]
        fitted = jnp.dot(window, weights[...], preferred_element_type=f32).astype(bf16)
        columns = slice(p * 2 * TILE, (p + 1) * 2 * TILE)
        a[:, columns] = fitted[:ROWS]
        b[:, columns] = fitted[ROWS:]
    for n, p in enumerate(EDGE):
        copies[p].wait()
        build(p, edge.at[n])


def fit_edge_kernel(left, right, own, edge, _, __, a, b, ext):
    ext[:, :HALO] = left[...]
    ext[:, HALO : 3 * HALO] = own[:, : 2 * HALO]
    ext[:, 3 * HALO : 5 * HALO] = own[:, AUX - 2 * HALO :]
    ext[:, 5 * HALO :] = right[...]
    for n, p in enumerate(EDGE):
        at = (0, 2, 12, 14)[n] * TILE
        window = ext[:, at : at + (BAND + 1) * TILE]
        fitted = jnp.dot(window, edge[n], preferred_element_type=f32).astype(bf16)
        columns = slice(p * 2 * TILE, (p + 1) * 2 * TILE)
        a[:, columns] = fitted[:ROWS]
        b[:, columns] = fitted[ROWS:]


def fit(index, own, tiles, left, right):
    banded = ((BAND + 1) * TILE, 2 * TILE)
    a, b, own, edge = call(
        fit_inner_kernel,
        [(index, SMEM), (own, ANY), (tiles, ANY)],
        [vmem((ROWS, AUX)), vmem((ROWS, AUX)), vmem((2 * ROWS, AUX)), vmem((4, *banded))],
        [pltpu.VMEM(tiles.shape, bf16), pltpu.VMEM(banded, bf16), DMA((2,)), DMA((10,))],
        name="fit_inner",
        mib=56,
    )
    return call(
        fit_edge_kernel,
        [(v, VMEM) for v in (left, right, own, edge, a, b)],
        [vmem((ROWS, AUX))] * 2,
        [pltpu.VMEM((2 * ROWS, 6 * HALO), bf16)],
        name="fit_edge",
        aliases={4: 0, 5: 1},
    )


def ends_kernel(own, last, first, sems):
    copies = [
        pltpu.make_async_copy(own.at[:, pl.ds(AUX - HALO, HALO)], last, sems.at[0]),
        pltpu.make_async_copy(own.at[:, pl.ds(0, HALO)], first, sems.at[1]),
    ]
    for c in copies:
        c.start()
    for c in copies:
        c.wait()


def ends(own):
    outs = [vmem((2 * ROWS, HALO))] * 2
    return call(ends_kernel, [(own, ANY)], outs, [DMA((2,))], name="ends", mib=60)


def cut(parts, after=(), name=None):
    def kernel(*refs):
        for i, o, (_, r, n) in zip(refs, refs[len(parts) + len(after) :], parts):
            o[...] = i[r : r + n]

    return call(
        kernel,
        [(p[0], VMEM) for p in parts] + [(v, ANY) for v in after],
        [hbm((n, AUX)) for _, _, n in parts],
        name=name,
    )


def arrive(parts, after):
    n = len(parts)
    return pl.pallas_call(
        lambda *refs: None,
        in_specs=[ANY] * (n + len(after)),
        out_specs=[ANY] * n,
        out_shape=[hbm(v.shape, v.dtype) for v in parts],
        input_output_aliases={i: i for i in range(n)},
        compiler_params=params(),
        cost_estimate=cost(),
        name="arrive",
    )(*parts, *after)


def row_copies(moves, out, sems, part):
    columns = pl.ds(pl.multiple_of(part * K4, K4), K4)
    return [
        pltpu.make_async_copy(
            v.at[pl.ds(r, n), columns], out.at[pl.ds(at, n), columns], sems.at[i, part]
        )
        for i, (v, r, n, at) in enumerate(moves)
    ]


def b_moves(parts, at=0):
    moves = []
    for p in parts:
        moves.append((p, 0, p.shape[0], at))
        at += p.shape[0]
    return moves


def products(copies, acat, bcat, wanted, unroll=False):
    for part in range(4):
        for c in copies(part):
            c.start()

    if unroll:
        for c in (c for part in range(4) for c in copies(part)):
            c.wait()
        for a_rows, b_rows, total in wanted:
            total[...] = lax.dot_general(
                acat[a_rows], bcat[b_rows], (((1,), (1,)), ((), ())),
                preferred_element_type=f32,
            )
        return

    @pl.loop(0, 4)
    def _(part):
        for c in copies(part):
            c.wait()
        columns = pl.ds(pl.multiple_of(part * K4, K4), K4)
        for a_rows, b_rows, total in wanted:
            value = lax.dot_general(
                acat[a_rows, columns], bcat[b_rows, columns], (((1,), (1,)), ((), ())),
                preferred_element_type=f32,
            )

            @pl.when(part == 0)
            def _():
                total[...] = value

            @pl.when(part > 0)
            def _():
                total[...] += value


def pair_first_kernel(own, ax, am, *refs):
    b_refs = refs[:4]
    total, bcat, acat, a_sems, b_sems = refs[4:]
    a_moves = [
        (own, 0, ROWS, 0),
        (ax, 0, HALF, ROWS),
        (ax, HALF, HALF, 2 * ROWS),
        (am, 0, HALF, 2 * ROWS + HALF),
        (am, HALF, HALF, ROWS + HALF),
    ]
    rows = slice(0, 3 * ROWS)
    products(
        lambda part: row_copies(a_moves, acat, a_sems, part)
        + row_copies(b_moves(b_refs), bcat, b_sems, part),
        acat, bcat, [(rows, slice(0, WIDE), total.at[rows])],
    )


def pair_first(a_parts, b_parts):
    return call(
        pair_first_kernel,
        [(v, ANY) for v in (*a_parts, *b_parts)],
        [vmem((WIDE, WIDE), f32), vmem((2 * WIDE, AUX)), vmem((WIDE, AUX))],
        [DMA((5, 4)), DMA((4, 4))],
        name="pair_first",
    )


def pair_early_kernel(first_in, bcat_in, acat_in, ad, *refs):
    b_refs = refs[:3]
    first, bcat, acat, keep, send, early, a_sems, b_sems = refs[3:]
    rows = slice(3 * ROWS, WIDE)
    products(
        lambda part: row_copies([(ad, 0, ROWS, 3 * ROWS)], acat, a_sems, part)
        + row_copies(b_moves(b_refs, WIDE), bcat, b_sems, part),
        acat, bcat,
        [
            (rows, slice(0, WIDE), first.at[rows]),
            (slice(0, WIDE), slice(WIDE, 7 * ROWS), early),
        ],
        unroll=True,
    )
    core = position()[1]
    split = 3 * ROWS

    @pl.when(core == 0)
    def _():
        keep[...] = first[...]
        send[:, :split] = early[...].astype(bf16)

    @pl.when(core == 1)
    def _():
        send[...] = first[...].astype(bf16)
        keep[:, :split] = early[...]


def pair_early(first, bcat, acat, ad, b_parts):
    return call(
        pair_early_kernel,
        [(v, VMEM) for v in (first, bcat, acat)] + [(v, ANY) for v in (ad, *b_parts)],
        [
            vmem((WIDE, WIDE), f32),
            vmem((2 * WIDE, AUX)),
            vmem((WIDE, AUX)),
            vmem((WIDE, WIDE), f32),
            vmem((WIDE, WIDE)),
        ],
        [pltpu.VMEM((WIDE, 3 * ROWS), f32), DMA((1, 4)), DMA((3, 4))],
        name="pair_early",
        aliases={0: 0, 1: 1, 2: 2},
    )


def pair_late_kernel(keep_in, send_in, acat, bcat_in, *refs):
    b_refs = refs[:3]
    keep, send, bcat = refs[3:]
    at = 7 * ROWS
    for v in b_refs:
        bcat[at : at + v.shape[0]] = v[...]
        at += v.shape[0]
    late = lax.dot_general(
        acat[...], bcat[7 * ROWS :], (((1,), (1,)), ((), ())), preferred_element_type=f32
    )
    core = position()[1]
    columns = slice(3 * ROWS, WIDE)

    @pl.when(core == 0)
    def _():
        send[:, columns] = late.astype(bf16)

    @pl.when(core == 1)
    def _():
        keep[:, columns] = late


def pair_late(keep, send, acat, bcat, b_parts):
    return call(
        pair_late_kernel,
        [(v, VMEM) for v in (keep, send, acat, bcat, *b_parts)],
        [vmem((WIDE, WIDE), f32), vmem((WIDE, WIDE)), vmem((2 * WIDE, AUX))],
        name="pair_late",
        aliases={0: 0, 1: 1, 3: 2},
    )


def core_sum_kernel(keep, got, own, s1, s2, s3):
    high = position()[0]
    for step, out in enumerate((own, s1, s2, s3)):
        for wave in range(2):
            at = pl.multiple_of((1 - wave) * 2 * ROWS + ((high + step) % 4) * SHARE, SHARE)
            value = keep[pl.ds(at, SHARE)] + got[pl.ds(at, SHARE)].astype(f32)
            out[wave * SHARE : (wave + 1) * SHARE] = value.astype(out.dtype)


def core_sum(keep, got):
    share = (2 * SHARE, WIDE)
    return call(
        core_sum_kernel,
        [(keep, VMEM), (got, VMEM)],
        [vmem(share, f32)] + [hbm(share)] * 3,
        name="core_sum",
    )


BLOCKS = (((0, 0), (3, 0), (1, 0), (0, 1)), ((3, 1), (2, 0), (1, 1), (2, 1)))


def amplitude_kernel(vir, occ, chosen, own, *refs):
    arrived, outs = refs[:3], refs[3:5]
    high, core, y, x, z = position()
    occ_total = occ[chosen[0]] + occ[chosen[1]]
    lane = lax.broadcasted_iota(jnp.int32, (SHARE, ROWS), 1)
    row = lax.broadcasted_iota(jnp.int32, (SHARE, ROWS), 0)

    def row_energy(shift, second):
        block = vir[pl.ds((y * 4 + (x + shift) % 4) * 2 + z, 1), :]
        own_lane = lane == row + second * SHARE
        return jnp.sum(jnp.where(own_lane, block, 0.0), axis=1, keepdims=True)

    rows = (
        row_energy(
            jnp.where(high == 0, 1, jnp.where(high == 1, 3, 2)),
            jnp.where((high == 0) | (high == 3), 1, 0),
        ),
        row_energy(jnp.where(high < 2, 0, 2 * high - 3), high % 2),
    )
    places = []
    for first, last in zip(*BLOCKS):
        step = jnp.where(core == 0, first[0], last[0])
        away = jnp.where(core == 0, first[1], last[1])
        places.append((((y + step) % 4) * 4 + x) * 2 + jnp.where(away == 1, 1 - z, z))
    columns = jnp.concatenate([vir[pl.ds(at, 1), :] for at in places], axis=1)
    for wave, out in enumerate(outs):
        part = slice(wave * SHARE, (wave + 1) * SHARE)
        total = own[part]
        for r in arrived:
            total = total + r[part].astype(f32)
        denominator = (rows[wave] + columns) - occ_total
        out[...] = (total / denominator).astype(bf16)


def amplitude(vir, occ, chosen, own, arrived):
    return call(
        amplitude_kernel,
        [(vir, VMEM), (occ, SMEM), (chosen, SMEM), (own, VMEM)]
        + [(v, VMEM) for v in arrived],
        [hbm((SHARE, WIDE))] * 2,
        name="amplitude",
    )


def gather_rows(mine, other, tcat):
    high, core = position()[:2]
    for k in range(4):
        rows = pl.ds(pl.multiple_of(((high - k + 4) % 4) * SHARE, SHARE), SHARE)
        for v, of in ((mine[k], core), (other[k], 1 - core)):
            tcat[rows, pl.ds(pl.multiple_of(of * WIDE, WIDE), WIDE)] = v[...]


def product(tcat, bcat, half):
    columns = pl.ds(pl.multiple_of(half * K2, K2), K2)
    return columns, jnp.dot(tcat[...], bcat[:, columns], preferred_element_type=f32)


TCAT = (2 * ROWS, 2 * WIDE)


def density_first_kernel(*refs):
    mine, other, bcat = refs[:4], refs[4:8], refs[8]
    outs, tcat = refs[9:11], refs[11]
    gather_rows(mine, other, tcat)

    @pl.loop(0, 2)
    def _(half):
        columns, value = product(tcat, bcat, half)
        value = value.astype(bf16)
        for i, out in enumerate(outs):
            out[:HALF, columns] = value[i * HALF : (i + 1) * HALF]
            out[HALF:, columns] = value[(i + 2) * HALF : (i + 3) * HALF]


def density_first(mine, other, bcat):
    return call(
        density_first_kernel,
        [(v, VMEM) for v in (*mine, *other, bcat)],
        [hbm((ROWS, AUX))] * 2,
        [pltpu.VMEM(TCAT, bf16)],
        name="density_first",
    )


def density_second_kernel(*refs):
    mine, other, (bcat, got_m, got_x) = refs[:4], refs[4:8], refs[8:11]
    x1, m2, own_rows, tcat = refs[11:]
    gather_rows(mine, other, tcat)
    own_rows[...] = tcat[:ROWS]

    @pl.loop(0, 2)
    def _(half):
        columns, value = product(tcat.at[ROWS:], bcat, half)
        x = value[:HALF] + got_m[HALF:, columns].astype(f32)
        m = value[HALF:] + got_x[HALF:, columns].astype(f32)
        x1[:, columns] = x.astype(bf16)
        m2[:, columns] = m.astype(bf16)


def density_second(mine, other, bcat, from_m, from_x):
    return call(
        density_second_kernel,
        [(v, VMEM) for v in (*mine, *other, bcat, from_m, from_x)],
        [hbm((HALF, AUX))] * 2 + [vmem((ROWS, 2 * WIDE))],
        [pltpu.VMEM(TCAT, bf16)],
        name="density_second",
    )


def density_own_kernel(rows, bcat, got_m, got_x, own):
    @pl.loop(0, 2)
    def _(half):
        columns, value = product(rows, bcat, half)
        own[:HALF, columns] = value[:HALF] + got_x[:HALF, columns].astype(f32)
        own[HALF:, columns] = value[HALF:] + got_m[:HALF, columns].astype(f32)


def density_own(rows, bcat, from_m, from_x):
    return call(
        density_own_kernel,
        [(v, VMEM) for v in (rows, bcat, from_m, from_x)],
        [vmem((ROWS, AUX), f32)],
        name="density_own",
    )[0]


def add_kernel(own, one, two, out):
    out[:HALF] = (own[:HALF] + one[...].astype(f32)).astype(bf16)
    out[HALF:] = (own[HALF:] + two[...].astype(f32)).astype(bf16)


def add(own, one, two):
    return call(
        add_kernel,
        [(own, VMEM), (one, VMEM), (two, VMEM)],
        [hbm((ROWS, AUX))],
        name="add",
    )[0]


def local(integrals, tiles, tile_index, vir_energy, occ_energy, pair_index):
    window = integrals.reshape(2 * ROWS, AUX)
    vir = vir_energy.reshape(-1, ROWS)
    up = [(g, g + 1) for g in range(7)]
    down = [(g + 1, g) for g in range(7)]
    last, first = ends(window)
    left = lax.ppermute(last, "grp", up)
    right = lax.ppermute(first, "grp", down)
    a, b = fit(tile_index.T, window, tiles, left, right)

    with jax.named_scope("first"):
        ax = send_x(a, -1)
        am = send_x(a, 1)
        bo = send_z(b)
        bp = send_y(b, -1)
        bm = send_y(b, 1)
    bo, bp = arrive((bo, bp), (bm, vir))
    with jax.named_scope("second"):
        bom = send_y(bo, 1)
        b2 = send_y(bp, -1)
        bop = send_z(bp)
        ad = send_x(ax, -1)
    early_sums, bcat, acat = pair_first((a, ax, am), (b, bm, bp, bo))
    (c1,) = cut([(b2, 0, 64)], (early_sums,), name="cut_b1")
    (c2,) = cut([(bom, 64, 48)], (early_sums,), name="cut_b2")
    (c3,) = cut([(bop, 112, 48)], (early_sums,), name="cut_b3")
    with jax.named_scope("third"):
        c1 = send_z(c1)
        c2 = send_y(c2, 1)
        c3 = send_y(c3, -1)
    _, bcat, acat, keep, send = pair_early(early_sums, bcat, acat, ad, (bom, b2, bop))
    keep, send, bcat = pair_late(keep, send, acat, bcat, (c1, c2, c3))
    with jax.named_scope("core"):
        own, *s = core_sum(keep, send_core(send))
    with jax.named_scope("shares"):
        arrived = [send_high(s[k - 1], k) for k in (2, 1, 3)]
    mine = amplitude(vir, occ_energy, pair_index, own, arrived)

    def spread(wave):
        with jax.named_scope(f"spread_{wave}"):
            sent = {k: send_high(mine[wave], k) for k in (1, 3, 2)}
            return [mine[wave]] + [sent[k] for k in (1, 2, 3)]

    def other_core(wave, mine):
        with jax.named_scope(f"other_{wave}"):
            return [send_core(v) for v in mine]

    mine0, mine1 = spread(0), spread(1)
    other0 = other_core(0, mine0)
    other1 = other_core(1, mine1)
    x2_d1, m1_d2 = density_first(mine0, other0, bcat)
    with jax.named_scope("out"):
        from_m = send_x(x2_d1, 1)
        from_x = send_x(m1_d2, -1)
    x1, m2, own_rows = density_second(mine1, other1, bcat, from_m, from_x)
    with jax.named_scope("out"):
        got_x1 = send_x(x1, 1)
        got_m2 = send_x(m2, -1)
    own = density_own(own_rows, bcat, from_m, from_x)
    return add(own, got_x1, got_m2)


def solution(mesh):
    in_specs = (P(None, "blk", "grp"), P("grp", None, None), P("grp", None), P(), P(), P())
    return jax.shard_map(
        local, mesh=mesh, in_specs=in_specs, out_specs=P("blk", "grp"), check_vma=False
    )
```

```python
import functools

import jax
import jax.numpy as jnp
from jax import lax
from jax.experimental import pallas as pl
from jax.experimental.pallas import tpu as pltpu
from jax.sharding import PartitionSpec as P

TILE = 128
HB = 4
BAND = 2 * HB + 1
ROWS = 160
AUX = 2560
HALO = HB * TILE
bf16 = jnp.bfloat16
f32 = jnp.float32
MIB = 1 << 20


def blk_index(y, x, z):
    return ((y % 4) * 4 + x % 4) * 2 + z


PLACES = [(y, x, z) for y in range(4) for x in range(4) for z in range(2)]


def send_y(v, step):
    pairs = [(blk_index(y, x, z), blk_index(y + step, x, z)) for y, x, z in PLACES]
    return lax.ppermute(v, "blk", pairs)


def send_x(v, step):
    pairs = [(blk_index(y, x, z), blk_index(y, x + step, z)) for y, x, z in PLACES]
    return lax.ppermute(v, "blk", pairs)


def send_z(v):
    pairs = [(blk_index(y, x, z), blk_index(y, x, 1 - z)) for y, x, z in PLACES]
    return lax.ppermute(v, "blk", pairs)


def send_core(v):
    return lax.ppermute(v, "grp", [(g, g ^ 1) for g in range(8)])


def send_high(v, step):
    return lax.ppermute(v, "grp", [(g, (g + 2 * step) % 8) for g in range(8)])


def params(mib=28):
    return pltpu.CompilerParams(vmem_limit_bytes=mib * MIB)


def cost():
    return pl.CostEstimate(flops=1000, bytes_accessed=1000, transcendentals=0)


def position():
    group = lax.axis_index("grp").astype(jnp.int32)
    me = lax.axis_index("blk").astype(jnp.int32)
    return group // 2, group % 2, me // 8, (me // 2) % 4, me % 2


ANY = pl.BlockSpec(memory_space=pl.ANY)
VMEM = pl.BlockSpec(memory_space=pltpu.VMEM)
SMEM = pl.BlockSpec(memory_space=pltpu.SMEM)
DMA = pltpu.SemaphoreType.DMA
HALF = ROWS // 2
SHARE = ROWS // 2
WIDE = 4 * ROWS
K2 = AUX // 2
K4 = AUX // 4


def hbm(shape, dtype=bf16):
    return jax.ShapeDtypeStruct(shape, dtype)


def vmem(shape, dtype=bf16):
    return pltpu.VMEM(shape, dtype)


def call(kernel, args, outs, scratch=(), name=None, aliases=None, mib=28):
    return pl.pallas_call(
        kernel,
        in_specs=[spec for _, spec in args],
        out_specs=[VMEM] * len(outs),
        out_shape=list(outs),
        scratch_shapes=list(scratch),
        input_output_aliases=aliases or {},
        compiler_params=params(mib),
        cost_estimate=cost(),
        name=name,
    )(*[a for a, _ in args])


INNER = (2, 3, 4, 5, 6, 7)
EDGE = (0, 1, 8, 9)


def fit_inner_kernel(index, own_in, tiles_in, a, b, own, edge, tiles, weights, own_sem, sems):
    own_copies = [
        pltpu.make_async_copy(
            own_in.at[pl.ds(i * ROWS, ROWS)], own.at[pl.ds(i * ROWS, ROWS)], own_sem.at[i]
        )
        for i in range(2)
    ]
    copies = {}
    for p in INNER + EDGE:
        part = pl.ds(p * 2 * BAND, 2 * BAND)
        copies[p] = pltpu.make_async_copy(tiles_in.at[part], tiles.at[part], sems.at[p])
    copies[INNER[0]].start()
    for c in own_copies:
        c.start()
    for p in (INNER + EDGE)[1:]:
        copies[p].start()
    zero = jnp.zeros((TILE, TILE), bf16)

    def build(p, out):
        out[:TILE, TILE:] = zero
        out[BAND * TILE :, :TILE] = zero
        for q in range(2):
            for o in range(BAND):
                slot = p * 2 * BAND + q * BAND + o
                at = (q + o) * TILE
                out[at : at + TILE, q * TILE : (q + 1) * TILE] = jnp.where(
                    index[1, slot] == 1, tiles[slot], zero
                )

    for p in INNER:
        copies[p].wait()
        if p == INNER[0]:
            for c in own_copies:
                c.wait()
        build(p, weights)
        window = own[:, (2 * p - HB) * TILE : (2 * p + HB + 2) * TILE]
        fitted = jnp.dot(window, weights[...], preferred_element_type=f32).astype(bf16)
        columns = slice(p * 2 * TILE, (p + 1) * 2 * TILE)
        a[:, columns] = fitted[:ROWS]
        b[:, columns] = fitted[ROWS:]
    for n, p in enumerate(EDGE):
        copies[p].wait()
        build(p, edge.at[n])


def fit_edge_kernel(left, right, own, edge, _, __, a, b, ext):
    ext[:, :HALO] = left[...]
    ext[:, HALO : 3 * HALO] = own[:, : 2 * HALO]
    ext[:, 3 * HALO : 5 * HALO] = own[:, AUX - 2 * HALO :]
    ext[:, 5 * HALO :] = right[...]
    for n, p in enumerate(EDGE):
        at = (0, 2, 12, 14)[n] * TILE
        window = ext[:, at : at + (BAND + 1) * TILE]
        fitted = jnp.dot(window, edge[n], preferred_element_type=f32).astype(bf16)
        columns = slice(p * 2 * TILE, (p + 1) * 2 * TILE)
        a[:, columns] = fitted[:ROWS]
        b[:, columns] = fitted[ROWS:]


def fit(index, own, tiles, left, right):
    banded = ((BAND + 1) * TILE, 2 * TILE)
    a, b, own, edge = call(
        fit_inner_kernel,
        [(index, SMEM), (own, ANY), (tiles, ANY)],
        [vmem((ROWS, AUX)), vmem((ROWS, AUX)), vmem((2 * ROWS, AUX)), vmem((4, *banded))],
        [pltpu.VMEM(tiles.shape, bf16), pltpu.VMEM(banded, bf16), DMA((2,)), DMA((10,))],
        name="fit_inner",
        mib=56,
    )
    return call(
        fit_edge_kernel,
        [(v, VMEM) for v in (left, right, own, edge, a, b)],
        [vmem((ROWS, AUX))] * 2,
        [pltpu.VMEM((2 * ROWS, 6 * HALO), bf16)],
        name="fit_edge",
        aliases={4: 0, 5: 1},
    )


def ends_kernel(own, last, first, sems):
    copies = [
        pltpu.make_async_copy(own.at[:, pl.ds(AUX - HALO, HALO)], last, sems.at[0]),
        pltpu.make_async_copy(own.at[:, pl.ds(0, HALO)], first, sems.at[1]),
    ]
    for c in copies:
        c.start()
    for c in copies:
        c.wait()


def ends(own):
    outs = [vmem((2 * ROWS, HALO))] * 2
    return call(ends_kernel, [(own, ANY)], outs, [DMA((2,))], name="ends", mib=60)


def cut(parts, after=(), name=None):
    def kernel(*refs):
        for i, o, (_, r, n) in zip(refs, refs[len(parts) + len(after) :], parts):
            o[...] = i[r : r + n]

    return call(
        kernel,
        [(p[0], VMEM) for p in parts] + [(v, ANY) for v in after],
        [hbm((n, AUX)) for _, _, n in parts],
        name=name,
    )


def arrive(parts, after):
    n = len(parts)
    return pl.pallas_call(
        lambda *refs: None,
        in_specs=[ANY] * (n + len(after)),
        out_specs=[ANY] * n,
        out_shape=[hbm(v.shape, v.dtype) for v in parts],
        input_output_aliases={i: i for i in range(n)},
        compiler_params=params(),
        cost_estimate=cost(),
        name="arrive",
    )(*parts, *after)


def row_copies(moves, out, sems, part):
    columns = pl.ds(pl.multiple_of(part * K4, K4), K4)
    return [
        pltpu.make_async_copy(
            v.at[pl.ds(r, n), columns], out.at[pl.ds(at, n), columns], sems.at[i, part]
        )
        for i, (v, r, n, at) in enumerate(moves)
    ]


def b_moves(parts, at=0):
    moves = []
    for p in parts:
        moves.append((p, 0, p.shape[0], at))
        at += p.shape[0]
    return moves


def products(copies, acat, bcat, wanted, unroll=False):
    for part in range(4):
        for c in copies(part):
            c.start()

    if unroll:
        for c in (c for part in range(4) for c in copies(part)):
            c.wait()
        for a_rows, b_rows, total in wanted:
            total[...] = lax.dot_general(
                acat[a_rows], bcat[b_rows], (((1,), (1,)), ((), ())),
                preferred_element_type=f32,
            )
        return

    @pl.loop(0, 4)
    def _(part):
        for c in copies(part):
            c.wait()
        columns = pl.ds(pl.multiple_of(part * K4, K4), K4)
        for a_rows, b_rows, total in wanted:
            value = lax.dot_general(
                acat[a_rows, columns], bcat[b_rows, columns], (((1,), (1,)), ((), ())),
                preferred_element_type=f32,
            )

            @pl.when(part == 0)
            def _():
                total[...] = value

            @pl.when(part > 0)
            def _():
                total[...] += value


def pair_first_kernel(own, ax, am, *refs):
    b_refs = refs[:4]
    total, bcat, acat, a_sems, b_sems = refs[4:]
    a_moves = [
        (own, 0, ROWS, 0),
        (ax, 0, HALF, ROWS),
        (ax, HALF, HALF, 2 * ROWS),
        (am, 0, HALF, 2 * ROWS + HALF),
        (am, HALF, HALF, ROWS + HALF),
    ]
    rows = slice(0, 3 * ROWS)
    products(
        lambda part: row_copies(a_moves, acat, a_sems, part)
        + row_copies(b_moves(b_refs), bcat, b_sems, part),
        acat, bcat, [(rows, slice(0, WIDE), total.at[rows])],
    )


def pair_first(a_parts, b_parts):
    return call(
        pair_first_kernel,
        [(v, ANY) for v in (*a_parts, *b_parts)],
        [vmem((WIDE, WIDE), f32), vmem((2 * WIDE, AUX)), vmem((WIDE, AUX))],
        [DMA((5, 4)), DMA((4, 4))],
        name="pair_first",
    )


def pair_early_kernel(first_in, bcat_in, acat_in, ad, *refs):
    b_refs = refs[:3]
    first, bcat, acat, keep, send, early, a_sems, b_sems = refs[3:]
    rows = slice(3 * ROWS, WIDE)
    products(
        lambda part: row_copies([(ad, 0, ROWS, 3 * ROWS)], acat, a_sems, part)
        + row_copies(b_moves(b_refs, WIDE), bcat, b_sems, part),
        acat, bcat,
        [
            (rows, slice(0, WIDE), first.at[rows]),
            (slice(0, WIDE), slice(WIDE, 7 * ROWS), early),
        ],
        unroll=True,
    )
    core = position()[1]
    split = 3 * ROWS

    @pl.when(core == 0)
    def _():
        keep[...] = first[...]
        send[:, :split] = early[...].astype(bf16)

    @pl.when(core == 1)
    def _():
        send[...] = first[...].astype(bf16)
        keep[:, :split] = early[...]


def pair_early(first, bcat, acat, ad, b_parts):
    return call(
        pair_early_kernel,
        [(v, VMEM) for v in (first, bcat, acat)] + [(v, ANY) for v in (ad, *b_parts)],
        [
            vmem((WIDE, WIDE), f32),
            vmem((2 * WIDE, AUX)),
            vmem((WIDE, AUX)),
            vmem((WIDE, WIDE), f32),
            vmem((WIDE, WIDE)),
        ],
        [pltpu.VMEM((WIDE, 3 * ROWS), f32), DMA((1, 4)), DMA((3, 4))],
        name="pair_early",
        aliases={0: 0, 1: 1, 2: 2},
    )


def pair_late_kernel(keep_in, send_in, acat, bcat_in, *refs):
    b_refs = refs[:3]
    keep, send, bcat = refs[3:]
    at = 7 * ROWS
    for v in b_refs:
        bcat[at : at + v.shape[0]] = v[...]
        at += v.shape[0]
    late = lax.dot_general(
        acat[...], bcat[7 * ROWS :], (((1,), (1,)), ((), ())), preferred_element_type=f32
    )
    core = position()[1]
    columns = slice(3 * ROWS, WIDE)

    @pl.when(core == 0)
    def _():
        send[:, columns] = late.astype(bf16)

    @pl.when(core == 1)
    def _():
        keep[:, columns] = late


def pair_late(keep, send, acat, bcat, b_parts):
    return call(
        pair_late_kernel,
        [(v, VMEM) for v in (keep, send, acat, bcat, *b_parts)],
        [vmem((WIDE, WIDE), f32), vmem((WIDE, WIDE)), vmem((2 * WIDE, AUX))],
        name="pair_late",
        aliases={0: 0, 1: 1, 3: 2},
    )


def core_sum_kernel(keep, got, own, s1, s2, s3):
    high = position()[0]
    for step, out in enumerate((own, s1, s2, s3)):
        for wave in range(2):
            at = pl.multiple_of((1 - wave) * 2 * ROWS + ((high + step) % 4) * SHARE, SHARE)
            value = keep[pl.ds(at, SHARE)] + got[pl.ds(at, SHARE)].astype(f32)
            out[wave * SHARE : (wave + 1) * SHARE] = value.astype(out.dtype)


def core_sum(keep, got):
    share = (2 * SHARE, WIDE)
    return call(
        core_sum_kernel,
        [(keep, VMEM), (got, VMEM)],
        [vmem(share, f32)] + [hbm(share)] * 3,
        name="core_sum",
    )


BLOCKS = (((0, 0), (3, 0), (1, 0), (0, 1)), ((3, 1), (2, 0), (1, 1), (2, 1)))


def amplitude_kernel(vir, occ, chosen, own, *refs):
    arrived, outs = refs[:3], refs[3:5]
    high, core, y, x, z = position()
    occ_total = occ[chosen[0]] + occ[chosen[1]]
    lane = lax.broadcasted_iota(jnp.int32, (SHARE, ROWS), 1)
    row = lax.broadcasted_iota(jnp.int32, (SHARE, ROWS), 0)

    def row_energy(shift, second):
        block = vir[pl.ds((y * 4 + (x + shift) % 4) * 2 + z, 1), :]
        own_lane = lane == row + second * SHARE
        return jnp.sum(jnp.where(own_lane, block, 0.0), axis=1, keepdims=True)

    rows = (
        row_energy(
            jnp.where(high == 0, 1, jnp.where(high == 1, 3, 2)),
            jnp.where((high == 0) | (high == 3), 1, 0),
        ),
        row_energy(jnp.where(high < 2, 0, 2 * high - 3), high % 2),
    )
    places = []
    for first, last in zip(*BLOCKS):
        step = jnp.where(core == 0, first[0], last[0])
        away = jnp.where(core == 0, first[1], last[1])
        places.append((((y + step) % 4) * 4 + x) * 2 + jnp.where(away == 1, 1 - z, z))
    columns = jnp.concatenate([vir[pl.ds(at, 1), :] for at in places], axis=1)
    for wave, out in enumerate(outs):
        part = slice(wave * SHARE, (wave + 1) * SHARE)
        total = own[part]
        for r in arrived:
            total = total + r[part].astype(f32)
        denominator = (rows[wave] + columns) - occ_total
        out[...] = (total / denominator).astype(bf16)


def amplitude(vir, occ, chosen, own, arrived):
    return call(
        amplitude_kernel,
        [(vir, VMEM), (occ, SMEM), (chosen, SMEM), (own, VMEM)]
        + [(v, VMEM) for v in arrived],
        [hbm((SHARE, WIDE))] * 2,
        name="amplitude",
    )


def gather_rows(mine, other, tcat):
    high, core = position()[:2]
    for k in range(4):
        rows = pl.ds(pl.multiple_of(((high - k + 4) % 4) * SHARE, SHARE), SHARE)
        for v, of in ((mine[k], core), (other[k], 1 - core)):
            tcat[rows, pl.ds(pl.multiple_of(of * WIDE, WIDE), WIDE)] = v[...]


def product(tcat, bcat, half):
    columns = pl.ds(pl.multiple_of(half * K2, K2), K2)
    return columns, jnp.dot(tcat[...], bcat[:, columns], preferred_element_type=f32)


TCAT = (2 * ROWS, 2 * WIDE)


def density_first_kernel(*refs):
    mine, other, bcat = refs[:4], refs[4:8], refs[8]
    outs, tcat = refs[9:11], refs[11]
    gather_rows(mine, other, tcat)

    @pl.loop(0, 2)
    def _(half):
        columns, value = product(tcat, bcat, half)
        value = value.astype(bf16)
        for i, out in enumerate(outs):
            out[:HALF, columns] = value[i * HALF : (i + 1) * HALF]
            out[HALF:, columns] = value[(i + 2) * HALF : (i + 3) * HALF]


def density_first(mine, other, bcat):
    return call(
        density_first_kernel,
        [(v, VMEM) for v in (*mine, *other, bcat)],
        [hbm((ROWS, AUX))] * 2,
        [pltpu.VMEM(TCAT, bf16)],
        name="density_first",
    )


def density_second_kernel(*refs):
    mine, other, (bcat, got_m, got_x) = refs[:4], refs[4:8], refs[8:11]
    x1, m2, own_rows, tcat = refs[11:]
    gather_rows(mine, other, tcat)
    own_rows[...] = tcat[:ROWS]

    @pl.loop(0, 2)
    def _(half):
        columns, value = product(tcat.at[ROWS:], bcat, half)
        x = value[:HALF] + got_m[HALF:, columns].astype(f32)
        m = value[HALF:] + got_x[HALF:, columns].astype(f32)
        x1[:, columns] = x.astype(bf16)
        m2[:, columns] = m.astype(bf16)


def density_second(mine, other, bcat, from_m, from_x):
    return call(
        density_second_kernel,
        [(v, VMEM) for v in (*mine, *other, bcat, from_m, from_x)],
        [hbm((HALF, AUX))] * 2 + [vmem((ROWS, 2 * WIDE))],
        [pltpu.VMEM(TCAT, bf16)],
        name="density_second",
    )


def density_own_kernel(rows, bcat, got_m, got_x, own):
    @pl.loop(0, 2)
    def _(half):
        columns, value = product(rows, bcat, half)
        own[:HALF, columns] = value[:HALF] + got_x[:HALF, columns].astype(f32)
        own[HALF:, columns] = value[HALF:] + got_m[:HALF, columns].astype(f32)


def density_own(rows, bcat, from_m, from_x):
    return call(
        density_own_kernel,
        [(v, VMEM) for v in (rows, bcat, from_m, from_x)],
        [vmem((ROWS, AUX), f32)],
        name="density_own",
    )[0]


def add_kernel(own, one, two, out):
    out[:HALF] = (own[:HALF] + one[...].astype(f32)).astype(bf16)
    out[HALF:] = (own[HALF:] + two[...].astype(f32)).astype(bf16)


def add(own, one, two):
    return call(
        add_kernel,
        [(own, VMEM), (one, VMEM), (two, VMEM)],
        [hbm((ROWS, AUX))],
        name="add",
    )[0]


def local(integrals, tiles, tile_index, vir_energy, occ_energy, pair_index):
    window = integrals.reshape(2 * ROWS, AUX)
    vir = vir_energy.reshape(-1, ROWS)
    up = [(g, g + 1) for g in range(7)]
    down = [(g + 1, g) for g in range(7)]
    last, first = ends(window)
    left = lax.ppermute(last, "grp", up)
    right = lax.ppermute(first, "grp", down)
    a, b = fit(tile_index.T, window, tiles, left, right)

    with jax.named_scope("first"):
        ax = send_x(a, -1)
        am = send_x(a, 1)
        bo = send_z(b)
        bp = send_y(b, -1)
        bm = send_y(b, 1)
    (bp,) = arrive((bp,), (bm, vir))
    (bo,) = arrive((bo,), (bp,))
    with jax.named_scope("second"):
        bom = send_y(bo, 1)
        b2 = send_y(bp, -1)
        bop = send_z(bp)
        ad = send_x(ax, -1)
    early_sums, bcat, acat = pair_first((a, ax, am), (b, bm, bp, bo))
    (c1,) = cut([(b2, 0, 64)], (early_sums,), name="cut_b1")
    (c2,) = cut([(bom, 64, 48)], (early_sums,), name="cut_b2")
    (c3,) = cut([(bop, 112, 48)], (early_sums,), name="cut_b3")
    with jax.named_scope("third"):
        c1 = send_z(c1)
        c2 = send_y(c2, 1)
        c3 = send_y(c3, -1)
    _, bcat, acat, keep, send = pair_early(early_sums, bcat, acat, ad, (bom, b2, bop))
    keep, send, bcat = pair_late(keep, send, acat, bcat, (c1, c2, c3))
    with jax.named_scope("core"):
        own, *s = core_sum(keep, send_core(send))
    with jax.named_scope("shares"):
        arrived = [send_high(s[k - 1], k) for k in (2, 1, 3)]
    mine = amplitude(vir, occ_energy, pair_index, own, arrived)

    def spread(wave):
        with jax.named_scope(f"spread_{wave}"):
            sent = {k: send_high(mine[wave], k) for k in (1, 3, 2)}
            return [mine[wave]] + [sent[k] for k in (1, 2, 3)]

    def other_core(wave, mine):
        with jax.named_scope(f"other_{wave}"):
            return [send_core(v) for v in mine]

    mine0, mine1 = spread(0), spread(1)
    other0 = other_core(0, mine0)
    other1 = other_core(1, mine1)
    x2_d1, m1_d2 = density_first(mine0, other0, bcat)
    with jax.named_scope("out"):
        from_m = send_x(x2_d1, 1)
        from_x = send_x(m1_d2, -1)
    x1, m2, own_rows = density_second(mine1, other1, bcat, from_m, from_x)
    with jax.named_scope("out"):
        got_x1 = send_x(x1, 1)
        got_m2 = send_x(m2, -1)
    own = density_own(own_rows, bcat, from_m, from_x)
    return add(own, got_x1, got_m2)


def solution(mesh):
    in_specs = (P(None, "blk", "grp"), P("grp", None, None), P("grp", None), P(), P(), P())
    return jax.shard_map(
        local, mesh=mesh, in_specs=in_specs, out_specs=P("blk", "grp"), check_vma=False
    )
```
